32 devices in a mesh: src: 8 (over z, y), tgt: 4 (over x, core).
Axes of the slice: x: 2, y: 2, z: 4, core: 2. Of those that a mesh axis runs over, the one named last changes fastest.
Arguments:
- source_points: float32 [3, 32768], P(None, 'src'), may hold values from -3.5 to 3.5, as said below
- target_points: float32 [3, 16384], P(None, 'tgt'), may hold values from -3.5 to 3.5, as said below
- source_weight: float32 [32768], P('src'), may hold values from 0.1 to 3
- target_weight: float32 [16384], P('tgt'), may hold values from 0.1 to 3
- target_start: float32 [16384], P('tgt'), may hold values from -1.2 to 1.2
- tile_source: int32 [8, 4, 12], P('src', 'tgt'), may hold values from 0 to 7, as said below
- tile_target: int32 [8, 4, 12], P('src', 'tgt'), may hold values from 0 to 7, as said below
- tile_count: int32 [8, 4], P('src', 'tgt'), may hold values from 8 to 12, as said below
Outputs:
- source_potential: float32 [32768], P('src')
- target_potential: float32 [16384], P('tgt')
- source_gradient: float32 [3, 32768], P(None, ('src', 'tgt'))
- target_gradient: float32 [3, 16384], P(None, 'tgt')
The draws below stay inside these ranges and needn't reach their ends.
Inputs may be any that keep to these rules, and one draw needn't show every extreme that they name: `source_points`: coordinates are cluster centres plus offsets. `target_points`: coordinates are cluster centres plus offsets. `tile_source`: within one block pair the live slots name distinct cluster pairs; the first 8 slots name every source cluster of the block once and every target cluster of the block once; slots from tile_count on hold 0. `tile_target`: as for tile_source. `tile_count`: some block pair uses all 12 slots.
All inputs are finite; a program needn't handle non-finite values.
Results may differ from the reference program's by a relative error of at most 0.0003.
Values sent between devices are 32-bit elements; how exact they have to be, the bound alone decides.
No kernel may reach another device: no remote copies, remote signals or barrier semaphores. Data moves between devices by JAX's collectives and lax.ppermute only.
A program may use at most 64 MiB of HBM per device.

```python
import math
import jax
import jax.numpy as jnp
from jax import lax

CLUSTER = 512
CPD = 8
ITERS = 2
KMAX = 12
NS = 32768
NT = 16384
N_SRC = 8
N_TGT = 4


def tile_lists(key):
    shift_key, order_key, count_key, pick_key = jax.random.split(key, 4)
    shifts = jax.random.randint(shift_key, (N_SRC, N_TGT, 1), 0, CPD)
    base = jnp.arange(CPD, dtype=jnp.int32)[None, None, :]
    diag_src = jnp.broadcast_to(base, (N_SRC, N_TGT, CPD))
    diag_tgt = (base + shifts) % CPD
    others = CPD * (CPD - 1)

    def shuffled(one_key):
        return jax.random.permutation(one_key, others)
    order = jax.vmap(shuffled)(jax.random.split(order_key, N_SRC * N_TGT))
    order = order.reshape(N_SRC, N_TGT, others)[:, :, :KMAX - CPD].astype(jnp.int32)
    extra_src = order // (CPD - 1)
    extra_tgt = (extra_src + shifts + order % (CPD - 1) + 1) % CPD
    sources = jnp.concatenate([diag_src, extra_src], axis=2)
    targets = jnp.concatenate([diag_tgt, extra_tgt], axis=2)
    counts = jax.random.randint(count_key, (N_SRC * N_TGT,), CPD, KMAX + 1)
    full_at = jax.random.randint(pick_key, (), 0, N_SRC * N_TGT)
    counts = counts.at[full_at].set(KMAX).reshape(N_SRC, N_TGT).astype(jnp.int32)
    live = jnp.arange(KMAX, dtype=jnp.int32)[None, None, :] < counts[:, :, None]
    sources = jnp.where(live, sources, 0).astype(jnp.int32)
    targets = jnp.where(live, targets, 0).astype(jnp.int32)
    return (sources, targets, counts)


def draw_tile_source(key, part):
    lists = tile_lists(key)
    return lists[0]


def draw_tile_target(key, part):
    lists = tile_lists(key)
    return lists[1]


def draw_tile_count(key, part):
    lists = tile_lists(key)
    return lists[2]


def cloud(key, count, reach, normal_part):
    centre_key, normal_key = jax.random.split(key, 2)
    centres = jax.random.uniform(centre_key, (3, count // CLUSTER), jnp.float32, -reach, reach)
    normal_offsets = jnp.clip(jax.random.normal(normal_key, (3, count), jnp.float32), -3.0, 3.0)
    return jnp.repeat(centres, CLUSTER, axis=1) + normal_part * normal_offsets


def draw_source_points(key, part):
    key = jax.random.fold_in(key, 5)
    return cloud(key, NS, 2.0, 0.4)


def draw_target_points(key, part):
    key = jax.random.fold_in(key, 6)
    return cloud(key, NT, 2.0, 0.4)


def steps_of(stream_key, shape, cuts, smallest, top_value):
    def one(axis_at, blocks):
        heights = jax.random.uniform(jax.random.fold_in(jax.random.fold_in(stream_key, 6), axis_at), (blocks,), jnp.float32, smallest / len(cuts), top_value / len(cuts))
        return jnp.repeat(jnp.exp(heights), shape[axis_at] // blocks).reshape((-1,) + (1,) * (len(shape) - axis_at - 1))

    gain = one(*cuts[0])
    for cut in cuts[1:]:
        gain = gain * one(*cut)
    return gain


def bell_draw(stream_key, extent, scale, limit, pieces=(), kind=jnp.bfloat16):
    result = scale * jax.random.normal(stream_key, extent, jnp.float32)
    if pieces:
        result = result * steps_of(stream_key, extent, pieces, -0.22, 0.18)
    return jnp.clip(result, -limit, limit).astype(kind)


def setup_inputs(seed: int = 0) -> dict:
    key_list = jax.random.split(jax.random.key(seed), 9)
    return {
        "source_points": draw_source_points(jax.random.fold_in(key_list[8], 71), 0),
        "target_points": draw_target_points(jax.random.fold_in(key_list[8], 71), 0),
        "source_weight": jnp.clip(jnp.exp(math.log(3.0) - 3.4011974 * jax.random.uniform(key_list[2], (NS,), jnp.float32) ** steps_of(key_list[2], (NS,), ((0, 8),), -0.2, 0.2)), 0.1, 3.0),
        "target_weight": jnp.clip(jnp.exp(math.log(3.0) - 3.4011974 * jax.random.uniform(key_list[3], (NT,), jnp.float32) ** steps_of(key_list[3], (NT,), ((0, 4),), -0.2, 0.2)), 0.1, 3.0),
        "target_start": bell_draw(key_list[4], (NT,), 0.2, 1.2, ((0, 4),), jnp.float32),
        "tile_source": draw_tile_source(jax.random.fold_in(key_list[8], 71), 0),
        "tile_target": draw_tile_target(jax.random.fold_in(key_list[8], 71), 0),
        "tile_count": draw_tile_count(jax.random.fold_in(key_list[8], 71), 0),
    }


EPSILON = 0.02
FLOOR = -1.0e30


def tile_offsets(xs, ys):
    return [xs[c][:, None] - ys[c][None, :] for c in range(3)]


def tile_cost(offsets):
    return 0.5 * (offsets[0] * offsets[0] + offsets[1] * offsets[1] + offsets[2] * offsets[2])


def combine_parts(first, second):
    top = jnp.maximum(first[0], second[0])
    total = first[1] * jnp.exp(first[0] - top) + second[1] * jnp.exp(second[0] - top)
    return top, total


def reference(source_points, target_points, source_weight, target_weight, target_start, tile_source, tile_target, tile_count):
    slots = tile_source.shape[2]
    blocks_src = tile_source.shape[0]
    blocks_tgt = tile_source.shape[1]
    src_index = (jnp.arange(blocks_src, dtype=jnp.int32)[:, None, None] * CPD + tile_source).reshape(-1).astype(jnp.int32)
    tgt_index = (jnp.arange(blocks_tgt, dtype=jnp.int32)[None, :, None] * CPD + tile_target).reshape(-1).astype(jnp.int32)
    live_all = (jnp.arange(slots, dtype=jnp.int32)[None, None, :] < tile_count[:, :, None]).reshape(-1)
    log_source = jnp.log(source_weight)
    log_target = jnp.log(target_weight)
    tiles = (src_index, tgt_index, live_all)

    def tile_points(sc, tc):
        srow = (sc * CLUSTER).astype(jnp.int32)
        tcol = (tc * CLUSTER).astype(jnp.int32)
        xs = lax.dynamic_slice_in_dim(source_points, srow, CLUSTER, 1)
        ys = lax.dynamic_slice_in_dim(target_points, tcol, CLUSTER, 1)
        return srow, tcol, tile_offsets(xs, ys)

    def row_pass(target_pot):
        def step(carry, tile):
            tops, totals = carry
            srow, tcol, offs = tile_points(tile[0], tile[1])
            lb = lax.dynamic_slice_in_dim(log_target, tcol, CLUSTER)
            gs = lax.dynamic_slice_in_dim(target_pot, tcol, CLUSTER)
            scores = lb[None, :] + (gs[None, :] - tile_cost(offs)) / EPSILON
            part_top = jnp.max(scores, axis=1)
            part_total = jnp.sum(jnp.exp(scores - part_top[:, None]), axis=1)
            part_top = jnp.where(tile[2], part_top, FLOOR)
            part_total = jnp.where(tile[2], part_total, 0.0)
            old = (lax.dynamic_slice_in_dim(tops, srow, CLUSTER), lax.dynamic_slice_in_dim(totals, srow, CLUSTER))
            new = combine_parts(old, (part_top, part_total))
            tops = lax.dynamic_update_slice_in_dim(tops, new[0], srow, 0)
            totals = lax.dynamic_update_slice_in_dim(totals, new[1], srow, 0)
            return (tops, totals), None
        init = (jnp.full((NS,), FLOOR, jnp.float32), jnp.zeros((NS,), jnp.float32))
        (tops, totals), unused = lax.scan(step, init, tiles)
        return -EPSILON * (tops + jnp.log(totals))

    def col_pass(source_pot):
        def step(carry, tile):
            tops, totals = carry
            srow, tcol, offs = tile_points(tile[0], tile[1])
            la = lax.dynamic_slice_in_dim(log_source, srow, CLUSTER)
            fs = lax.dynamic_slice_in_dim(source_pot, srow, CLUSTER)
            scores = la[:, None] + (fs[:, None] - tile_cost(offs)) / EPSILON
            part_top = jnp.max(scores, axis=0)
            part_total = jnp.sum(jnp.exp(scores - part_top[None, :]), axis=0)
            part_top = jnp.where(tile[2], part_top, FLOOR)
            part_total = jnp.where(tile[2], part_total, 0.0)
            old = (lax.dynamic_slice_in_dim(tops, tcol, CLUSTER), lax.dynamic_slice_in_dim(totals, tcol, CLUSTER))
            new = combine_parts(old, (part_top, part_total))
            tops = lax.dynamic_update_slice_in_dim(tops, new[0], tcol, 0)
            totals = lax.dynamic_update_slice_in_dim(totals, new[1], tcol, 0)
            return (tops, totals), None
        init = (jnp.full((NT,), FLOOR, jnp.float32), jnp.zeros((NT,), jnp.float32))
        (tops, totals), unused = lax.scan(step, init, tiles)
        return -EPSILON * (tops + jnp.log(totals))

    target_pot = target_start
    source_pot = target_start[:0]
    for turn in range(ITERS):
        source_pot = row_pass(target_pot)
        target_pot = col_pass(source_pot)

    def grad_step(carry, tile):
        grad_src, grad_tgt = carry
        srow, tcol, offs = tile_points(tile[0], tile[1])
        la = lax.dynamic_slice_in_dim(log_source, srow, CLUSTER)
        lb = lax.dynamic_slice_in_dim(log_target, tcol, CLUSTER)
        fs = lax.dynamic_slice_in_dim(source_pot, srow, CLUSTER)
        gs = lax.dynamic_slice_in_dim(target_pot, tcol, CLUSTER)
        plan = jnp.exp(la[:, None] + lb[None, :] + (fs[:, None] + gs[None, :] - tile_cost(offs)) / EPSILON)
        plan = jnp.where(tile[2], plan, 0.0)
        src_part = jnp.stack([jnp.sum(plan * offs[c], axis=1) for c in range(3)])
        tgt_part = jnp.stack([-jnp.sum(plan * offs[c], axis=0) for c in range(3)])
        grad_src = lax.dynamic_update_slice_in_dim(grad_src, lax.dynamic_slice_in_dim(grad_src, srow, CLUSTER, 1) + src_part, srow, 1)
        grad_tgt = lax.dynamic_update_slice_in_dim(grad_tgt, lax.dynamic_slice_in_dim(grad_tgt, tcol, CLUSTER, 1) + tgt_part, tcol, 1)
        return (grad_src, grad_tgt), None

    init = (jnp.zeros((3, NS), jnp.float32), jnp.zeros((3, NT), jnp.float32))
    (grad_src, grad_tgt), unused = lax.scan(grad_step, init, tiles)
    return source_pot, target_pot, grad_src, grad_tgt
```

```python
import functools
import math

import jax
import jax.numpy as jnp
from jax import lax
from jax.experimental import pallas as pl
from jax.experimental.pallas import tpu as pltpu
from jax.sharding import PartitionSpec as P

CLUSTER = 512
EPSILON = 0.02
KAPPA = math.log2(math.e) / EPSILON
LOG2E = math.log2(math.e)
FLOOR = -1e30
CHUNK = 128
DEPTH = 32
F32 = jnp.float32
BF16 = jnp.bfloat16


def log2(value):
    return jnp.log(value) * LOG2E


def split(value):
    high = value.astype(BF16).astype(F32)
    rest = value - high
    middle = rest.astype(BF16).astype(F32)
    return (high, middle, rest - middle)


def half_square(points):
    return 0.5 * (points[0:1] * points[0:1] + points[1:2] * points[1:2] + points[2:3] * points[2:3])


def place(scratch, parts, order):
    scratch[...] = jnp.zeros_like(scratch)
    for at, which in enumerate(order):
        scratch[3 * at : 3 * at + 3, :] = parts[which]


SOURCE_ORDER = (0, 0, 1, 0, 2, 1)
TARGET_ORDER = (0, 1, 0, 2, 0, 1)


def with_rows(out, static, first, second):
    out[0:16, :] = static[0:16, :]
    low = static[16:32, :].astype(F32)
    row = lax.broadcasted_iota(jnp.int32, low.shape, 0)
    for at, part in enumerate(tuple(first) + tuple(second)):
        low = jnp.where(row == 2 + at, part, low)
    out[16:32, :] = low.astype(BF16)


ONES = (1.0, 1.0, 1.0)
ZEROS = (0.0, 0.0, 0.0)


def scores(left, right):
    return lax.dot_general(left, right, (((0,), (0,)), ((), ())), preferred_element_type=F32)


def start_of(index):
    return pl.multiple_of(index * CLUSTER, CLUSTER)


def lse_tiles(count, red_at, kept_at, red, kept, top, total, columns=None, sums=None):
    top[...] = jnp.full_like(top, FLOOR)
    total[...] = jnp.zeros_like(total)
    if sums is not None:
        sums[...] = jnp.zeros_like(sums)

    def step(slot, carry):
        r = start_of(red_at[0, 0, slot])
        k = start_of(kept_at[0, 0, slot])
        here = pl.ds(k, CLUSTER)
        right = kept[:, here]
        m = top[:, here]
        t = total[:, here]
        acc = None if sums is None else [sums[c, :, here] for c in range(3)]
        for at in range(CLUSTER // CHUNK):
            start = pl.multiple_of(r + at * CHUNK, CHUNK)
            s = scores(red[:, pl.ds(start, CHUNK)], right)
            s = s.reshape(CHUNK // 8, 8, CLUSTER)
            new = jnp.maximum(m, jnp.max(s, axis=0))
            old = jnp.exp2(m - new)
            p = jnp.exp2(s - new[None])
            t = t * old + jnp.sum(p, axis=0)
            if acc is not None:
                for c in range(3):
                    col = columns[pl.ds(start, CHUNK), 128 * c : 128 * (c + 1)]
                    col = jnp.concatenate([col] * (CLUSTER // 128), axis=1).reshape(s.shape)
                    acc[c] = acc[c] * old + jnp.sum(p * col, axis=0)
            m = new
        top[:, here] = m
        total[:, here] = t
        if acc is not None:
            for c in range(3):
                sums[c, :, here] = acc[c]
        return carry

    lax.fori_loop(0, count, step, 0)


def finish(top, total):
    m = top[...]
    largest = jnp.max(m, axis=0, keepdims=True)
    scale = jnp.exp2(m - largest)
    whole = jnp.sum(total[...] * scale, axis=0, keepdims=True)
    return largest + log2(whole), scale, whole


def combine(parts):
    largest = functools.reduce(jnp.maximum, parts)
    terms = [jnp.exp2(part - largest) for part in parts]
    whole = functools.reduce(jnp.add, terms)
    return largest + log2(whole), [term / whole for term in terms]


def rows_of(refs):
    return [refs[at] for at in range(refs.shape[0])]


def spread_columns(columns, static):
    pieces = static[1]
    row = lax.broadcasted_iota(jnp.int32, (DEPTH, 384), 0)
    lane = lax.broadcasted_iota(jnp.int32, (DEPTH, 384), 1) // 128
    pick = functools.reduce(jnp.logical_or, [row == lane + first for first in pieces])
    pick = jnp.where(pick, 1.0, 0.0).astype(BF16)

    def step(at, carry):
        here = pl.ds(start_of(at), CLUSTER)
        columns[here, :] = scores(static[0][:, here], pick)
        return carry

    lax.fori_loop(0, columns.shape[0] // CLUSTER, step, 0)


def fetch(pairs, sems):
    copies = [pltpu.make_async_copy(src, dst, sems.at[at]) for at, (src, dst) in enumerate(pairs)]
    for copy in copies:
        copy.start()
    return copies


def first_row_kernel(
    ys_in, tw_in, g0_in, xs_in, sw_in, t_src_in, t_tgt_in, count_in,
    xc_out, yc_out, part_out, xs, ys, sw, tw,
    g0, t_src, t_tgt, count, sems, stack, red, kept, top, total,
):
    copies = fetch(
        [
            (ys_in, ys), (tw_in, tw), (g0_in, g0), (xs_in, xs), (sw_in, sw),
            (t_src_in, t_src), (t_tgt_in, t_tgt), (count_in, count),
        ],
        sems,
    )
    for copy in copies[:3]:
        copy.wait()
    place(stack, split(ys[...] * KAPPA), TARGET_ORDER)
    yc_out[...] = stack[...].astype(BF16)
    potential = log2(tw[...]) + KAPPA * (g0[...] - half_square(ys[...]))
    with_rows(red, yc_out, split(potential), ONES)
    for copy in copies[3:]:
        copy.wait()
    place(stack, split(xs[...]), SOURCE_ORDER)
    xc_out[...] = stack[...].astype(BF16)
    with_rows(kept, xc_out, ONES, ZEROS)
    lse_tiles(count[0, 0], t_tgt, t_src, red, kept, top, total)
    part_out[...] = finish(top, total)[0]


def pass_kernel(
    parts, red_static, kept_static, weight, red_in, kept_in, count_in, part_out, red_at, kept_at, count, sems, red, kept, top, total
):
    copies = fetch([(red_in, red_at), (kept_in, kept_at), (count_in, count)], sems)
    potential = log2(weight[...]) - combine(rows_of(parts))[0]
    with_rows(red, red_static, split(potential), ONES)
    with_rows(kept, kept_static, ONES, ZEROS)
    for copy in copies:
        copy.wait()
    lse_tiles(count[0, 0], red_at, kept_at, red, kept, top, total)
    part_out[...] = finish(top, total)[0]


def last_col_kernel(
    parts, xs, xc, yc, sw, t_src_in, t_tgt_in, count_in, f_out, u_out, part_out,
    t_src, t_tgt, count, sems, red, kept, top, total, sums, columns,
):
    copies = fetch([(t_src_in, t_src), (t_tgt_in, t_tgt), (count_in, count)], sems)
    u = -combine(rows_of(parts))[0]
    u_out[...] = u
    f_out[...] = u * (1.0 / KAPPA) + half_square(xs[...])
    with_rows(red, xc, split(log2(sw[...]) + u), ONES)
    with_rows(kept, yc, ONES, ZEROS)
    spread_columns(columns, (xc, (0, 6, 12)))
    for copy in copies:
        copy.wait()
    lse_tiles(count[0, 0], t_src, t_tgt, red, kept, top, total, columns, sums)
    part, scale, whole = finish(top, total)
    part_out[0:1, :] = part
    for c in range(3):
        part_out[c + 1 : c + 2, :] = jnp.sum(sums[c] * scale, axis=0, keepdims=True) / whole


def gradient_kernel(
    parts, u, xs, ys, xc, yc, sw, tw, t_src_in, t_tgt_in, count_in, g_out, target_out, source_out,
    t_src, t_tgt, count, sems, red, kept, sums, columns,
):
    copies = fetch([(t_src_in, t_src), (t_tgt_in, t_tgt), (count_in, count)], sems)
    lse, shares = combine([parts[at, 0:1, :] for at in range(parts.shape[0])])
    v = -lse
    g_out[...] = v * (1.0 / KAPPA) + half_square(ys[...])
    for c in range(3):
        mean = functools.reduce(jnp.add, [w * parts[at, c + 1 : c + 2, :] for at, w in enumerate(shares)])
        target_out[c : c + 1, :] = tw[...] * (ys[c : c + 1, :] - mean)
    with_rows(red, yc, split(log2(tw[...]) + v), ONES)
    with_rows(kept, xc, ONES, split(log2(sw[...]) + u[...]))
    spread_columns(columns, (yc, (0, 3, 9)))
    sums[...] = jnp.zeros_like(sums)
    for copy in copies:
        copy.wait()

    def step(slot, carry):
        r = start_of(t_tgt[0, 0, slot])
        k = start_of(t_src[0, 0, slot])
        here = pl.ds(k, CLUSTER)
        right = kept[:, here]
        acc = [sums[c, :, here] for c in range(4)]
        for at in range(CLUSTER // CHUNK):
            start = pl.multiple_of(r + at * CHUNK, CHUNK)
            s = scores(red[:, pl.ds(start, CHUNK)], right)
            p = jnp.exp2(s.reshape(CHUNK // 8, 8, CLUSTER))
            acc[3] = acc[3] + jnp.sum(p, axis=0)
            for c in range(3):
                col = columns[pl.ds(start, CHUNK), 128 * c : 128 * (c + 1)]
                col = jnp.concatenate([col] * (CLUSTER // 128), axis=1).reshape(p.shape)
                acc[c] = acc[c] + jnp.sum(p * col, axis=0)
        for c in range(4):
            sums[c, :, here] = acc[c]
        return carry

    lax.fori_loop(0, count[0, 0], step, 0)
    mass = jnp.sum(sums[3], axis=0, keepdims=True)
    for c in range(3):
        moved = jnp.sum(sums[c], axis=0, keepdims=True) * (1.0 / KAPPA)
        whole = xs[c : c + 1, :] * mass - moved
        for at in range(source_out.shape[0]):
            width = source_out.shape[2]
            source_out[at, c : c + 1, :] = whole[:, at * width : (at + 1) * width]


VMEM = pl.BlockSpec(memory_space=pltpu.VMEM)
HBM = pl.BlockSpec(memory_space=pltpu.HBM)


def call(kernel, ins, far, outs, scratch):
    return pl.pallas_call(
        kernel,
        out_shape=outs,
        in_specs=[VMEM] * len(ins) + [HBM] * len(far),
        out_specs=[VMEM] * len(outs),
        scratch_shapes=scratch,
        compiler_params=pltpu.CompilerParams(vmem_limit_bytes=48 * 1024 * 1024),
    )(*ins, *far)


def body(source_points, target_points, source_weight, target_weight, target_start, tile_source, tile_target, tile_count):
    ns, nt = source_points.shape[1], target_points.shape[1]
    sw, tw, g0 = (a.reshape(1, -1) for a in (source_weight, target_weight, target_start))
    tiles = (tile_source, tile_target, tile_count)

    def row(n, k=1):
        return jax.ShapeDtypeStruct((k, n), F32)

    def work(red, kept):
        return [pltpu.VMEM((DEPTH, red), BF16), pltpu.VMEM((DEPTH, kept), BF16)]

    def state(kept):
        return [pltpu.VMEM((8, kept), F32), pltpu.VMEM((8, kept), F32)]

    def lists(copies):
        return [pltpu.SMEM(a.shape, jnp.int32) for a in tiles] + [pltpu.SemaphoreType.DMA((copies,))]

    xc, yc, part, xs, ys, sw, tw = call(
        first_row_kernel,
        (),
        (target_points, tw, g0, source_points, sw, *tiles),
        [
            jax.ShapeDtypeStruct((DEPTH, ns), BF16),
            jax.ShapeDtypeStruct((DEPTH, nt), BF16),
            row(ns), row(ns, 3), row(nt, 3), row(ns), row(nt),
        ],
        [pltpu.VMEM((1, nt), F32)] + lists(8) + [pltpu.VMEM((DEPTH, ns), F32)] + work(nt, ns) + state(ns),
    )
    (part,) = call(
        pass_kernel,
        (lax.all_gather(part, "tgt"), xc, yc, sw),
        tiles,
        [row(nt)],
        lists(3) + work(ns, nt) + state(nt),
    )
    (part,) = call(
        pass_kernel,
        (lax.all_gather(part, "src"), yc, xc, tw),
        (tile_target, tile_source, tile_count),
        [row(ns)],
        lists(3) + work(nt, ns) + state(ns),
    )
    f, u, part = call(
        last_col_kernel,
        (lax.all_gather(part, "tgt"), xs, xc, yc, sw),
        tiles,
        [row(ns), row(ns), row(nt, 4)],
        lists(3) + work(ns, nt) + state(nt) + [pltpu.VMEM((3, 8, nt), F32), pltpu.VMEM((ns, 384), F32)],
    )
    n = lax.axis_size("tgt")
    g, target_grad, source_parts = call(
        gradient_kernel,
        (lax.all_gather(part, "src"), u, xs, ys, xc, yc, sw, tw),
        tiles,
        [row(nt), row(nt, 3), jax.ShapeDtypeStruct((n, 3, ns // n), F32)],
        lists(3) + work(nt, ns) + [pltpu.VMEM((4, 8, ns), F32), pltpu.VMEM((nt, 384), F32)],
    )
    own_grad = jnp.sum(lax.all_to_all(source_parts, "tgt", 0, 0), axis=0)
    return (f.reshape(-1), g.reshape(-1), own_grad, target_grad)


def solution(mesh):
    return jax.shard_map(
        body,
        mesh=mesh,
        in_specs=(
            P(None, "src"),
            P(None, "tgt"),
            P("src"),
            P("tgt"),
            P("tgt"),
            P("src", "tgt", None),
            P("src", "tgt", None),
            P("src", "tgt"),
        ),
        out_specs=(P("src"), P("tgt"), P(None, ("src", "tgt")), P(None, "tgt")),
        check_vma=False,
    )
```

```python
import functools
import math

import jax
import jax.numpy as jnp
from jax import lax
from jax.experimental import pallas as pl
from jax.experimental.pallas import tpu as pltpu
from jax.sharding import PartitionSpec as P

CLUSTER = 512
EPSILON = 0.02
KAPPA = math.log2(math.e) / EPSILON
LOG2E = math.log2(math.e)
DEPTH = 32
F32 = jnp.float32
BF16 = jnp.bfloat16


def log2(value):
    return jnp.log(value) * LOG2E


def split(value):
    high = value.astype(BF16).astype(F32)
    rest = value - high
    middle = rest.astype(BF16).astype(F32)
    return (high, middle, rest - middle)


def half_square(points):
    return 0.5 * (points[0:1] * points[0:1] + points[1:2] * points[1:2] + points[2:3] * points[2:3])


def place(scratch, parts, order):
    scratch[...] = jnp.zeros_like(scratch)
    for at, which in enumerate(order):
        scratch[3 * at : 3 * at + 3, :] = parts[which]


SOURCE_ORDER = (0, 0, 1, 0, 2, 1)
TARGET_ORDER = (0, 1, 0, 2, 0, 1)


def with_rows(out, static, first, second):
    out[0:16, :] = static[0:16, :]
    low = static[16:32, :].astype(F32)
    row = lax.broadcasted_iota(jnp.int32, low.shape, 0)
    for at, part in enumerate(tuple(first) + tuple(second)):
        low = jnp.where(row == 2 + at, part, low)
    out[16:32, :] = low.astype(BF16)


ONES = (1.0, 1.0, 1.0)
ZEROS = (0.0, 0.0, 0.0)


def scores(left, right):
    return lax.dot_general(left, right, (((0,), (0,)), ((), ())), preferred_element_type=F32)


def start_of(index):
    return pl.multiple_of(index * CLUSTER, CLUSTER)


def grouped(value):
    return value.reshape(value.shape[0] // 8, 8, value.shape[1])


def each_tile(tiles, left, right, chunk, unroll, visit, first, more):
    count, red_at, kept_at = tiles
    turned = left.shape[1] == DEPTH
    once = right.shape[1] // CLUSTER

    def tile(slot, done):
        r = start_of(red_at[0, 0, slot])
        here = pl.ds(start_of(kept_at[0, 0, slot]), CLUSTER)
        kept = right[:, here]
        state = None
        for at in range(CLUSTER // chunk):
            rows = pl.ds(pl.multiple_of(r + at * chunk, chunk), chunk)
            if turned:
                s = jnp.dot(left[rows, :], kept, preferred_element_type=F32)
            else:
                s = scores(left[:, rows], kept)
            state = visit(grouped(s), state, rows)
        done(here, state)

    def several(at, carry):
        for k in range(unroll):
            tile(at * unroll + k, first)
        return carry

    def one(slot, carry):
        tile(slot, more)
        return carry

    lax.fori_loop(0, once // unroll, several, 0)
    lax.fori_loop(once, count[0, 0], one, 0)


def weighed(p, columns, rows):
    for c in range(3):
        col = columns[rows, 128 * c : 128 * (c + 1)]
        col = jnp.concatenate([col] * (CLUSTER // 128), axis=1).reshape(p.shape)
        yield jnp.sum(p * col, axis=0)


def lse_tiles(tiles, left, right, top, sums, chunk, unroll, columns=None):
    def visit(s, state, rows):
        largest = jnp.max(s, axis=0)
        new = largest if state is None else jnp.maximum(state[0], largest)
        p = jnp.exp2(s - new[None])
        totals = [jnp.sum(p, axis=0)]
        if columns is not None:
            totals += weighed(p, columns, rows)
        if state is not None:
            scale = jnp.exp2(state[0] - new)
            totals = [old * scale + total for old, total in zip(state[1:], totals)]
        return [new] + totals

    def first(here, state):
        top[:, here] = state[0]
        for c, total in enumerate(state[1:]):
            sums[c, :, here] = total

    def more(here, state):
        old = top[:, here]
        new = jnp.maximum(old, state[0])
        before, now = jnp.exp2(old - new), jnp.exp2(state[0] - new)
        top[:, here] = new
        for c, total in enumerate(state[1:]):
            sums[c, :, here] = sums[c, :, here] * before + total * now

    each_tile(tiles, left, right, chunk, unroll, visit, first, more)
    m = top[...]
    largest = jnp.max(m, axis=0, keepdims=True)
    scale = jnp.exp2(m - largest)
    whole, *others = [jnp.sum(sums[c] * scale, axis=0, keepdims=True) for c in range(sums.shape[0])]
    return [largest + log2(whole)] + [other / whole for other in others]


def combine(parts):
    largest = functools.reduce(jnp.maximum, parts)
    terms = [jnp.exp2(part - largest) for part in parts]
    whole = functools.reduce(jnp.add, terms)
    return largest + log2(whole), [term / whole for term in terms]


def rows_of(refs):
    return [refs[at] for at in range(refs.shape[0])]


def spread_columns(columns, points, start):
    def step(at, carry):
        here = pl.ds(start_of(at), CLUSTER)
        block = points[0:8, here].T
        for c in range(3):
            columns[here, 128 * c : 128 * (c + 1)] = jnp.broadcast_to(block[:, start + c : start + c + 1], (CLUSTER, 128))
        return carry

    lax.fori_loop(0, columns.shape[0] // CLUSTER, step, 0)


def fetch(lists_in, lists, sem):
    copy = pltpu.make_async_copy(lists_in, lists, sem)
    copy.start()
    return copy


class List:
    def __init__(self, ref, first):
        self.ref, self.first = ref, first

    def __getitem__(self, at):
        return self.ref[self.first + at[-1]]


def lists_of(ref):
    slots = (ref.shape[0] - 1) // 2
    return List(ref, 2 * slots), List(ref, 0), List(ref, slots)


def turn(out, operand):
    out[...] = operand[...].T


def repeat(out, value):
    for at in range(out.shape[0]):
        out[at] = value


def first_row_kernel(points, lists_in, xc_out, yc_out, part_out, lists, sem, stack, red, turned, kept, top, total):
    copy = fetch(lists_in, lists, sem)
    xs, ys = points[0:3, :], points[3:6, :]
    place(stack, split(ys * KAPPA), TARGET_ORDER)
    yc_out[...] = stack[...].astype(BF16)
    potential = log2(points[7:8, :]) + KAPPA * (points[8:9, :] - half_square(ys))
    with_rows(red, yc_out, split(potential), ONES)
    turn(turned, red)
    place(stack, split(xs), SOURCE_ORDER)
    xc_out[...] = stack[...].astype(BF16)
    with_rows(kept, xc_out, ONES, ZEROS)
    copy.wait()
    count, t_src, t_tgt = lists_of(lists)
    part_out[...] = lse_tiles((count, t_tgt, t_src), turned, kept, top, total, 128, 4)[0]


def col_kernel(parts, points, xc, yc, lists_in, part_out, lists, sem, red, turned, kept, top, total):
    copy = fetch(lists_in, lists, sem)
    potential = log2(points[6:7, :]) - combine([parts[at] for at in range(parts.shape[0])])[0]
    with_rows(red, xc, split(potential), ONES)
    turn(turned, red)
    with_rows(kept, yc, ONES, ZEROS)
    copy.wait()
    count, t_src, t_tgt = lists_of(lists)
    repeat(part_out, lse_tiles((count, t_src, t_tgt), turned, kept, top, total, 128, 2)[0])


def row_kernel(parts, points, xc, yc, lists_in, part_out, lists, sem, red, turned, kept, top, total):
    copy = fetch(lists_in, lists, sem)
    potential = log2(points[7:8, :]) - combine([parts[at] for at in range(parts.shape[0])])[0]
    with_rows(red, yc, split(potential), ONES)
    turn(turned, red)
    with_rows(kept, xc, ONES, ZEROS)
    copy.wait()
    count, t_src, t_tgt = lists_of(lists)
    part_out[...] = lse_tiles((count, t_tgt, t_src), turned, kept, top, total, 256, 2)[0]


def last_col_kernel(
    parts, points, xc, yc, lists_in, f_out, u_out, part_out, lists, sem, red, turned, kept, top, total, columns
):
    copy = fetch(lists_in, lists, sem)
    u = -combine([parts[at] for at in range(parts.shape[0])])[0]
    u_out[...] = u
    f_out[...] = u * (1.0 / KAPPA) + half_square(points[0:3, :])
    with_rows(red, xc, split(log2(points[6:7, :]) + u), ONES)
    with_rows(kept, yc, ONES, ZEROS)
    turn(turned, red)
    spread_columns(columns, points, 0)
    copy.wait()
    count, t_src, t_tgt = lists_of(lists)
    cut(part_out, lse_tiles((count, t_src, t_tgt), turned, kept, top, total, 128, 2, columns))


def cut(out, rows):
    width = out.shape[2]
    for r, row in enumerate(rows):
        for at in range(out.shape[0]):
            out[at, r : r + 1, :] = row[:, at * width : (at + 1) * width]


def combine_kernel(parts, out):
    n = parts.shape[0]
    lse, shares = combine([parts[at, 0:1, :] for at in range(n)])
    means = [functools.reduce(jnp.add, [shares[at] * parts[at, c : c + 1, :] for at in range(n)]) for c in (1, 2, 3)]
    for at in range(n):
        for r, row in enumerate([lse] + means):
            out[at, r : r + 1, :] = row


def gradient_kernel(
    parts, u, points, xc, yc, lists_in, g_out, target_out, source_out, lists, sem, red, turned, kept, sums, columns
):
    copy = fetch(lists_in, lists, sem)
    joined = [jnp.concatenate([parts[at, r : r + 1, :] for at in range(parts.shape[0])], axis=1) for r in range(4)]
    xs, ys = points[0:3, :], points[3:6, :]
    v = -joined[0]
    g_out[...] = v * (1.0 / KAPPA) + half_square(ys)
    for c in range(3):
        target_out[c : c + 1, :] = points[7:8, :] * (ys[c : c + 1, :] - joined[c + 1])
    with_rows(red, yc, split(log2(points[7:8, :]) + v), ONES)
    with_rows(kept, xc, ONES, split(log2(points[6:7, :]) + u[...]))
    turn(turned, red)
    spread_columns(columns, points, 3)
    copy.wait()
    count, t_src, t_tgt = lists_of(lists)

    def visit(s, state, rows):
        p = jnp.exp2(s)
        totals = [jnp.sum(p, axis=0)] + list(weighed(p, columns, rows))
        return totals if state is None else [old + new for old, new in zip(state, totals)]

    def first(here, state):
        for c, value in enumerate(state):
            sums[c, :, here] = value

    def more(here, state):
        for c, value in enumerate(state):
            sums[c, :, here] += value

    each_tile((count, t_tgt, t_src), turned, kept, 128, 2, visit, first, more)
    mass, *moved = [jnp.sum(sums[c], axis=0, keepdims=True) for c in range(4)]
    cut(source_out, [xs[c : c + 1, :] * mass - moved[c] for c in range(3)])


VMEM = pl.BlockSpec(memory_space=pltpu.VMEM)
HBM = pl.BlockSpec(memory_space=pltpu.HBM)


def call(kernel, ins, lists, outs, scratch):
    return pl.pallas_call(
        kernel,
        out_shape=outs,
        in_specs=[VMEM] * len(ins) + [HBM] * len(lists),
        out_specs=[VMEM] * len(outs),
        scratch_shapes=scratch,
        compiler_params=pltpu.CompilerParams(vmem_limit_bytes=48 * 1024 * 1024),
    )(*ins, *lists)


def body(source_points, target_points, source_weight, target_weight, target_start, tile_source, tile_target, tile_count):
    ns, nt = source_points.shape[1], target_points.shape[1]
    n_src, n_tgt = lax.axis_size("src"), lax.axis_size("tgt")
    points = jnp.concatenate(
        [source_points, target_points] + [a.reshape(1, -1) for a in (source_weight, target_weight, target_start)]
    )
    lists = (jnp.concatenate([a.reshape(-1) for a in (tile_source, tile_target, tile_count)]),)

    def rows(n, *k):
        return jax.ShapeDtypeStruct((*k, n), F32)

    def split_rows(n):
        return jax.ShapeDtypeStruct((DEPTH, n), BF16)

    def work(red, kept):
        whole = [pltpu.SMEM(lists[0].shape, jnp.int32), pltpu.SemaphoreType.DMA, pltpu.VMEM((DEPTH, red), BF16)]
        whole += [pltpu.VMEM((red, DEPTH), BF16)]
        return whole + [pltpu.VMEM((DEPTH, kept), BF16)]

    def state(kept, totals=1):
        return [pltpu.VMEM((8, kept), F32), pltpu.VMEM((totals, 8, kept), F32)]

    first = work(nt, ns)
    xc, yc, part = call(
        first_row_kernel,
        (points,),
        lists,
        [split_rows(ns), split_rows(nt), rows(ns, 1)],
        first[:2] + [pltpu.VMEM((DEPTH, ns), F32)] + first[2:] + state(ns),
    )
    known = (points, xc, yc)
    (part,) = call(
        col_kernel, (lax.all_gather(part, "tgt"), *known), lists, [rows(nt, n_src, 1)], work(ns, nt) + state(nt)
    )
    (part,) = call(
        row_kernel, (lax.all_to_all(part, "src", 0, 0), *known), lists, [rows(ns, 1)], work(nt, ns) + state(ns)
    )
    f, u, part = call(
        last_col_kernel,
        (lax.all_gather(part, "tgt"), *known),
        lists,
        [rows(ns, 1), rows(ns, 1), rows(nt // n_src, n_src, 4)],
        work(ns, nt) + state(nt, 4) + [pltpu.VMEM((ns, 384), F32)],
    )
    (part,) = call(combine_kernel, (lax.all_to_all(part, "src", 0, 0),), (), [rows(nt // n_src, n_src, 4)], [])
    g, target_grad, part = call(
        gradient_kernel,
        (lax.all_to_all(part, "src", 0, 0), u, *known),
        lists,
        [rows(nt, 1), rows(nt, 3), rows(ns // n_tgt, n_tgt, 3)],
        work(nt, ns) + [pltpu.VMEM((4, 8, ns), F32), pltpu.VMEM((nt, 384), F32)],
    )
    own_grad = jnp.sum(lax.all_to_all(part, "tgt", 0, 0), axis=0)
    return (f.reshape(-1), g.reshape(-1), own_grad, target_grad)


def solution(mesh):
    return jax.shard_map(
        body,
        mesh=mesh,
        in_specs=(
            P(None, "src"),
            P(None, "tgt"),
            P("src"),
            P("tgt"),
            P("tgt"),
            P("src", "tgt", None),
            P("src", "tgt", None),
            P("src", "tgt"),
        ),
        out_specs=(P("src"), P("tgt"), P(None, ("src", "tgt")), P(None, "tgt")),
        check_vma=False,
    )
```

```python
import functools
import math

import jax
import jax.numpy as jnp
from jax import lax
from jax.experimental import pallas as pl
from jax.experimental.pallas import tpu as pltpu
from jax.sharding import PartitionSpec as P

CLUSTER = 512
EPSILON = 0.02
KAPPA = math.log2(math.e) / EPSILON
LOG2E = math.log2(math.e)
DEPTH = 32
FLOOR = -1e30
F32 = jnp.float32
BF16 = jnp.bfloat16


def log2(value):
    return jnp.log(value) * LOG2E


def split(value):
    high = value.astype(BF16).astype(F32)
    rest = value - high
    middle = rest.astype(BF16).astype(F32)
    return (high, middle, rest - middle)


def half_square(points):
    return 0.5 * (points[0:1] * points[0:1] + points[1:2] * points[1:2] + points[2:3] * points[2:3])


SOURCE_ORDER = (0, 1, 2, 0, 0, 1)
TARGET_ORDER = (0, 0, 0, 1, 2, 1)
TARGET_PARTS = (0, 9, 12)
ONE = 15


def place(scratch, parts, order):
    scratch[...] = jnp.zeros_like(scratch)
    for at, which in enumerate(order[:5]):
        scratch[3 * at : 3 * at + 3, :] = parts[which]
    scratch[ONE : ONE + 1, :] = jnp.ones_like(parts[0][0:1])
    scratch[16:19, :] = parts[order[5]]


def with_rows(out, static, first, second):
    out[0:16, :] = static[0:16, :]
    low = static[16:32, :].astype(F32)
    row = lax.broadcasted_iota(jnp.int32, low.shape, 0)
    for at, part in enumerate(tuple(first) + tuple(second)):
        low = jnp.where(row == 3 + at, part, low)
    out[16:32, :] = low.astype(BF16)


def pieces(potential):
    return split(potential - 1.0)


ONES = (1.0, 1.0, 1.0)
ZEROS = (0.0, 0.0, 0.0)


def scores(left, right):
    return lax.dot_general(left, right, (((0,), (0,)), ((), ())), preferred_element_type=F32)


def start_of(index):
    return pl.multiple_of(index * CLUSTER, CLUSTER)


def grouped(value):
    return value.reshape(value.shape[0] // 8, 8, value.shape[1])


def each_tile(tiles, left, right, visit, first, more, chunk=128, unroll=2, ahead=0, halves=False):
    slots = tiles.slots
    once = right.shape[1] // CLUSTER

    def product(left_rows, kept):
        if not halves:
            return jnp.dot(left_rows, kept, preferred_element_type=F32)
        half = CLUSTER // 2
        both = [jnp.dot(left_rows, kept[:, at * half : (at + 1) * half], preferred_element_type=F32) for at in (0, 1)]
        return jnp.concatenate(both, axis=1)

    def tile_group(group):
        steps = []
        for which, slot in enumerate(group):
            r, k = tiles.starts(slot)
            for at in range(CLUSTER // chunk):
                steps.append((which, pl.ds(k, CLUSTER), pl.ds(pl.multiple_of(r + at * chunk, chunk), chunk)))
        states = [None] * len(group)
        scores = [None] * len(steps)

        def start(n):
            if n < len(steps):
                which, here, rows = steps[n]
                scores[n] = grouped(product(left[rows, :], right[:, here]))

        for n in range(ahead):
            start(n)
        for n, (which, here, rows) in enumerate(steps):
            start(n + ahead)
            states[which] = visit(scores[n], states[which], rows)
        return [(steps[which * (CLUSTER // chunk)][1], state) for which, state in enumerate(states)]

    def several(at, carry):
        for here, state in tile_group([at * unroll + k for k in range(unroll)]):
            first(here, state)
        return carry

    def others(at, carry):
        group = [jnp.minimum(once + at * 2 + k, slots - 1) for k in range(2)]
        live = [once + at * 2 + k < tiles.count() for k in range(2)]
        for alive, (here, state) in zip(live, tile_group(group)):
            more(here, state, alive)
        return carry

    lax.fori_loop(0, once // unroll, several, 0)
    lax.fori_loop(0, lax.div(tiles.count() - once + 1, 2), others, 0)


def lse_tiles(tiles, left, right, top, total, **how):
    def visit(s, state, rows):
        largest = jnp.max(s, axis=0)
        if state is None:
            return largest, jnp.sum(jnp.exp2(s - largest[None]), axis=0)
        new = jnp.maximum(state[0], largest)
        return new, state[1] * jnp.exp2(state[0] - new) + jnp.sum(jnp.exp2(s - new[None]), axis=0)

    def first(here, state):
        top[:, here], total[:, here] = state

    def more(here, state, live):
        old, m = top[:, here], jnp.where(live, state[0], FLOOR)
        new = jnp.maximum(old, m)
        top[:, here] = new
        total[:, here] = total[:, here] * jnp.exp2(old - new) + state[1] * jnp.exp2(m - new)

    each_tile(tiles, left, right, visit, first, more, **how)
    m = top[...]
    largest = jnp.max(m, axis=0, keepdims=True)
    return largest + log2(jnp.sum(total[...] * jnp.exp2(m - largest), axis=0, keepdims=True))


def moments(p, static, rows):
    p = p.reshape(p.shape[0] * 8, p.shape[2])
    high = p.astype(BF16)
    low = (p - high.astype(F32)).astype(BF16)
    weights = static[0:16, rows]
    half = CLUSTER // 2
    both = []
    for at in (0, 1):
        here = slice(at * half, (at + 1) * half)
        both.append(sum(jnp.dot(weights, part[:, here], preferred_element_type=F32) for part in (high, low)))
    return jnp.concatenate(both, axis=1)


def joined(sums, parts):
    return [functools.reduce(jnp.add, [sums[at + c : at + c + 1, :] for at in parts]) for c in range(3)]


def weighed(p, columns, rows):
    for c in range(3):
        col = columns[rows, 128 * c : 128 * (c + 1)]
        col = jnp.concatenate([col] * (CLUSTER // 128), axis=1).reshape(p.shape)
        yield jnp.sum(p * col, axis=0)


def mean_tiles(tiles, left, right, columns, top, sums, **how):
    def visit(s, state, rows):
        largest = jnp.max(s, axis=0)
        new = largest if state is None else jnp.maximum(state[0], largest)
        p = jnp.exp2(s - new[None])
        totals = [jnp.sum(p, axis=0)] + list(weighed(p, columns, rows))
        if state is not None:
            scale = jnp.exp2(state[0] - new)
            totals = [old * scale + total for old, total in zip(state[1:], totals)]
        return [new] + totals

    def first(here, state):
        top[:, here] = state[0]
        for c, total in enumerate(state[1:]):
            sums[c, :, here] = total

    def more(here, state, live):
        old, m = top[:, here], jnp.where(live, state[0], FLOOR)
        new = jnp.maximum(old, m)
        before, now = jnp.exp2(old - new), jnp.exp2(m - new)
        top[:, here] = new
        for c, total in enumerate(state[1:]):
            sums[c, :, here] = sums[c, :, here] * before + total * now

    each_tile(tiles, left, right, visit, first, more, **how)
    m = top[...]
    largest = jnp.max(m, axis=0, keepdims=True)
    scale = jnp.exp2(m - largest)
    mass, *others = [jnp.sum(sums[c] * scale, axis=0, keepdims=True) for c in range(4)]
    return [largest + log2(mass)] + [other / mass for other in others]


def spread_columns(columns, points, start):
    def step(at, carry):
        here = pl.ds(start_of(at), CLUSTER)
        block = points[0:8, here].T
        for c in range(3):
            columns[here, 128 * c : 128 * (c + 1)] = jnp.broadcast_to(block[:, start + c : start + c + 1], (CLUSTER, 128))
        return carry

    lax.fori_loop(0, columns.shape[0] // CLUSTER, step, 0)


def plan_tiles(tiles, left, right, static, parts, sums, **how):
    def visit(s, state, rows):
        total = moments(jnp.exp2(s), static, rows)
        return total if state is None else state + total

    def first(here, state):
        sums[:, here] = state

    def more(here, state, live):
        sums[:, here] += jnp.where(live, state, 0.0)

    each_tile(tiles, left, right, visit, first, more, **how)
    return [sums[ONE : ONE + 1, :]] + joined(sums, parts)


def combine(parts):
    largest = functools.reduce(jnp.maximum, parts)
    terms = [jnp.exp2(part - largest) for part in parts]
    whole = functools.reduce(jnp.add, terms)
    return largest + log2(whole), [term / whole for term in terms]


def rows_of(refs):
    return [refs[at] for at in range(refs.shape[0])]


class Tiles:
    def __init__(self, ref, points, kept_source):
        self.ref, self.slots, self.kept_source = ref, ref.shape[-1], kept_source
        self.sources, self.targets = points

    def count(self):
        return lax.div(self.ref[0, 0, 0], self.sources * self.targets)

    def starts(self, slot):
        packed = self.ref[0, 0, slot]
        source = start_of(lax.rem(packed, self.sources))
        target = start_of(lax.rem(lax.div(packed, self.sources), self.targets))
        return (target, source) if self.kept_source else (source, target)


def fetch(lists_in, lists, sem):
    copy = pltpu.make_async_copy(lists_in, lists, sem)
    copy.start()
    return copy


def turn(out, operand):
    out[...] = operand[...].T


def repeat(out, value):
    for at in range(out.shape[0]):
        out[at] = value


def sides(xc, yc):
    return xc.shape[1] // CLUSTER, yc.shape[1] // CLUSTER


def first_row_kernel(points, lists_in, xc_out, yc_out, part_out, lists, sem, stack, red, turned, kept, top, total):
    copy = fetch(lists_in, lists, sem)
    xs, ys = points[0:3, :], points[3:6, :]
    place(stack, split(ys * KAPPA), TARGET_ORDER)
    yc_out[...] = stack[...].astype(BF16)
    potential = log2(points[7:8, :]) + KAPPA * (points[8:9, :] - half_square(ys))
    with_rows(red, yc_out, pieces(potential), ONES)
    turn(turned, red)
    place(stack, split(xs), SOURCE_ORDER)
    xc_out[...] = stack[...].astype(BF16)
    with_rows(kept, xc_out, ONES, ZEROS)
    copy.wait()
    part_out[...] = lse_tiles(Tiles(lists, sides(kept, red), True), turned, kept, top, total, unroll=4, ahead=1)


def col_kernel(parts, points, xc, yc, lists_in, part_out, lists, sem, red, turned, kept, top, total):
    copy = fetch(lists_in, lists, sem)
    potential = log2(points[6:7, :]) - combine([ref[...] for ref in parts])[0]
    with_rows(red, xc, pieces(potential), ONES)
    turn(turned, red)
    with_rows(kept, yc, ONES, ZEROS)
    copy.wait()
    repeat(part_out, lse_tiles(Tiles(lists, sides(xc, yc), False), turned, kept, top, total, halves=True))


def row_kernel(parts, points, xc, yc, lists_in, part_out, lists, sem, red, turned, kept, top, total):
    copy = fetch(lists_in, lists, sem)
    potential = log2(points[7:8, :]) - combine([parts[at] for at in range(parts.shape[0])])[0]
    with_rows(red, yc, pieces(potential), ONES)
    turn(turned, red)
    with_rows(kept, xc, ONES, ZEROS)
    copy.wait()
    part_out[...] = lse_tiles(Tiles(lists, sides(xc, yc), True), turned, kept, top, total, unroll=8)


def last_col_kernel(
    parts, points, xc, yc, lists_in, f_out, u_out, part_out, lists, sem, red, turned, kept, top, sums, columns, f, sem_out
):
    copy = fetch(lists_in, lists, sem)
    u = -combine([ref[...] for ref in parts])[0]
    u_out[...] = u
    f[...] = u * (1.0 / KAPPA) + half_square(points[0:3, :])
    back = fetch(f, f_out, sem_out)
    with_rows(red, xc, pieces(log2(points[6:7, :]) + u), ONES)
    turn(turned, red)
    with_rows(kept, yc, ONES, ZEROS)
    copy.wait()
    tiles = Tiles(lists, sides(xc, yc), False)
    spread_columns(columns, points, 0)
    cut(part_out, mean_tiles(tiles, turned, kept, columns, top, sums))
    back.wait()


def cut(out, rows):
    width = out.shape[2]
    for r, row in enumerate(rows):
        for at in range(out.shape[0]):
            out[at, r : r + 1, :] = row[:, at * width : (at + 1) * width]


def combine_kernel(parts, out):
    n = parts.shape[0]
    lse, shares = combine([parts[at, 0:1, :] for at in range(n)])
    means = [functools.reduce(jnp.add, [shares[at] * parts[at, c : c + 1, :] for at in range(n)]) for c in (1, 2, 3)]
    for at in range(n):
        for r, row in enumerate([lse] + means):
            out[at, r : r + 1, :] = row


def gradient_kernel(
    parts, u, points, xc, yc, lists_in, g_out, target_out, *rest, shares
):
    source_out, (lists, sem, red, turned, kept, sums, g, target, whole, sems) = rest[:shares], rest[shares:]
    copy = fetch(lists_in, lists, sem)
    lse, *means = [jnp.concatenate([parts[at, r : r + 1, :] for at in range(parts.shape[0])], axis=1) for r in range(4)]
    xs, ys = points[0:3, :], points[3:6, :]
    g[...] = half_square(ys) - lse * (1.0 / KAPPA)
    for c in range(3):
        target[c : c + 1, :] = points[7:8, :] * (ys[c : c + 1, :] - means[c])
    back = [fetch(g, g_out, sems.at[0]), fetch(target, target_out, sems.at[1])]
    with_rows(red, yc, pieces(log2(points[7:8, :]) - lse), ONES)
    turn(turned, red)
    with_rows(kept, xc, ONES, split(log2(points[6:7, :]) + u[...]))
    copy.wait()
    tiles = Tiles(lists, sides(xc, yc), True)
    mass, *moved = plan_tiles(tiles, turned, kept, yc, TARGET_PARTS, sums)
    for c in range(3):
        whole[c : c + 1, :] = xs[c : c + 1, :] * mass - moved[c] * (1.0 / KAPPA)
    place_tgt = lax.axis_index("tgt")
    for k, out in enumerate(source_out):
        width = out.shape[1]
        at = pl.multiple_of(peer(place_tgt, k, shares) * width, width)
        out[...] = whole[:, pl.ds(at, width)]
    for one in back:
        one.wait()


VMEM = pl.BlockSpec(memory_space=pltpu.VMEM)
HBM = pl.BlockSpec(memory_space=pltpu.HBM)


def call(kernel, ins, lists, outs, scratch, far=()):
    return pl.pallas_call(
        kernel,
        out_shape=outs,
        in_specs=[VMEM] * len(ins) + [HBM] * len(lists),
        out_specs=[HBM if at in far else VMEM for at in range(len(outs))],
        scratch_shapes=scratch,
        compiler_params=pltpu.CompilerParams(vmem_limit_bytes=48 * 1024 * 1024),
    )(*ins, *lists)


def peer(i, k, n):
    return i ^ k if n & (n - 1) == 0 else (i + k) % n


def exchange(values, axis):
    n = lax.axis_size(axis)
    return values[:1] + [
        lax.ppermute(values[k], axis, [(i, peer(i, k, n)) for i in range(n)]) for k in range(1, n)
    ]


def body(source_points, target_points, source_weight, target_weight, target_start, tile_source, tile_target, tile_count):
    ns, nt = source_points.shape[1], target_points.shape[1]
    n_src, n_tgt = lax.axis_size("src"), lax.axis_size("tgt")
    points = jnp.concatenate(
        [source_points, target_points] + [a.reshape(1, -1) for a in (source_weight, target_weight, target_start)]
    )
    lists = ((tile_count[:, :, None] * (nt // CLUSTER) + tile_target) * (ns // CLUSTER) + tile_source,)

    def rows(n, *k):
        return jax.ShapeDtypeStruct((*k, n), F32)

    def split_rows(n):
        return jax.ShapeDtypeStruct((DEPTH, n), BF16)

    def work(red, kept):
        return [
            pltpu.SMEM(lists[0].shape, jnp.int32),
            pltpu.SemaphoreType.DMA,
            pltpu.VMEM((DEPTH, red), BF16),
            pltpu.VMEM((red, DEPTH), BF16),
            pltpu.VMEM((DEPTH, kept), BF16),
        ]

    def state(kept):
        return [pltpu.VMEM((8, kept), F32), pltpu.VMEM((8, kept), F32)]

    first = work(nt, ns)
    xc, yc, part = call(
        first_row_kernel,
        (points,),
        lists,
        [split_rows(ns), split_rows(nt), rows(ns, 1)],
        first[:2] + [pltpu.VMEM((DEPTH, ns), F32)] + first[2:] + state(ns),
    )
    known = (points, xc, yc)
    parts = exchange([part] * n_tgt, "tgt")
    (part,) = call(
        lambda *refs: col_kernel(refs[:n_tgt], *refs[n_tgt:]),
        (*parts, *known),
        lists,
        [rows(nt, n_src, 1)],
        work(ns, nt) + state(nt),
    )
    (part,) = call(
        row_kernel, (lax.all_to_all(part, "src", 0, 0), *known), lists, [rows(ns, 1)], work(nt, ns) + state(ns)
    )
    parts = exchange([part] * n_tgt, "tgt")
    f, u, part = call(
        lambda *refs: last_col_kernel(refs[:n_tgt], *refs[n_tgt:]),
        (*parts, *known),
        lists,
        [rows(ns, 1), rows(ns, 1), rows(nt // n_src, n_src, 4)],
        work(ns, nt)
        + [
            pltpu.VMEM((8, nt), F32),
            pltpu.VMEM((4, 8, nt), F32),
            pltpu.VMEM((ns, 384), F32),
            pltpu.VMEM((1, ns), F32),
            pltpu.SemaphoreType.DMA,
        ],
        far=(0,),
    )
    (part,) = call(combine_kernel, (lax.all_to_all(part, "src", 0, 0),), (), [rows(nt // n_src, n_src, 4)], [])
    g, target_grad, *parts = call(
        functools.partial(gradient_kernel, shares=n_tgt),
        (lax.all_to_all(part, "src", 0, 0), u, *known),
        lists,
        [rows(nt, 1), rows(nt, 3)] + [rows(ns // n_tgt, 3)] * n_tgt,
        work(nt, ns)
        + [
            pltpu.VMEM((16, ns), F32),
            pltpu.VMEM((1, nt), F32),
            pltpu.VMEM((3, nt), F32),
            pltpu.VMEM((3, ns), F32),
            pltpu.SemaphoreType.DMA((2,)),
        ],
        far=(0, 1),
    )
    own_grad = functools.reduce(jnp.add, exchange(parts, "tgt"))
    return (f.reshape(-1), g.reshape(-1), own_grad, target_grad)


def solution(mesh):
    return jax.shard_map(
        body,
        mesh=mesh,
        in_specs=(
            P(None, "src"),
            P(None, "tgt"),
            P("src"),
            P("tgt"),
            P("tgt"),
            P("src", "tgt", None),
            P("src", "tgt", None),
            P("src", "tgt"),
        ),
        out_specs=(P("src"), P("tgt"), P(None, ("src", "tgt")), P(None, "tgt")),
        check_vma=False,
    )
```

```python
import functools
import math

import jax
import jax.numpy as jnp
from jax import lax
from jax.experimental import pallas as pl
from jax.experimental.pallas import tpu as pltpu
from jax.sharding import PartitionSpec as P

CLUSTER = 512
EPSILON = 0.02
KAPPA = math.log2(math.e) / EPSILON
LOG2E = math.log2(math.e)
DEPTH = 32
FLOOR = -1e30
EXTRAS = 4
F32 = jnp.float32
BF16 = jnp.bfloat16


def log2(value):
    return jnp.log(value) * LOG2E


def split(value):
    high = value.astype(BF16).astype(F32)
    rest = value - high
    middle = rest.astype(BF16).astype(F32)
    return (high, middle, rest - middle)


def half_square(points):
    return 0.5 * (points[0:1] * points[0:1] + points[1:2] * points[1:2] + points[2:3] * points[2:3])


SOURCE_ORDER = (0, 1, 2, 0, 0, 1)
TARGET_ORDER = (0, 0, 0, 1, 2, 1)
ONE = 15


def place(scratch, parts, order):
    scratch[...] = jnp.zeros_like(scratch)
    for at, which in enumerate(order[:5]):
        scratch[3 * at : 3 * at + 3, :] = parts[which]
    scratch[ONE : ONE + 1, :] = jnp.ones_like(parts[0][0:1])
    scratch[16:19, :] = parts[order[5]]
    scratch[19:22, :] = jnp.ones_like(parts[0])


def with_rows(out, static, first, second=()):
    out[0:16, :] = static[0:16, :]
    low = static[16:32, :].astype(F32)
    row = lax.broadcasted_iota(jnp.int32, low.shape, 0)
    for at, part in enumerate(tuple(first) + tuple(second)):
        low = jnp.where(row == 3 + at, part, low)
    out[16:32, :] = low.astype(BF16)


def pieces(potential):
    return split(potential - 1.0)


ONES = (1.0, 1.0, 1.0)


def scores(left, right):
    return lax.dot_general(left, right, (((0,), (0,)), ((), ())), preferred_element_type=F32)


def start_of(index):
    return pl.multiple_of(index * CLUSTER, CLUSTER)


def grouped(value):
    return value.reshape(value.shape[0] // 8, 8, value.shape[1])


def each_tile(tiles, left, right, visit, first, more, unroll=8, ahead=1, chunk=128):
    once = right.shape[1] // CLUSTER

    def group_states(group, fresh):
        steps = []
        for which, slot in enumerate(group):
            r, k = tiles.starts(slot)
            for at in range(CLUSTER // chunk):
                steps.append((which, pl.ds(k, CLUSTER), pl.ds(pl.multiple_of(r + at * chunk, chunk), chunk)))
        states = [None] * len(group)
        scores = [None] * len(steps)

        def start(n):
            if n < len(steps):
                which, here, rows = steps[n]
                scores[n] = grouped(jnp.dot(left[rows, :], right[:, here], preferred_element_type=F32))

        for n in range(ahead):
            start(n)
        for n, (which, here, rows) in enumerate(steps):
            start(n + ahead)
            states[which] = visit(scores[n], states[which], rows, fresh)
        return [(steps[which * (CLUSTER // chunk)][1], state) for which, state in enumerate(states)]

    def several(at, carry):
        for here, state in group_states([at * unroll + k for k in range(unroll)], True):
            first(here, state)
        return carry

    def others(at, carry):
        slots = [once + at * EXTRAS + k for k in range(EXTRAS)]
        states = group_states([jnp.minimum(slot, tiles.slots - 1) for slot in slots], False)
        for slot, (here, state) in zip(slots, states):
            more(here, state, slot < tiles.count())
        return carry

    lax.fori_loop(0, once // unroll, several, 0)
    lax.fori_loop(0, lax.div(tiles.count() - once + EXTRAS - 1, EXTRAS), others, 0)


def lse_tiles(tiles, left, right, top, total, **how):
    def visit(s, state, rows, fresh):
        largest = jnp.max(s, axis=0)
        if state is None:
            return largest, jnp.sum(jnp.exp2(s - largest[None]), axis=0)
        new = jnp.maximum(state[0], largest)
        return new, state[1] * jnp.exp2(state[0] - new) + jnp.sum(jnp.exp2(s - new[None]), axis=0)

    def first(here, state):
        top[:, here], total[:, here] = state

    def more(here, state, live):
        old, m = top[:, here], jnp.where(live, state[0], FLOOR)
        new = jnp.maximum(old, m)
        top[:, here] = new
        total[:, here] = total[:, here] * jnp.exp2(old - new) + state[1] * jnp.exp2(m - new)

    each_tile(tiles, left, right, visit, first, more, **how)
    m = top[...]
    largest = jnp.max(m, axis=0, keepdims=True)
    return largest + log2(jnp.sum(total[...] * jnp.exp2(m - largest), axis=0, keepdims=True))


def weighed(p, columns, points, start, rows, fresh):
    block = points[0:8, rows].T if fresh else None
    for c in range(3):
        lanes = slice(128 * c, 128 * (c + 1))
        if fresh:
            col = jnp.broadcast_to(block[:, start + c : start + c + 1], (block.shape[0], 128))
            columns[rows, lanes] = col
        else:
            col = columns[rows, lanes]
        yield jnp.sum(p * jnp.concatenate([col] * (CLUSTER // 128), axis=1).reshape(p.shape), axis=0)


def mean_tiles(tiles, left, right, columns, points, start, top, sums, **how):
    def visit(s, state, rows, fresh):
        largest = jnp.max(s, axis=0)
        new = largest if state is None else jnp.maximum(state[0], largest)
        p = jnp.exp2(s - new[None])
        totals = [jnp.sum(p, axis=0)] + list(weighed(p, columns, points, start, rows, fresh))
        if state is not None:
            scale = jnp.exp2(state[0] - new)
            totals = [old * scale + total for old, total in zip(state[1:], totals)]
        return [new] + totals

    def first(here, state):
        top[:, here] = state[0]
        for c, total in enumerate(state[1:]):
            sums[c, :, here] = total

    def more(here, state, live):
        old, m = top[:, here], jnp.where(live, state[0], FLOOR)
        new = jnp.maximum(old, m)
        before, now = jnp.exp2(old - new), jnp.exp2(m - new)
        top[:, here] = new
        for c, total in enumerate(state[1:]):
            sums[c, :, here] = sums[c, :, here] * before + total * now

    each_tile(tiles, left, right, visit, first, more, **how)
    m = top[...]
    largest = jnp.max(m, axis=0, keepdims=True)
    scale = jnp.exp2(m - largest)
    mass, *others = [jnp.sum(sums[c] * scale, axis=0, keepdims=True) for c in range(4)]
    return [largest + log2(mass)] + [other / mass for other in others]


def plan_tiles(tiles, left, right, columns, points, start, sums, **how):
    def visit(s, state, rows, fresh):
        p = jnp.exp2(s)
        totals = [jnp.sum(p, axis=0)] + list(weighed(p, columns, points, start, rows, fresh))
        return totals if state is None else [old + new for old, new in zip(state, totals)]

    def first(here, state):
        for c, total in enumerate(state):
            sums[c, :, here] = total

    def more(here, state, live):
        for c, total in enumerate(state):
            sums[c, :, here] += jnp.where(live, total, 0.0)

    each_tile(tiles, left, right, visit, first, more, **how)
    return [jnp.sum(sums[c], axis=0, keepdims=True) for c in range(4)]


def combine(parts):
    largest = functools.reduce(jnp.maximum, parts)
    terms = [jnp.exp2(part - largest) for part in parts]
    whole = functools.reduce(jnp.add, terms)
    return largest + log2(whole), [term / whole for term in terms]


def rows_of(refs):
    return [refs[at] for at in range(refs.shape[0])]


class Tiles:
    def __init__(self, ref, points, kept_source):
        self.ref, self.slots, self.kept_source = ref, ref.shape[-1], kept_source
        self.sources, self.targets = points

    def count(self):
        return lax.div(self.ref[0, 0, 0], self.sources * self.targets)

    def starts(self, slot):
        packed = self.ref[0, 0, slot]
        source = start_of(lax.rem(packed, self.sources))
        target = start_of(lax.rem(lax.div(packed, self.sources), self.targets))
        return (target, source) if self.kept_source else (source, target)


def fetch(lists_in, lists, sem):
    copy = pltpu.make_async_copy(lists_in, lists, sem)
    copy.start()
    return copy


def turn(out, operand):
    out[...] = operand[...].T


def sides(xc, yc):
    return xc.shape[1] // CLUSTER, yc.shape[1] // CLUSTER


def first_row_kernel(points, lists_in, xc_out, yc_out, part_out, lists, sem, stack, red, turned, top, total):
    copy = fetch(lists_in, lists, sem)
    xs, ys = points[0:3, :], points[3:6, :]
    place(stack, split(ys * KAPPA), TARGET_ORDER)
    yc_out[...] = stack[...].astype(BF16)
    potential = log2(points[7:8, :]) + KAPPA * (points[8:9, :] - half_square(ys))
    with_rows(red, yc_out, pieces(potential))
    turn(turned, red)
    place(stack, split(xs), SOURCE_ORDER)
    xc_out[...] = stack[...].astype(BF16)
    copy.wait()
    part_out[...] = lse_tiles(Tiles(lists, sides(xc_out, yc_out), True), turned, xc_out, top, total)


def col_kernel(parts, points, xc, yc, lists_in, part_out, lists, sem, red, turned, top, total):
    copy = fetch(lists_in, lists, sem)
    potential = log2(points[6:7, :]) - combine([ref[...] for ref in parts])[0]
    with_rows(red, xc, pieces(potential))
    turn(turned, red)
    copy.wait()
    part_out[...] = lse_tiles(Tiles(lists, sides(xc, yc), False), turned, yc, top, total)


def row_kernel(parts, points, xc, yc, lists_in, part_out, lists, sem, red, turned, top, total):
    copy = fetch(lists_in, lists, sem)
    potential = log2(points[7:8, :]) - combine([ref[...] for ref in parts])[0]
    with_rows(red, yc, pieces(potential))
    turn(turned, red)
    copy.wait()
    part_out[...] = lse_tiles(Tiles(lists, sides(xc, yc), True), turned, xc, top, total)


def last_col_kernel(
    parts, points, xc, yc, lists_in, f_out, u_out, part_out, means_out, lists, sem, red, turned, top, sums, columns, f, sem_out
):
    copy = fetch(lists_in, lists, sem)
    u = -combine([ref[...] for ref in parts])[0]
    u_out[...] = u
    f[...] = u * (1.0 / KAPPA) + half_square(points[0:3, :])
    back = fetch(f, f_out, sem_out)
    with_rows(red, xc, pieces(log2(points[6:7, :]) + u))
    turn(turned, red)
    copy.wait()
    tiles = Tiles(lists, sides(xc, yc), False)
    part_out[...], *means = mean_tiles(tiles, turned, yc, columns, points, 0, top, sums, unroll=4)
    for c, row in enumerate(means):
        means_out[c : c + 1, :] = row
    back.wait()


def merge_kernel(parts, out):
    out[...] = combine([ref[...] for ref in parts])[0]


def merge_and_pass_kernel(parts, means, out, means_out):
    merge_kernel(parts, out)
    means_out[...] = means[...]


def mean_of(parts, means):
    shares = combine([ref[...] for ref in parts])[1]
    return functools.reduce(jnp.add, [share * ref[...] for share, ref in zip(shares, means)])


def merge_means_kernel(parts, means, after, out):
    out[...] = mean_of(parts, means)


def closing_kernel(parts, means, moved, points, target_out, source_out):
    target_out[...] = points[7:8, :] * (points[3:6, :] - mean_of(parts, means))
    source_out[...] = functools.reduce(jnp.add, [ref[...] for ref in moved])


def gradient_kernel(
    parts, u, points, xc, yc, lists_in, g_out, *rest, shares
):
    source_out, (lists, sem, red, turned, kept, sums, columns, g, whole, sem_out) = rest[:shares], rest[shares:]
    copy = fetch(lists_in, lists, sem)
    lse = combine([ref[...] for ref in parts])[0]
    xs, ys = points[0:3, :], points[3:6, :]
    g[...] = half_square(ys) - lse * (1.0 / KAPPA)
    back = fetch(g, g_out, sem_out)
    with_rows(red, yc, pieces(log2(points[7:8, :]) - lse), ONES)
    turn(turned, red)
    with_rows(kept, xc, ONES, split(log2(points[6:7, :]) + u[...]))
    copy.wait()
    tiles = Tiles(lists, sides(xc, yc), True)
    mass, *moved = plan_tiles(tiles, turned, kept, columns, points, 3, sums, unroll=4)
    for c in range(3):
        whole[c : c + 1, :] = xs[c : c + 1, :] * mass - moved[c]
    place_tgt = lax.axis_index("tgt")
    for k, out in enumerate(source_out):
        width = out.shape[1]
        at = pl.multiple_of(peer(place_tgt, k, shares) * width, width)
        out[...] = whole[:, pl.ds(at, width)]
    back.wait()


VMEM = pl.BlockSpec(memory_space=pltpu.VMEM)
HBM = pl.BlockSpec(memory_space=pltpu.HBM)


def call(kernel, ins, lists, outs, scratch, far=(), flops=0):
    return pl.pallas_call(
        kernel,
        out_shape=outs,
        in_specs=[VMEM] * len(ins) + [HBM] * len(lists),
        out_specs=[HBM if at in far else VMEM for at in range(len(outs))],
        scratch_shapes=scratch,
        compiler_params=pltpu.CompilerParams(vmem_limit_bytes=48 * 1024 * 1024),
        cost_estimate=pl.CostEstimate(flops=flops, bytes_accessed=0, transcendentals=0) if flops else None,
    )(*ins, *lists)


def peer(i, k, n):
    return i ^ k if n & (n - 1) == 0 else (i + k) % n


def exchange(values, axis):
    n = lax.axis_size(axis)
    return values[:1] + [
        lax.ppermute(values[k], axis, [(i, peer(i, k, n)) for i in range(n)]) for k in range(1, n)
    ]


def exchange_step(value, axis, step):
    n = lax.axis_size(axis)
    others = [k * step for k in range(1, min(4, n // step))]
    return [value] + [lax.ppermute(value, axis, [(i, i ^ k) for i in range(n)]) for k in others]


def bunch(kernel, *sizes):
    def run(*refs):
        lists = []
        for size in sizes:
            lists.append(refs[:size])
            refs = refs[size:]
        kernel(*lists, *refs)

    return run


def like(*values):
    return [jax.ShapeDtypeStruct(value.shape, value.dtype) for value in values]


def sum_up(axis, part):
    n, step = lax.axis_size(axis), 1
    while True:
        parts = exchange_step(part, axis, step)
        step *= 4
        if step >= n:
            return parts
        (part,) = call(bunch(merge_kernel, len(parts)), parts, (), like(part), [])


def body(source_points, target_points, source_weight, target_weight, target_start, tile_source, tile_target, tile_count):
    ns, nt = source_points.shape[1], target_points.shape[1]
    n_tgt = lax.axis_size("tgt")
    points = jnp.concatenate(
        [source_points, target_points] + [a.reshape(1, -1) for a in (source_weight, target_weight, target_start)]
    )
    lists = ((tile_count[:, :, None] * (nt // CLUSTER) + tile_target) * (ns // CLUSTER) + tile_source,)

    def rows(n, *k):
        return jax.ShapeDtypeStruct((*k, n), F32)

    def split_rows(n):
        return jax.ShapeDtypeStruct((DEPTH, n), BF16)

    def work(red):
        return [
            pltpu.SMEM(lists[0].shape, jnp.int32),
            pltpu.SemaphoreType.DMA,
            pltpu.VMEM((DEPTH, red), BF16),
            pltpu.VMEM((red, DEPTH), BF16),
        ]

    def state(kept):
        return [pltpu.VMEM((8, kept), F32), pltpu.VMEM((8, kept), F32)]

    first = work(nt)
    xc, yc, part = call(
        first_row_kernel,
        (points,),
        lists,
        [split_rows(ns), split_rows(nt), rows(ns, 1)],
        first[:2] + [pltpu.VMEM((DEPTH, ns), F32)] + first[2:] + state(ns),
    )
    known = (points, xc, yc)
    parts = exchange([part] * n_tgt, "tgt")
    (part,) = call(
        bunch(col_kernel, n_tgt),
        (*parts, *known),
        lists,
        [rows(nt, 1)],
        work(ns) + state(nt),
    )
    parts = sum_up("src", part)
    (part,) = call(
        bunch(row_kernel, len(parts)),
        (*parts, *known),
        lists,
        [rows(ns, 1)],
        work(nt) + state(ns),
    )
    parts = exchange([part] * n_tgt, "tgt")
    f, u, part, means = call(
        bunch(last_col_kernel, n_tgt),
        (*parts, *known),
        lists,
        [rows(ns, 1), rows(ns, 1), rows(nt, 1), rows(nt, 3)],
        work(ns)
        + [
            pltpu.VMEM((8, nt), F32),
            pltpu.VMEM((4, 8, nt), F32),
            pltpu.VMEM((ns, 384), F32),
            pltpu.VMEM((1, ns), F32),
            pltpu.SemaphoreType.DMA,
        ],
        far=(0,),
    )
    n_src, step, late = lax.axis_size("src"), 1, []
    while True:
        parts = exchange_step(part, "src", step)
        if 4 * step >= n_src:
            break
        part, means = call(
            bunch(merge_and_pass_kernel, len(parts)), (*parts, means), (), like(part, means), []
        )
        late.append((step, parts))
        step *= 4
    n = len(parts)
    g, *moved = call(
        bunch(functools.partial(gradient_kernel, shares=n_tgt), n),
        (*parts, u, *known),
        lists,
        [rows(nt, 1)] + [rows(ns // n_tgt, 3)] * n_tgt,
        work(nt)
        + [
            pltpu.VMEM((DEPTH, ns), BF16),
            pltpu.VMEM((4, 8, ns), F32),
            pltpu.VMEM((nt, 384), F32),
            pltpu.VMEM((1, nt), F32),
            pltpu.VMEM((3, ns), F32),
            pltpu.SemaphoreType.DMA,
        ],
        far=(0,),
        flops=40 * ns * CLUSTER,
    )
    for at, some in late:
        others = exchange_step(means, "src", at)
        (means,) = call(
            bunch(merge_means_kernel, len(some), len(some)), (*some, *others, moved[0]), (), like(means), []
        )
    means = exchange_step(means, "src", step)
    moved = exchange(moved, "tgt")
    target_grad, own_grad = call(
        bunch(closing_kernel, n, n, n_tgt),
        (*parts, *means, *moved, points),
        (),
        [rows(nt, 3), rows(ns // n_tgt, 3)],
        [],
    )
    return (f.reshape(-1), g.reshape(-1), own_grad, target_grad)


def solution(mesh):
    return jax.shard_map(
        body,
        mesh=mesh,
        in_specs=(
            P(None, "src"),
            P(None, "tgt"),
            P("src"),
            P("tgt"),
            P("tgt"),
            P("src", "tgt", None),
            P("src", "tgt", None),
            P("src", "tgt"),
        ),
        out_specs=(P("src"), P("tgt"), P(None, ("src", "tgt")), P(None, "tgt")),
        check_vma=False,
    )
```

```python
import functools
import math

import jax
import jax.numpy as jnp
from jax import lax
from jax.experimental import pallas as pl
from jax.experimental.pallas import tpu as pltpu
from jax.sharding import PartitionSpec as P

CLUSTER = 512
EPSILON = 0.02
KAPPA = math.log2(math.e) / EPSILON
LOG2E = math.log2(math.e)
DEPTH = 32
FLOOR = -1e30
EXTRAS = 4
F32 = jnp.float32
BF16 = jnp.bfloat16


def log2(value):
    return jnp.log(value) * LOG2E


def split(value):
    high = value.astype(BF16).astype(F32)
    rest = value - high
    middle = rest.astype(BF16).astype(F32)
    return (high, middle, rest - middle)


def half_square(points):
    return 0.5 * (points[0:1] * points[0:1] + points[1:2] * points[1:2] + points[2:3] * points[2:3])


SOURCE_ORDER = (0, 1, 2, 0, 0, 1)
TARGET_ORDER = (0, 0, 0, 1, 2, 1)
ONE = 15


def place(scratch, parts, order):
    scratch[...] = jnp.zeros_like(scratch)
    for at, which in enumerate(order[:5]):
        scratch[3 * at : 3 * at + 3, :] = parts[which]
    scratch[ONE : ONE + 1, :] = jnp.ones_like(parts[0][0:1])
    scratch[16:19, :] = parts[order[5]]
    scratch[19:22, :] = jnp.ones_like(parts[0])


def with_rows(out, static, first, second=()):
    out[0:16, :] = static[0:16, :]
    low = static[16:32, :].astype(F32)
    row = lax.broadcasted_iota(jnp.int32, low.shape, 0)
    for at, part in enumerate(tuple(first) + tuple(second)):
        low = jnp.where(row == 3 + at, part, low)
    out[16:32, :] = low.astype(BF16)


def pieces(potential):
    return split(potential - 1.0)


ONES = (1.0, 1.0, 1.0)


def scores(left, right):
    return lax.dot_general(left, right, (((0,), (0,)), ((), ())), preferred_element_type=F32)


def start_of(index):
    return pl.multiple_of(index * CLUSTER, CLUSTER)


def grouped(value):
    return value.reshape(value.shape[0] // 8, 8, value.shape[1])


def each_tile(tiles, left, right, visit, first, more, unroll=8, ahead=1, chunk=128):
    once = right.shape[1] // CLUSTER

    def group_states(group, fresh):
        steps = []
        for which, slot in enumerate(group):
            r, k = tiles.starts(slot)
            for at in range(CLUSTER // chunk):
                steps.append((which, pl.ds(k, CLUSTER), pl.ds(pl.multiple_of(r + at * chunk, chunk), chunk)))
        states = [None] * len(group)
        scores = [None] * len(steps)

        def start(n):
            if n < len(steps):
                which, here, rows = steps[n]
                scores[n] = grouped(jnp.dot(left[rows, :], right[:, here], preferred_element_type=F32))

        for n in range(ahead):
            start(n)
        for n, (which, here, rows) in enumerate(steps):
            start(n + ahead)
            states[which] = visit(scores[n], states[which], rows, fresh)
        return [(steps[which * (CLUSTER // chunk)][1], state) for which, state in enumerate(states)]

    def several(at, carry):
        for here, state in group_states([at * unroll + k for k in range(unroll)], True):
            first(here, state)
        return carry

    def others(at, carry):
        slots = [once + at * EXTRAS + k for k in range(EXTRAS)]
        states = group_states([jnp.minimum(slot, tiles.slots - 1) for slot in slots], False)
        for slot, (here, state) in zip(slots, states):
            more(here, state, slot < tiles.count())
        return carry

    lax.fori_loop(0, once // unroll, several, 0)
    lax.fori_loop(0, lax.div(tiles.count() - once + EXTRAS - 1, EXTRAS), others, 0)


def lse_tiles(tiles, left, right, top, total, **how):
    def visit(s, state, rows, fresh):
        largest = jnp.max(s, axis=0)
        if state is None:
            return largest, jnp.sum(jnp.exp2(s - largest[None]), axis=0)
        new = jnp.maximum(state[0], largest)
        return new, state[1] * jnp.exp2(state[0] - new) + jnp.sum(jnp.exp2(s - new[None]), axis=0)

    def first(here, state):
        top[:, here], total[:, here] = state

    def more(here, state, live):
        old, m = top[:, here], jnp.where(live, state[0], FLOOR)
        new = jnp.maximum(old, m)
        top[:, here] = new
        total[:, here] = total[:, here] * jnp.exp2(old - new) + state[1] * jnp.exp2(m - new)

    each_tile(tiles, left, right, visit, first, more, **how)
    m = top[...]
    largest = jnp.max(m, axis=0, keepdims=True)
    return largest + log2(jnp.sum(total[...] * jnp.exp2(m - largest), axis=0, keepdims=True))


def weighed(p, columns, points, start, rows, fresh):
    block = points[0:8, rows].T if fresh else None
    for c in range(3):
        lanes = slice(128 * c, 128 * (c + 1))
        if fresh:
            col = jnp.broadcast_to(block[:, start + c : start + c + 1], (block.shape[0], 128))
            columns[rows, lanes] = col
        else:
            col = columns[rows, lanes]
        yield jnp.sum(p * jnp.concatenate([col] * (CLUSTER // 128), axis=1).reshape(p.shape), axis=0)


def mean_tiles(tiles, left, right, columns, points, start, top, sums, **how):
    def visit(s, state, rows, fresh):
        largest = jnp.max(s, axis=0)
        new = largest if state is None else jnp.maximum(state[0], largest)
        p = jnp.exp2(s - new[None])
        totals = [jnp.sum(p, axis=0)] + list(weighed(p, columns, points, start, rows, fresh))
        if state is not None:
            scale = jnp.exp2(state[0] - new)
            totals = [old * scale + total for old, total in zip(state[1:], totals)]
        return [new] + totals

    def first(here, state):
        top[:, here] = state[0]
        for c, total in enumerate(state[1:]):
            sums[c, :, here] = total

    def more(here, state, live):
        old, m = top[:, here], jnp.where(live, state[0], FLOOR)
        new = jnp.maximum(old, m)
        before, now = jnp.exp2(old - new), jnp.exp2(m - new)
        top[:, here] = new
        for c, total in enumerate(state[1:]):
            sums[c, :, here] = sums[c, :, here] * before + total * now

    each_tile(tiles, left, right, visit, first, more, **how)
    m = top[...]
    largest = jnp.max(m, axis=0, keepdims=True)
    scale = jnp.exp2(m - largest)
    mass, *others = [jnp.sum(sums[c] * scale, axis=0, keepdims=True) for c in range(4)]
    return [largest + log2(mass)] + [other / mass for other in others]


def plan_tiles(tiles, left, right, columns, points, start, sums, **how):
    def visit(s, state, rows, fresh):
        p = jnp.exp2(s)
        totals = [jnp.sum(p, axis=0)] + list(weighed(p, columns, points, start, rows, fresh))
        return totals if state is None else [old + new for old, new in zip(state, totals)]

    def first(here, state):
        for c, total in enumerate(state):
            sums[c, :, here] = total

    def more(here, state, live):
        for c, total in enumerate(state):
            sums[c, :, here] += jnp.where(live, total, 0.0)

    each_tile(tiles, left, right, visit, first, more, **how)
    return [jnp.sum(sums[c], axis=0, keepdims=True) for c in range(4)]


def combine(parts):
    largest = functools.reduce(jnp.maximum, parts)
    terms = [jnp.exp2(part - largest) for part in parts]
    whole = functools.reduce(jnp.add, terms)
    return largest + log2(whole), [term / whole for term in terms]


def rows_of(refs):
    return [refs[at] for at in range(refs.shape[0])]


class Tiles:
    def __init__(self, ref, points, kept_source):
        self.ref, self.slots, self.kept_source = ref, ref.shape[-1], kept_source
        self.sources, self.targets = points

    def count(self):
        return lax.div(self.ref[0, 0, 0], self.sources * self.targets)

    def starts(self, slot):
        packed = self.ref[0, 0, slot]
        source = start_of(lax.rem(packed, self.sources))
        target = start_of(lax.rem(lax.div(packed, self.sources), self.targets))
        return (target, source) if self.kept_source else (source, target)


def fetch(lists_in, lists, sem):
    copy = pltpu.make_async_copy(lists_in, lists, sem)
    copy.start()
    return copy


def turn(out, operand):
    out[...] = operand[...].T


def sides(xc, yc):
    return xc.shape[1] // CLUSTER, yc.shape[1] // CLUSTER


def first_row_kernel(
    points, sources, targets, xc_out, yc_out, part_out, lists_out, lists, sem, stack, red, turned, top, total
):
    cps, cpt = sides(xc_out, yc_out)
    count = points[9:10, 0:1].astype(jnp.int32)
    lists_out[...] = (count.reshape(1, 1, 1) * cpt + targets[...]) * cps + sources[...]
    copy = fetch(lists_out, lists, sem)
    xs, ys = points[0:3, :], points[3:6, :]
    place(stack, split(ys * KAPPA), TARGET_ORDER)
    yc_out[...] = stack[...].astype(BF16)
    potential = log2(points[7:8, :]) + KAPPA * (points[8:9, :] - half_square(ys))
    with_rows(red, yc_out, pieces(potential))
    turn(turned, red)
    place(stack, split(xs), SOURCE_ORDER)
    xc_out[...] = stack[...].astype(BF16)
    copy.wait()
    part_out[...] = lse_tiles(Tiles(lists, sides(xc_out, yc_out), True), turned, xc_out, top, total)


def col_kernel(parts, points, xc, yc, lists_in, part_out, lists, sem, red, turned, top, total):
    copy = fetch(lists_in, lists, sem)
    potential = log2(points[6:7, :]) - combine([ref[...] for ref in parts])[0]
    with_rows(red, xc, pieces(potential))
    turn(turned, red)
    copy.wait()
    part_out[...] = lse_tiles(Tiles(lists, sides(xc, yc), False), turned, yc, top, total)


def row_kernel(parts, points, xc, yc, lists_in, part_out, lists, sem, red, turned, top, total):
    copy = fetch(lists_in, lists, sem)
    potential = log2(points[7:8, :]) - combine([ref[...] for ref in parts])[0]
    with_rows(red, yc, pieces(potential))
    turn(turned, red)
    copy.wait()
    part_out[...] = lse_tiles(Tiles(lists, sides(xc, yc), True), turned, xc, top, total)


def last_col_kernel(
    parts, points, xc, yc, lists_in, f_out, u_out, part_out, lists, sem, red, turned, top, sums, columns, f, sem_out
):
    copy = fetch(lists_in, lists, sem)
    u = -combine([ref[...] for ref in parts])[0]
    u_out[...] = u
    f[...] = u * (1.0 / KAPPA) + half_square(points[0:3, :])
    back = fetch(f, f_out, sem_out)
    with_rows(red, xc, pieces(log2(points[6:7, :]) + u))
    turn(turned, red)
    copy.wait()
    tiles = Tiles(lists, sides(xc, yc), False)
    for r, row in enumerate(mean_tiles(tiles, turned, yc, columns, points, 0, top, sums, unroll=4)):
        part_out[r : r + 1, :] = row
    back.wait()


def merged(parts):
    lse, shares = combine([ref[0:1, :] for ref in parts])
    rows = range(1, parts[0].shape[0])
    return [lse] + [functools.reduce(jnp.add, [w * ref[r : r + 1, :] for w, ref in zip(shares, parts)]) for r in rows]


def merge_kernel(*refs):
    for r, row in enumerate(merged(refs[:-1])):
        refs[-1][r : r + 1, :] = row


def gradient_kernel(
    parts, u, points, xc, yc, lists_in, g_out, target_out, *rest, shares
):
    source_out, (lists, sem, red, turned, kept, sums, columns, g, target, whole, sems) = rest[:shares], rest[shares:]
    copy = fetch(lists_in, lists, sem)
    lse, *means = merged(parts)
    xs, ys = points[0:3, :], points[3:6, :]
    g[...] = half_square(ys) - lse * (1.0 / KAPPA)
    for c in range(3):
        target[c : c + 1, :] = points[7:8, :] * (ys[c : c + 1, :] - means[c])
    back = [fetch(g, g_out, sems.at[0]), fetch(target, target_out, sems.at[1])]
    with_rows(red, yc, pieces(log2(points[7:8, :]) - lse), ONES)
    turn(turned, red)
    with_rows(kept, xc, ONES, split(log2(points[6:7, :]) + u[...]))
    copy.wait()
    tiles = Tiles(lists, sides(xc, yc), True)
    mass, *moved = plan_tiles(tiles, turned, kept, columns, points, 3, sums, unroll=4)
    for c in range(3):
        whole[c : c + 1, :] = xs[c : c + 1, :] * mass - moved[c]
    place_tgt = lax.axis_index("tgt")
    for k, out in enumerate(source_out):
        width = out.shape[1]
        at = pl.multiple_of(peer(place_tgt, k, shares) * width, width)
        out[...] = whole[:, pl.ds(at, width)]
    for one in back:
        one.wait()


VMEM = pl.BlockSpec(memory_space=pltpu.VMEM)
HBM = pl.BlockSpec(memory_space=pltpu.HBM)


def call(kernel, ins, lists, outs, scratch, far=()):
    return pl.pallas_call(
        kernel,
        out_shape=outs,
        in_specs=[VMEM] * len(ins) + [HBM] * len(lists),
        out_specs=[HBM if at in far else VMEM for at in range(len(outs))],
        scratch_shapes=scratch,
        compiler_params=pltpu.CompilerParams(vmem_limit_bytes=48 * 1024 * 1024),
    )(*ins, *lists)


def peer(i, k, n):
    return i ^ k if n & (n - 1) == 0 else (i + k) % n


def exchange(values, axis):
    n = lax.axis_size(axis)
    return values[:1] + [
        lax.ppermute(values[k], axis, [(i, peer(i, k, n)) for i in range(n)]) for k in range(1, n)
    ]


def sum_up(value, axis):
    n = lax.axis_size(axis)
    step = 1
    while True:
        others = [k * step for k in range(1, min(4, n // step))]
        values = [value] + [lax.ppermute(value, axis, [(i, i ^ k) for i in range(n)]) for k in others]
        step *= 4
        if step >= n:
            return values
        (value,) = call(merge_kernel, values, (), [jax.ShapeDtypeStruct(value.shape, F32)], [])


def bunch(kernel, size):
    return lambda *refs: kernel(refs[:size], *refs[size:])


def stacked(values, width):
    whole = sum(value.shape[0] for value in values)
    total, first = None, 0
    for value in values:
        after = whole - first - value.shape[0]
        padded = lax.pad(value, jnp.zeros((), value.dtype), [(first, after, 0), (0, width - value.shape[1], 0)]).astype(F32)
        total = padded if total is None else total + padded
        first += value.shape[0]
    return total


def body(source_points, target_points, source_weight, target_weight, target_start, tile_source, tile_target, tile_count):
    ns, nt = source_points.shape[1], target_points.shape[1]
    n_tgt = lax.axis_size("tgt")
    given = (source_points, target_points) + tuple(a.reshape(1, -1) for a in (source_weight, target_weight, target_start))
    points = stacked(given + (tile_count,), ns)
    given = (tile_source, tile_target)

    def rows(n, *k):
        return jax.ShapeDtypeStruct((*k, n), F32)

    def split_rows(n):
        return jax.ShapeDtypeStruct((DEPTH, n), BF16)

    def work(red):
        return [
            pltpu.SMEM(tile_source.shape, jnp.int32),
            pltpu.SemaphoreType.DMA,
            pltpu.VMEM((DEPTH, red), BF16),
            pltpu.VMEM((red, DEPTH), BF16),
        ]

    def state(kept):
        return [pltpu.VMEM((8, kept), F32), pltpu.VMEM((8, kept), F32)]

    first = work(nt)
    xc, yc, part, *lists = call(
        first_row_kernel,
        (points, *given),
        (),
        [split_rows(ns), split_rows(nt), rows(ns, 1), jax.ShapeDtypeStruct(tile_source.shape, jnp.int32)],
        first[:2] + [pltpu.VMEM((DEPTH, ns), F32)] + first[2:] + state(ns),
    )
    known = (points, xc, yc)
    parts = exchange([part] * n_tgt, "tgt")
    (part,) = call(
        bunch(col_kernel, n_tgt),
        (*parts, *known),
        lists,
        [rows(nt, 1)],
        work(ns) + state(nt),
    )
    parts = sum_up(part, "src")
    (part,) = call(
        bunch(row_kernel, len(parts)),
        (*parts, *known),
        lists,
        [rows(ns, 1)],
        work(nt) + state(ns),
    )
    parts = exchange([part] * n_tgt, "tgt")
    f, u, part = call(
        bunch(last_col_kernel, n_tgt),
        (*parts, *known),
        lists,
        [rows(ns, 1), rows(ns, 1), rows(nt, 4)],
        work(ns)
        + [
            pltpu.VMEM((8, nt), F32),
            pltpu.VMEM((4, 8, nt), F32),
            pltpu.VMEM((ns, 384), F32),
            pltpu.VMEM((1, ns), F32),
            pltpu.SemaphoreType.DMA,
        ],
        far=(0,),
    )
    parts = sum_up(part, "src")
    g, target_grad, *parts = call(
        bunch(functools.partial(gradient_kernel, shares=n_tgt), len(parts)),
        (*parts, u, *known),
        lists,
        [rows(nt, 1), rows(nt, 3)] + [rows(ns // n_tgt, 3)] * n_tgt,
        work(nt)
        + [
            pltpu.VMEM((DEPTH, ns), BF16),
            pltpu.VMEM((4, 8, ns), F32),
            pltpu.VMEM((nt, 384), F32),
            pltpu.VMEM((1, nt), F32),
            pltpu.VMEM((3, nt), F32),
            pltpu.VMEM((3, ns), F32),
            pltpu.SemaphoreType.DMA((2,)),
        ],
        far=(0, 1),
    )
    own_grad = functools.reduce(jnp.add, exchange(parts, "tgt"))
    return (f.reshape(-1), g.reshape(-1), own_grad, target_grad)


def solution(mesh):
    return jax.shard_map(
        body,
        mesh=mesh,
        in_specs=(
            P(None, "src"),
            P(None, "tgt"),
            P("src"),
            P("tgt"),
            P("tgt"),
            P("src", "tgt", None),
            P("src", "tgt", None),
            P("src", "tgt"),
        ),
        out_specs=(P("src"), P("tgt"), P(None, ("src", "tgt")), P(None, "tgt")),
        check_vma=False,
    )
```

```python
import functools
import math

import jax
import jax.numpy as jnp
from jax import lax
from jax.experimental import pallas as pl
from jax.experimental.pallas import tpu as pltpu
from jax.sharding import PartitionSpec as P

CLUSTER = 512
EPSILON = 0.02
KAPPA = math.log2(math.e) / EPSILON
LOG2E = math.log2(math.e)
DEPTH = 32
FLOOR = -1e30
EXTRAS = 4
F32 = jnp.float32
BF16 = jnp.bfloat16


def log2(value):
    return jnp.log(value) * LOG2E


def split(value):
    high = value.astype(BF16).astype(F32)
    rest = value - high
    middle = rest.astype(BF16).astype(F32)
    return (high, middle, rest - middle)


def half_square(points):
    return 0.5 * (points[0:1] * points[0:1] + points[1:2] * points[1:2] + points[2:3] * points[2:3])


SOURCE_ORDER = (0, 1, 2, 0, 0, 1)
TARGET_ORDER = (0, 0, 0, 1, 2, 1)


def place(scratch, parts, order):
    scratch[...] = jnp.zeros_like(scratch)
    for at, which in enumerate(order[:5]):
        scratch[3 * at : 3 * at + 3, :] = parts[which]
    scratch[16:19, :] = parts[order[5]]
    scratch[19:22, :] = jnp.ones_like(parts[0])


def lower_half(low, static, first=None, second=None):
    low[...] = static[16:32, :].astype(F32)
    for start, parts in ((3, first), (6, second)):
        for at, part in enumerate(parts or ()):
            low[start + at : start + at + 1, :] = part
    return low[...].astype(BF16)


def turn(turned, low, static, first, second=None):
    turned[...] = jnp.concatenate([static[0:16, :], lower_half(low, static, first, second)], axis=0).T


def start_of(index):
    return pl.multiple_of(index * CLUSTER, CLUSTER)


def grouped(value):
    return value.reshape(value.shape[0] // 8, 8, value.shape[1])


def each_tile(tiles, left, right, visit, first, more, unroll=8, ahead=1, chunk=128):
    once = right.shape[1] // CLUSTER

    def group_states(group, fresh):
        steps = []
        for which, slot in enumerate(group):
            r, k = tiles.starts(slot)
            for at in range(CLUSTER // chunk):
                steps.append((which, pl.ds(k, CLUSTER), pl.ds(pl.multiple_of(r + at * chunk, chunk), chunk)))
        states = [None] * len(group)
        scores = [None] * len(steps)

        def start(n):
            if n < len(steps):
                which, here, rows = steps[n]
                scores[n] = grouped(jnp.dot(left[rows, :], right[:, here], preferred_element_type=F32))

        for n in range(ahead):
            start(n)
        for n, (which, here, rows) in enumerate(steps):
            start(n + ahead)
            states[which] = visit(scores[n], states[which], rows, fresh)
        return [(steps[which * (CLUSTER // chunk)][1], state) for which, state in enumerate(states)]

    def several(at, carry):
        for here, state in group_states([at * unroll + k for k in range(unroll)], True):
            first(here, state)
        return carry

    def others(at, carry):
        slots = [once + at * EXTRAS + k for k in range(EXTRAS)]
        states = group_states([jnp.minimum(slot, tiles.slots - 1) for slot in slots], False)
        for slot, (here, state) in zip(slots, states):
            more(here, state, slot < tiles.count())
        return carry

    lax.fori_loop(0, once // unroll, several, 0)
    lax.fori_loop(0, lax.div(tiles.count() - once + EXTRAS - 1, EXTRAS), others, 0)


def lse_tiles(tiles, left, right, top, total, **how):
    def visit(s, state, rows, fresh):
        largest = jnp.max(s, axis=0)
        if state is None:
            return largest, jnp.sum(jnp.exp2(s - largest[None]), axis=0)
        new = jnp.maximum(state[0], largest)
        return new, state[1] * jnp.exp2(state[0] - new) + jnp.sum(jnp.exp2(s - new[None]), axis=0)

    def first(here, state):
        top[:, here], total[:, here] = state

    def more(here, state, live):
        old, m = top[:, here], jnp.where(live, state[0], FLOOR)
        new = jnp.maximum(old, m)
        top[:, here] = new
        total[:, here] = total[:, here] * jnp.exp2(old - new) + state[1] * jnp.exp2(m - new)

    each_tile(tiles, left, right, visit, first, more, **how)
    m = top[...]
    largest = jnp.max(m, axis=0, keepdims=True)
    return largest + log2(jnp.sum(total[...] * jnp.exp2(m - largest), axis=0, keepdims=True))


def weighed(p, columns, points, start, rows, fresh):
    block = points[0:8, rows].T if fresh else None
    for c in range(3):
        lanes = slice(128 * c, 128 * (c + 1))
        if fresh:
            col = jnp.broadcast_to(block[:, start + c : start + c + 1], (block.shape[0], 128))
            columns[rows, lanes] = col
        else:
            col = columns[rows, lanes]
        yield jnp.sum(p * jnp.concatenate([col] * (CLUSTER // 128), axis=1).reshape(p.shape), axis=0)


def mean_tiles(tiles, left, right, columns, points, start, top, sums, **how):
    def visit(s, state, rows, fresh):
        largest = jnp.max(s, axis=0)
        new = largest if state is None else jnp.maximum(state[0], largest)
        p = jnp.exp2(s - new[None])
        totals = [jnp.sum(p, axis=0)] + list(weighed(p, columns, points, start, rows, fresh))
        if state is not None:
            scale = jnp.exp2(state[0] - new)
            totals = [old * scale + total for old, total in zip(state[1:], totals)]
        return [new] + totals

    def first(here, state):
        top[:, here] = state[0]
        for c, total in enumerate(state[1:]):
            sums[c, :, here] = total

    def more(here, state, live):
        old, m = top[:, here], jnp.where(live, state[0], FLOOR)
        new = jnp.maximum(old, m)
        before, now = jnp.exp2(old - new), jnp.exp2(m - new)
        top[:, here] = new
        for c, total in enumerate(state[1:]):
            sums[c, :, here] = sums[c, :, here] * before + total * now

    each_tile(tiles, left, right, visit, first, more, **how)
    m = top[...]
    largest = jnp.max(m, axis=0, keepdims=True)
    scale = jnp.exp2(m - largest)
    mass, *others = [jnp.sum(sums[c] * scale, axis=0, keepdims=True) for c in range(4)]
    return [largest + log2(mass)] + [other / mass for other in others]


def plan_tiles(tiles, left, right, columns, points, start, sums, **how):
    def visit(s, state, rows, fresh):
        p = jnp.exp2(s)
        totals = [jnp.sum(p, axis=0)] + list(weighed(p, columns, points, start, rows, fresh))
        return totals if state is None else [old + new for old, new in zip(state, totals)]

    def first(here, state):
        for c, total in enumerate(state):
            sums[c, :, here] = total

    def more(here, state, live):
        for c, total in enumerate(state):
            sums[c, :, here] += jnp.where(live, total, 0.0)

    each_tile(tiles, left, right, visit, first, more, **how)
    return [jnp.sum(sums[c], axis=0, keepdims=True) for c in range(4)]


def combine(parts):
    largest = functools.reduce(jnp.maximum, parts)
    terms = [jnp.exp2(part - largest) for part in parts]
    whole = functools.reduce(jnp.add, terms)
    return largest + log2(whole), [term / whole for term in terms]


def rows_of(refs):
    return [refs[at] for at in range(refs.shape[0])]


class Tiles:
    def __init__(self, ref, points, kept_source):
        self.ref, self.slots, self.kept_source = ref, ref.shape[-1], kept_source
        self.sources, self.targets = points

    def count(self):
        return lax.div(self.ref[0, 0, 0], self.sources * self.targets)

    def starts(self, slot):
        packed = self.ref[0, 0, slot]
        source = start_of(lax.rem(packed, self.sources))
        target = start_of(lax.rem(lax.div(packed, self.sources), self.targets))
        return (target, source) if self.kept_source else (source, target)


def fetch(lists_in, lists, sem):
    copy = pltpu.make_async_copy(lists_in, lists, sem)
    copy.start()
    return copy


def sides(xc, yc):
    return xc.shape[1] // CLUSTER, yc.shape[1] // CLUSTER


def first_row_kernel(
    points, sources, targets, xc_out, yc_out, part_out, lists_out, log_source, log_target,
    lists, sem, stack, low, turned, top, total,
):
    cps, cpt = sides(xc_out, yc_out)
    count = points[9:10, 0:1].astype(jnp.int32)
    lists_out[...] = (count.reshape(1, 1, 1) * cpt + targets[...]) * cps + sources[...]
    copy = fetch(lists_out, lists, sem)
    log_source[...] = log2(points[6:7, :])
    log_target[...] = log2(points[7:8, :])
    xs, ys = points[0:3, :], points[3:6, :]
    place(stack, split(ys * KAPPA), TARGET_ORDER)
    yc_out[...] = stack[...].astype(BF16)
    turn(turned, low, yc_out, split(log_target[...] + KAPPA * (points[8:9, :] - half_square(ys))))
    place(stack, split(xs), SOURCE_ORDER)
    xc_out[...] = stack[...].astype(BF16)
    copy.wait()
    part_out[...] = lse_tiles(Tiles(lists, sides(xc_out, yc_out), True), turned, xc_out, top, total)


def col_kernel(parts, log_source, xc, yc, lists_in, part_out, lists, sem, low, turned, top, total):
    copy = fetch(lists_in, lists, sem)
    turn(turned, low, xc, split(log_source[...] - combine([ref[...] for ref in parts])[0]))
    copy.wait()
    part_out[...] = lse_tiles(Tiles(lists, sides(xc, yc), False), turned, yc, top, total, chunk=256)


def row_kernel(parts, log_target, xc, yc, lists_in, part_out, lists, sem, low, turned, top, total):
    copy = fetch(lists_in, lists, sem)
    turn(turned, low, yc, split(log_target[...] - combine([ref[...] for ref in parts])[0]))
    copy.wait()
    part_out[...] = lse_tiles(Tiles(lists, sides(xc, yc), True), turned, xc, top, total)


def last_col_kernel(
    parts, log_source, points, xc, yc, lists_in, f_out, u_out, part_out,
    lists, sem, low, turned, top, sums, columns, f, sem_out,
):
    copy = fetch(lists_in, lists, sem)
    u = -combine([ref[...] for ref in parts])[0]
    u_out[...] = log_source[...] + u
    f[...] = u * (1.0 / KAPPA) + half_square(points[0:3, :])
    back = fetch(f, f_out, sem_out)
    turn(turned, low, xc, split(u_out[...]))
    copy.wait()
    tiles = Tiles(lists, sides(xc, yc), False)
    for r, row in enumerate(mean_tiles(tiles, turned, yc, columns, points, 0, top, sums)):
        part_out[r : r + 1, :] = row
    back.wait()


def merged(parts):
    lse, shares = combine([ref[0:1, :] for ref in parts])
    rows = range(1, parts[0].shape[0])
    return [lse] + [functools.reduce(jnp.add, [w * ref[r : r + 1, :] for w, ref in zip(shares, parts)]) for r in rows]


def merge_kernel(*refs):
    for r, row in enumerate(merged(refs[:-1])):
        refs[-1][r : r + 1, :] = row


def gradient_kernel(
    parts, u, log_target, points, xc, yc, lists_in, g_out, target_out, *rest, shares
):
    source_out, (lists, sem, low, turned, kept, sums, columns, g, target, whole, sems) = rest[:shares], rest[shares:]
    copy = fetch(lists_in, lists, sem)
    lse, *means = merged(parts)
    xs, ys = points[0:3, :], points[3:6, :]
    g[...] = half_square(ys) - lse * (1.0 / KAPPA)
    for c in range(3):
        target[c : c + 1, :] = points[7:8, :] * (ys[c : c + 1, :] - means[c])
    back = [fetch(g, g_out, sems.at[0]), fetch(target, target_out, sems.at[1])]
    turn(turned, low, yc, split(log_target[...] - lse), [jnp.ones_like(lse)] * 3)
    kept[0:16, :] = xc[0:16, :]
    kept[16:32, :] = lower_half(low, xc, None, split(u[...]))
    copy.wait()
    tiles = Tiles(lists, sides(xc, yc), True)
    mass, *moved = plan_tiles(tiles, turned, kept, columns, points, 3, sums)
    for c in range(3):
        whole[c : c + 1, :] = xs[c : c + 1, :] * mass - moved[c]
    place_tgt = lax.axis_index("tgt")
    for k, out in enumerate(source_out):
        width = out.shape[1]
        at = pl.multiple_of(peer(place_tgt, k, shares) * width, width)
        out[...] = whole[:, pl.ds(at, width)]
    for one in back:
        one.wait()


VMEM = pl.BlockSpec(memory_space=pltpu.VMEM)
HBM = pl.BlockSpec(memory_space=pltpu.HBM)


def call(kernel, ins, lists, outs, scratch, far=()):
    return pl.pallas_call(
        kernel,
        out_shape=outs,
        in_specs=[VMEM] * len(ins) + [HBM] * len(lists),
        out_specs=[HBM if at in far else VMEM for at in range(len(outs))],
        scratch_shapes=scratch,
        compiler_params=pltpu.CompilerParams(vmem_limit_bytes=48 * 1024 * 1024),
    )(*ins, *lists)


def peer(i, k, n):
    return i ^ k if n & (n - 1) == 0 else (i + k) % n


def exchange(values, axis):
    n = lax.axis_size(axis)
    return values[:1] + [
        lax.ppermute(values[k], axis, [(i, peer(i, k, n)) for i in range(n)]) for k in range(1, n)
    ]


def sum_up(value, axis):
    n = lax.axis_size(axis)
    step = 1
    while True:
        others = [k * step for k in range(1, min(4, n // step))]
        values = [value] + [lax.ppermute(value, axis, [(i, i ^ k) for i in range(n)]) for k in others]
        step *= 4
        if step >= n:
            return values
        (value,) = call(merge_kernel, values, (), [jax.ShapeDtypeStruct(value.shape, F32)], [])


def bunch(kernel, size):
    return lambda *refs: kernel(refs[:size], *refs[size:])


def stacked(values, width):
    whole = sum(value.shape[0] for value in values)
    total, first = None, 0
    for value in values:
        after = whole - first - value.shape[0]
        padded = lax.pad(value, jnp.zeros((), value.dtype), [(first, after, 0), (0, width - value.shape[1], 0)]).astype(F32)
        total = padded if total is None else total + padded
        first += value.shape[0]
    return total


def body(source_points, target_points, source_weight, target_weight, target_start, tile_source, tile_target, tile_count):
    ns, nt = source_points.shape[1], target_points.shape[1]
    n_tgt = lax.axis_size("tgt")
    given = (source_points, target_points) + tuple(a.reshape(1, -1) for a in (source_weight, target_weight, target_start))
    points = stacked(given + (tile_count,), ns)
    given = (tile_source, tile_target)

    def rows(n, *k):
        return jax.ShapeDtypeStruct((*k, n), F32)

    def split_rows(n):
        return jax.ShapeDtypeStruct((DEPTH, n), BF16)

    def work(red):
        return [
            pltpu.SMEM(tile_source.shape, jnp.int32),
            pltpu.SemaphoreType.DMA,
            pltpu.VMEM((DEPTH // 2, red), F32),
            pltpu.VMEM((red, DEPTH), BF16),
        ]

    def state(kept):
        return [pltpu.VMEM((8, kept), F32), pltpu.VMEM((8, kept), F32)]

    first = work(nt)
    xc, yc, part, lists, log_source, log_target = call(
        first_row_kernel,
        (points, *given),
        (),
        [split_rows(ns), split_rows(nt), rows(ns, 1), jax.ShapeDtypeStruct(tile_source.shape, jnp.int32), rows(ns, 1), rows(nt, 1)],
        first[:2] + [pltpu.VMEM((DEPTH, ns), F32)] + first[2:] + state(ns),
    )
    known, lists = (xc, yc), (lists,)
    parts = exchange([part] * n_tgt, "tgt")
    (part,) = call(
        bunch(col_kernel, n_tgt),
        (*parts, log_source, *known),
        lists,
        [rows(nt, 1)],
        work(ns) + state(nt),
    )
    parts = sum_up(part, "src")
    (part,) = call(
        bunch(row_kernel, len(parts)),
        (*parts, log_target, *known),
        lists,
        [rows(ns, 1)],
        work(nt) + state(ns),
    )
    parts = exchange([part] * n_tgt, "tgt")
    f, u, part = call(
        bunch(last_col_kernel, n_tgt),
        (*parts, log_source, points, *known),
        lists,
        [rows(ns, 1), rows(ns, 1), rows(nt, 4)],
        work(ns)
        + [
            pltpu.VMEM((8, nt), F32),
            pltpu.VMEM((4, 8, nt), F32),
            pltpu.VMEM((ns, 384), F32),
            pltpu.VMEM((1, ns), F32),
            pltpu.SemaphoreType.DMA,
        ],
        far=(0,),
    )
    parts = sum_up(part, "src")
    g, target_grad, *parts = call(
        bunch(functools.partial(gradient_kernel, shares=n_tgt), len(parts)),
        (*parts, u, log_target, points, *known),
        lists,
        [rows(nt, 1), rows(nt, 3)] + [rows(ns // n_tgt, 3)] * n_tgt,
        work(nt)
        + [
            pltpu.VMEM((DEPTH, ns), BF16),
            pltpu.VMEM((4, 8, ns), F32),
            pltpu.VMEM((nt, 384), F32),
            pltpu.VMEM((1, nt), F32),
            pltpu.VMEM((3, nt), F32),
            pltpu.VMEM((3, ns), F32),
            pltpu.SemaphoreType.DMA((2,)),
        ],
        far=(0, 1),
    )
    own_grad = functools.reduce(jnp.add, exchange(parts, "tgt"))
    return (f.reshape(-1), g.reshape(-1), own_grad, target_grad)


def solution(mesh):
    return jax.shard_map(
        body,
        mesh=mesh,
        in_specs=(
            P(None, "src"),
            P(None, "tgt"),
            P("src"),
            P("tgt"),
            P("tgt"),
            P("src", "tgt", None),
            P("src", "tgt", None),
            P("src", "tgt"),
        ),
        out_specs=(P("src"), P("tgt"), P(None, ("src", "tgt")), P(None, "tgt")),
        check_vma=False,
    )
```

```python
import functools
import math

import jax
import jax.numpy as jnp
from jax import lax
from jax.experimental import pallas as pl
from jax.experimental.pallas import tpu as pltpu
from jax.sharding import PartitionSpec as P

CLUSTER = 512
EPSILON = 0.02
KAPPA = math.log2(math.e) / EPSILON
LOG2E = math.log2(math.e)
DEPTH = 32
FLOOR = -1e30
F32 = jnp.float32
BF16 = jnp.bfloat16


def log2(value):
    return jnp.log(value) * LOG2E


def split(value):
    high = value.astype(BF16).astype(F32)
    rest = value - high
    middle = rest.astype(BF16).astype(F32)
    return (high, middle, rest - middle)


def half_square(points):
    return 0.5 * (points[0:1] * points[0:1] + points[1:2] * points[1:2] + points[2:3] * points[2:3])


SOURCE_ORDER = (0, 1, 2, 0, 0, 1)
TARGET_ORDER = (0, 0, 0, 1, 2, 1)


def place(scratch, parts, order):
    scratch[...] = jnp.zeros_like(scratch)
    for at, which in enumerate(order[:5]):
        scratch[3 * at : 3 * at + 3, :] = parts[which]
    scratch[16:19, :] = parts[order[5]]
    scratch[19:22, :] = jnp.ones_like(parts[0])


def lower_half(low, static, first=None, second=None):
    low[...] = static[16:32, :].astype(F32)
    for start, parts in ((3, first), (6, second)):
        for at, part in enumerate(parts or ()):
            low[start + at : start + at + 1, :] = part
    return low[...].astype(BF16)


def turn(turned, low, static, first, second=None):
    turned[...] = jnp.concatenate([static[0:16, :], lower_half(low, static, first, second)], axis=0).T


def start_of(index):
    return pl.multiple_of(index * CLUSTER, CLUSTER)


def grouped(value):
    return value.reshape(value.shape[0] // 8, 8, value.shape[1])


def each_tile(tiles, left, right, visit, first, more, ahead=1, chunk=128):
    once = right.shape[1] // CLUSTER

    def group_states(group, fresh):
        steps = []
        for which, slot in enumerate(group):
            r, k = tiles.starts(slot)
            for at in range(CLUSTER // chunk):
                steps.append((which, pl.ds(k, CLUSTER), pl.ds(pl.multiple_of(r + at * chunk, chunk), chunk)))
        states = [None] * len(group)
        scores = [None] * len(steps)

        def start(n):
            if n < len(steps):
                which, here, rows = steps[n]
                scores[n] = grouped(jnp.dot(left[rows, :], right[:, here], preferred_element_type=F32))

        for n in range(ahead):
            start(n)
        for n, (which, here, rows) in enumerate(steps):
            start(n + ahead)
            states[which] = visit(scores[n], states[which], rows, fresh)
        return [(steps[which * (CLUSTER // chunk)][1], state) for which, state in enumerate(states)]

    slots = list(range(tiles.slots))
    count = tiles.count()
    for here, state in group_states(slots[:once], True):
        first(here, state)
    for slot, (here, state) in zip(slots[once:], group_states(slots[once:], False)):
        more(here, state, slot < count)


def lse_tiles(tiles, left, right, top, total, **how):
    def visit(s, state, rows, fresh):
        largest = jnp.max(s, axis=0)
        if state is None:
            return largest, jnp.sum(jnp.exp2(s - largest[None]), axis=0)
        new = jnp.maximum(state[0], largest)
        return new, state[1] * jnp.exp2(state[0] - new) + jnp.sum(jnp.exp2(s - new[None]), axis=0)

    def first(here, state):
        top[:, here], total[:, here] = state

    def more(here, state, live):
        old, m = top[:, here], jnp.where(live, state[0], FLOOR)
        new = jnp.maximum(old, m)
        top[:, here] = new
        total[:, here] = total[:, here] * jnp.exp2(old - new) + state[1] * jnp.exp2(m - new)

    each_tile(tiles, left, right, visit, first, more, **how)
    m = top[...]
    largest = jnp.max(m, axis=0, keepdims=True)
    return largest + log2(jnp.sum(total[...] * jnp.exp2(m - largest), axis=0, keepdims=True))


def weighed(p, columns, points, start, rows, fresh):
    block = points[0:8, rows].T if fresh else None
    for c in range(3):
        lanes = slice(128 * c, 128 * (c + 1))
        if fresh:
            col = jnp.broadcast_to(block[:, start + c : start + c + 1], (block.shape[0], 128))
            columns[rows, lanes] = col
        else:
            col = columns[rows, lanes]
        yield jnp.sum(p * jnp.concatenate([col] * (CLUSTER // 128), axis=1).reshape(p.shape), axis=0)


def mean_tiles(tiles, left, right, columns, points, start, top, sums, **how):
    def visit(s, state, rows, fresh):
        largest = jnp.max(s, axis=0)
        new = largest if state is None else jnp.maximum(state[0], largest)
        p = jnp.exp2(s - new[None])
        totals = [jnp.sum(p, axis=0)] + list(weighed(p, columns, points, start, rows, fresh))
        if state is not None:
            scale = jnp.exp2(state[0] - new)
            totals = [old * scale + total for old, total in zip(state[1:], totals)]
        return [new] + totals

    def first(here, state):
        top[:, here] = state[0]
        for c, total in enumerate(state[1:]):
            sums[c, :, here] = total

    def more(here, state, live):
        old, m = top[:, here], jnp.where(live, state[0], FLOOR)
        new = jnp.maximum(old, m)
        before, now = jnp.exp2(old - new), jnp.exp2(m - new)
        top[:, here] = new
        for c, total in enumerate(state[1:]):
            sums[c, :, here] = sums[c, :, here] * before + total * now

    each_tile(tiles, left, right, visit, first, more, **how)
    m = top[...]
    largest = jnp.max(m, axis=0, keepdims=True)
    scale = jnp.exp2(m - largest)
    mass, *others = [jnp.sum(sums[c] * scale, axis=0, keepdims=True) for c in range(4)]
    return [largest + log2(mass)] + [other / mass for other in others]


def plan_tiles(tiles, left, right, columns, points, start, sums, **how):
    def visit(s, state, rows, fresh):
        p = jnp.exp2(s)
        totals = [jnp.sum(p, axis=0)] + list(weighed(p, columns, points, start, rows, fresh))
        return totals if state is None else [old + new for old, new in zip(state, totals)]

    def first(here, state):
        for c, total in enumerate(state):
            sums[c, :, here] = total

    def more(here, state, live):
        for c, total in enumerate(state):
            sums[c, :, here] += jnp.where(live, total, 0.0)

    each_tile(tiles, left, right, visit, first, more, **how)
    return [jnp.sum(sums[c], axis=0, keepdims=True) for c in range(4)]


def combine(parts):
    largest = functools.reduce(jnp.maximum, parts)
    terms = [jnp.exp2(part - largest) for part in parts]
    whole = functools.reduce(jnp.add, terms)
    return largest + log2(whole), [term / whole for term in terms]


def rows_of(refs):
    return [refs[at] for at in range(refs.shape[0])]


class Tiles:
    def __init__(self, ref, points, kept_source):
        self.ref, self.slots, self.kept_source = ref, ref.shape[-1], kept_source
        self.sources, self.targets = points

    def count(self):
        return lax.div(self.ref[0, 0, 0], self.sources * self.targets)

    def starts(self, slot):
        packed = self.ref[0, 0, slot]
        source = start_of(lax.rem(packed, self.sources))
        target = start_of(lax.rem(lax.div(packed, self.sources), self.targets))
        return (target, source) if self.kept_source else (source, target)


def fetch(lists_in, lists, sem):
    copy = pltpu.make_async_copy(lists_in, lists, sem)
    copy.start()
    return copy


def sides(xc, yc):
    return xc.shape[1] // CLUSTER, yc.shape[1] // CLUSTER


def first_row_kernel(
    points, sources, targets, xc_out, yc_out, part_out, lists_out, log_source, log_target,
    lists, sem, stack, low, turned, top, total,
):
    cps, cpt = sides(xc_out, yc_out)
    count = points[9:10, 0:1].astype(jnp.int32)
    lists_out[...] = (count.reshape(1, 1, 1) * cpt + targets[...]) * cps + sources[...]
    copy = fetch(lists_out, lists, sem)
    log_source[...] = log2(points[6:7, :])
    log_target[...] = log2(points[7:8, :])
    xs, ys = points[0:3, :], points[3:6, :]
    place(stack, split(ys * KAPPA), TARGET_ORDER)
    yc_out[...] = stack[...].astype(BF16)
    turn(turned, low, yc_out, split(log_target[...] + KAPPA * (points[8:9, :] - half_square(ys))))
    place(stack, split(xs), SOURCE_ORDER)
    xc_out[...] = stack[...].astype(BF16)
    copy.wait()
    part_out[...] = lse_tiles(Tiles(lists, sides(xc_out, yc_out), True), turned, xc_out, top, total)


def col_kernel(parts, log_source, xc, yc, lists_in, part_out, lists, sem, low, turned, top, total):
    copy = fetch(lists_in, lists, sem)
    turn(turned, low, xc, split(log_source[...] - combine([ref[...] for ref in parts])[0]))
    copy.wait()
    part_out[...] = lse_tiles(Tiles(lists, sides(xc, yc), False), turned, yc, top, total)


def row_kernel(parts, log_target, xc, yc, lists_in, part_out, lists, sem, low, turned, top, total):
    copy = fetch(lists_in, lists, sem)
    turn(turned, low, yc, split(log_target[...] - combine([ref[...] for ref in parts])[0]))
    copy.wait()
    part_out[...] = lse_tiles(Tiles(lists, sides(xc, yc), True), turned, xc, top, total)


def last_col_kernel(
    parts, log_source, points, xc, yc, lists_in, f_out, u_out, part_out,
    lists, sem, low, turned, top, sums, columns, f, sem_out,
):
    copy = fetch(lists_in, lists, sem)
    u = -combine([ref[...] for ref in parts])[0]
    u_out[...] = log_source[...] + u
    f[...] = u * (1.0 / KAPPA) + half_square(points[0:3, :])
    back = fetch(f, f_out, sem_out)
    turn(turned, low, xc, split(u_out[...]))
    copy.wait()
    tiles = Tiles(lists, sides(xc, yc), False)
    for r, row in enumerate(mean_tiles(tiles, turned, yc, columns, points, 0, top, sums)):
        part_out[r : r + 1, :] = row
    back.wait()


def merged(parts):
    lse, shares = combine([ref[0:1, :] for ref in parts])
    rows = range(1, parts[0].shape[0])
    return [lse] + [functools.reduce(jnp.add, [w * ref[r : r + 1, :] for w, ref in zip(shares, parts)]) for r in rows]


def merge_kernel(*refs):
    for r, row in enumerate(merged(refs[:-1])):
        refs[-1][r : r + 1, :] = row


def kept_kernel(u, xc, out, low):
    out[0:16, :] = xc[0:16, :]
    out[16:32, :] = lower_half(low, xc, None, split(u[...]))


def target_kernel(parts, points, after, out):
    means = merged(parts)[1:]
    for c in range(3):
        out[c : c + 1, :] = points[7:8, :] * (points[3 + c : 4 + c, :] - means[c])


def gradient_kernel(parts, kept, log_target, points, xc, yc, lists_in, g_out, *rest, shares):
    source_out, (lists, sem, low, turned, sums, columns, g, whole, sem_out) = rest[:shares], rest[shares:]
    copy = fetch(lists_in, lists, sem)
    lse = combine([ref[0:1, :] for ref in parts])[0]
    xs = points[0:3, :]
    g[...] = half_square(points[3:6, :]) - lse * (1.0 / KAPPA)
    back = fetch(g, g_out, sem_out)
    turn(turned, low, yc, split(log_target[...] - lse), [jnp.ones_like(lse)] * 3)
    copy.wait()
    tiles = Tiles(lists, sides(xc, yc), True)
    mass, *moved = plan_tiles(tiles, turned, kept, columns, points, 3, sums)
    for c in range(3):
        whole[c : c + 1, :] = xs[c : c + 1, :] * mass - moved[c]
    place_tgt = lax.axis_index("tgt")
    for k, out in enumerate(source_out):
        width = out.shape[1]
        at = pl.multiple_of(peer(place_tgt, k, shares) * width, width)
        out[...] = whole[:, pl.ds(at, width)]
    back.wait()


VMEM = pl.BlockSpec(memory_space=pltpu.VMEM)
HBM = pl.BlockSpec(memory_space=pltpu.HBM)


def call(kernel, ins, lists, outs, scratch, far=()):
    return pl.pallas_call(
        kernel,
        out_shape=outs,
        in_specs=[VMEM] * len(ins) + [HBM] * len(lists),
        out_specs=[HBM if at in far else VMEM for at in range(len(outs))],
        scratch_shapes=scratch,
        compiler_params=pltpu.CompilerParams(vmem_limit_bytes=48 * 1024 * 1024),
    )(*ins, *lists)


def peer(i, k, n):
    return i ^ k if n & (n - 1) == 0 else (i + k) % n


def exchange(values, axis):
    n = lax.axis_size(axis)
    return values[:1] + [
        lax.ppermute(values[k], axis, [(i, peer(i, k, n)) for i in range(n)]) for k in range(1, n)
    ]


def sum_up(value, axis):
    n = lax.axis_size(axis)
    step = 1
    while True:
        others = [k * step for k in range(1, min(4, n // step))]
        values = [value] + [lax.ppermute(value, axis, [(i, i ^ k) for i in range(n)]) for k in others]
        step *= 4
        if step >= n:
            return values
        (value,) = call(merge_kernel, values, (), [jax.ShapeDtypeStruct(value.shape, F32)], [])


def bunch(kernel, size):
    return lambda *refs: kernel(refs[:size], *refs[size:])


def stacked(values, width):
    whole = sum(value.shape[0] for value in values)
    total, first = None, 0
    for value in values:
        after = whole - first - value.shape[0]
        padded = lax.pad(value, jnp.zeros((), value.dtype), [(first, after, 0), (0, width - value.shape[1], 0)]).astype(F32)
        total = padded if total is None else total + padded
        first += value.shape[0]
    return total


def body(source_points, target_points, source_weight, target_weight, target_start, tile_source, tile_target, tile_count):
    ns, nt = source_points.shape[1], target_points.shape[1]
    n_tgt = lax.axis_size("tgt")
    given = (source_points, target_points) + tuple(a.reshape(1, -1) for a in (source_weight, target_weight, target_start))
    points = stacked(given + (tile_count,), ns)
    given = (tile_source, tile_target)

    def rows(n, *k):
        return jax.ShapeDtypeStruct((*k, n), F32)

    def split_rows(n):
        return jax.ShapeDtypeStruct((DEPTH, n), BF16)

    def work(red):
        return [
            pltpu.SMEM(tile_source.shape, jnp.int32),
            pltpu.SemaphoreType.DMA,
            pltpu.VMEM((DEPTH // 2, red), F32),
            pltpu.VMEM((red, DEPTH), BF16),
        ]

    def state(kept):
        return [pltpu.VMEM((8, kept), F32), pltpu.VMEM((8, kept), F32)]

    first = work(nt)
    xc, yc, part, lists, log_source, log_target = call(
        first_row_kernel,
        (points, *given),
        (),
        [split_rows(ns), split_rows(nt), rows(ns, 1), jax.ShapeDtypeStruct(tile_source.shape, jnp.int32), rows(ns, 1), rows(nt, 1)],
        first[:2] + [pltpu.VMEM((DEPTH, ns), F32)] + first[2:] + state(ns),
    )
    known, lists = (xc, yc), (lists,)
    parts = exchange([part] * n_tgt, "tgt")
    (part,) = call(
        bunch(col_kernel, n_tgt),
        (*parts, log_source, *known),
        lists,
        [rows(nt, 1)],
        work(ns) + state(nt),
    )
    parts = sum_up(part, "src")
    (part,) = call(
        bunch(row_kernel, len(parts)),
        (*parts, log_target, *known),
        lists,
        [rows(ns, 1)],
        work(nt) + state(ns),
    )
    parts = exchange([part] * n_tgt, "tgt")
    f, u, part = call(
        bunch(last_col_kernel, n_tgt),
        (*parts, log_source, points, *known),
        lists,
        [rows(ns, 1), rows(ns, 1), rows(nt, 4)],
        work(ns)
        + [
            pltpu.VMEM((8, nt), F32),
            pltpu.VMEM((4, 8, nt), F32),
            pltpu.VMEM((ns, 384), F32),
            pltpu.VMEM((1, ns), F32),
            pltpu.SemaphoreType.DMA,
        ],
        far=(0,),
    )
    (kept,) = call(kept_kernel, (u, xc), (), [split_rows(ns)], [pltpu.VMEM((DEPTH // 2, ns), F32)])
    parts = sum_up(part, "src")
    g, *moved = call(
        bunch(functools.partial(gradient_kernel, shares=n_tgt), len(parts)),
        (*parts, kept, log_target, points, *known),
        lists,
        [rows(nt, 1)] + [rows(ns // n_tgt, 3)] * n_tgt,
        work(nt)
        + [
            pltpu.VMEM((4, 8, ns), F32),
            pltpu.VMEM((nt, 384), F32),
            pltpu.VMEM((1, nt), F32),
            pltpu.VMEM((3, ns), F32),
            pltpu.SemaphoreType.DMA,
        ],
        far=(0,),
    )
    (target_grad,) = call(bunch(target_kernel, len(parts)), (*parts, points, moved[0]), (), [rows(nt, 3)], [])
    own_grad = functools.reduce(jnp.add, exchange(moved, "tgt"))
    return (f.reshape(-1), g.reshape(-1), own_grad, target_grad)


def solution(mesh):
    return jax.shard_map(
        body,
        mesh=mesh,
        in_specs=(
            P(None, "src"),
            P(None, "tgt"),
            P("src"),
            P("tgt"),
            P("tgt"),
            P("src", "tgt", None),
            P("src", "tgt", None),
            P("src", "tgt"),
        ),
        out_specs=(P("src"), P("tgt"), P(None, ("src", "tgt")), P(None, "tgt")),
        check_vma=False,
    )
```

```python
import functools
import math

import jax
import jax.numpy as jnp
from jax import lax
from jax.experimental import pallas as pl
from jax.experimental.pallas import tpu as pltpu
from jax.sharding import PartitionSpec as P

CLUSTER = 512
EPSILON = 0.02
KAPPA = math.log2(math.e) / EPSILON
LOG2E = math.log2(math.e)
DEPTH = 32
FLOOR = -1e30
RANGE = 90.0
F32 = jnp.float32
BF16 = jnp.bfloat16


def log2(value):
    return jnp.log(value) * LOG2E


def split(value):
    high = value.astype(BF16).astype(F32)
    rest = value - high
    middle = rest.astype(BF16).astype(F32)
    return (high, middle, rest - middle)


def half_square(points):
    return 0.5 * (points[0:1] * points[0:1] + points[1:2] * points[1:2] + points[2:3] * points[2:3])


SOURCE_ORDER = (0, 1, 2, 0, 0, 1)
SOURCE_PARTS = (0, 3, 6)
TARGET_ORDER = (0, 0, 0, 1, 2, 1)
TARGET_PARTS = (0, 9, 12)


def place(scratch, parts, order):
    scratch[...] = jnp.zeros_like(scratch)
    for at, which in enumerate(order[:5]):
        scratch[3 * at : 3 * at + 3, :] = parts[which]
    scratch[16:19, :] = parts[order[5]]
    scratch[19:22, :] = jnp.ones_like(parts[0])


def lower_half(low, static, first=None, second=None):
    low[...] = static[16:32, :].astype(F32)
    for start, parts in ((3, first), (6, second)):
        for at, part in enumerate(parts or ()):
            low[start + at : start + at + 1, :] = part
    return low[...].astype(BF16)


def turn(turned, low, static, first, second=None):
    turned[...] = jnp.concatenate([static[0:16, :], lower_half(low, static, first, second)], axis=0).T


def start_of(index):
    return pl.multiple_of(index * CLUSTER, CLUSTER)


def grouped(value):
    return value.reshape(value.shape[0] // 8, 8, value.shape[1])


def each_tile(tiles, left, right, visit, first, more, ahead=1, chunk=128, loop=False):
    once = right.shape[1] // CLUSTER
    chunks = CLUSTER // chunk

    def group_states(group, fresh):
        steps = []
        for which, slot in enumerate(group):
            r, k = tiles.starts(slot)
            for at in range(chunks):
                steps.append((which, at, pl.ds(k, CLUSTER), pl.ds(pl.multiple_of(r + at * chunk, chunk), chunk)))
        states = [None] * len(group)
        scores = [None] * len(steps)

        def start(n):
            if n < len(steps):
                _, _, here, rows = steps[n]
                scores[n] = grouped(jnp.dot(left[rows, :], right[:, here], preferred_element_type=F32))

        for n in range(ahead):
            start(n)
        for n, (which, at, here, rows) in enumerate(steps):
            start(n + ahead)
            states[which] = visit(scores[n], states[which], rows, fresh, at)
        return [(steps[which * chunks][2], state) for which, state in enumerate(states)]

    count = tiles.count()
    if loop:

        def one(slot, carry):
            ((here, state),) = group_states([slot], True)
            first(here, state)
            return carry

        def another(slot, carry):
            ((here, state),) = group_states([slot], False)
            more(here, state, slot < count)
            return carry

        lax.fori_loop(0, once, one, 0)
        lax.fori_loop(once, count, another, 0)
        return
    slots = list(range(tiles.slots))
    for here, state in group_states(slots[:once], True):
        first(here, state)
    for slot, (here, state) in zip(slots[once:], group_states(slots[once:], False)):
        more(here, state, slot < count)


def lse_tiles(tiles, left, right, top, total, **how):
    def visit(s, state, rows, fresh, at):
        largest = jnp.max(s, axis=0)
        if state is None:
            return largest, jnp.sum(jnp.exp2(s - largest[None]), axis=0)
        new = jnp.maximum(state[0], largest)
        return new, state[1] * jnp.exp2(state[0] - new) + jnp.sum(jnp.exp2(s - new[None]), axis=0)

    def first(here, state):
        top[:, here], total[:, here] = state

    def more(here, state, live):
        old, m = top[:, here], jnp.where(live, state[0], FLOOR)
        new = jnp.maximum(old, m)
        top[:, here] = new
        total[:, here] = total[:, here] * jnp.exp2(old - new) + state[1] * jnp.exp2(m - new)

    each_tile(tiles, left, right, visit, first, more, **how)
    m = top[...]
    largest = jnp.max(m, axis=0, keepdims=True)
    return largest, largest + log2(jnp.sum(total[...] * jnp.exp2(m - largest), axis=0, keepdims=True))


def weighed(p, columns, points, start, rows, fresh):
    block = points[0:8, rows].T if fresh else None
    for c in range(3):
        lanes = slice(128 * c, 128 * (c + 1))
        if fresh:
            col = jnp.broadcast_to(block[:, start + c : start + c + 1], (block.shape[0], 128))
            columns[rows, lanes] = col
        else:
            col = columns[rows, lanes]
        yield jnp.sum(p * jnp.concatenate([col] * (CLUSTER // 128), axis=1).reshape(p.shape), axis=0)


def mean_tiles(tiles, left, right, columns, points, start, top, sums, **how):
    def visit(s, state, rows, fresh, at):
        largest = jnp.max(s, axis=0)
        new = largest if state is None else jnp.maximum(state[0], largest)
        p = jnp.exp2(s - new[None])
        totals = [jnp.sum(p, axis=0)] + list(weighed(p, columns, points, start, rows, fresh))
        if state is not None:
            scale = jnp.exp2(state[0] - new)
            totals = [old * scale + total for old, total in zip(state[1:], totals)]
        return [new] + totals

    def first(here, state):
        top[:, here] = state[0]
        for c, total in enumerate(state[1:]):
            sums[c, :, here] = total

    def more(here, state, live):
        old, m = top[:, here], jnp.where(live, state[0], FLOOR)
        new = jnp.maximum(old, m)
        before, now = jnp.exp2(old - new), jnp.exp2(m - new)
        top[:, here] = new
        for c, total in enumerate(state[1:]):
            sums[c, :, here] = sums[c, :, here] * before + total * now

    each_tile(tiles, left, right, visit, first, more, **how)
    m = top[...]
    largest = jnp.max(m, axis=0, keepdims=True)
    scale = jnp.exp2(m - largest)
    mass, *others = [jnp.sum(sums[c] * scale, axis=0, keepdims=True) for c in range(4)]
    return [largest + log2(mass)] + [other / mass for other in others]


def moments(p, static, rows):
    p = p.reshape(p.shape[0] * 8, p.shape[2])
    high = p.astype(BF16)
    low = (p - high.astype(F32)).astype(BF16)
    weights = static[:, rows]
    return jnp.dot(
        jnp.concatenate([weights, weights], axis=1), jnp.concatenate([high, low], axis=0), preferred_element_type=F32
    )


def added(state, totals):
    return totals if state is None else [old + new for old, new in zip(state, totals)]


def plan_tiles(tiles, left, right, columns, points, start, sums, product=None):
    def visit(s, state, rows, fresh, at):
        p = jnp.exp2(s)
        plain, other = state or (None, None)
        if product is not None and at == CLUSTER // 128 - 1:
            return plain, moments(p, product[0], rows)
        return added(plain, [jnp.sum(p, axis=0)] + list(weighed(p, columns, points, start, rows, fresh))), other

    def first(here, state):
        for c, total in enumerate(state[0]):
            sums[c, :, here] = total
        if product is not None:
            product[3][:, here] = state[1]

    def more(here, state, live):
        for c, total in enumerate(state[0]):
            sums[c, :, here] += jnp.where(live, total, 0.0)
        if product is not None:
            product[3][:, here] += jnp.where(live, state[1], 0.0)

    each_tile(tiles, left, right, visit, first, more)
    out = [jnp.sum(sums[c], axis=0, keepdims=True) for c in range(4)]
    if product is not None:
        _, starts, scale, other = product
        out[0] += other[19:20, :]
        for c in range(3):
            out[c + 1] += scale * functools.reduce(jnp.add, [other[at + c : at + c + 1, :] for at in starts])
    return out


def combine(parts):
    largest = functools.reduce(jnp.maximum, parts)
    terms = [jnp.exp2(part - largest) for part in parts]
    whole = functools.reduce(jnp.add, terms)
    return largest + log2(whole), [term / whole for term in terms]


def rows_of(refs):
    return [refs[at] for at in range(refs.shape[0])]


class Tiles:
    def __init__(self, ref, points, kept_source):
        self.ref, self.slots, self.kept_source = ref, ref.shape[-1], kept_source
        self.sources, self.targets = points

    def count(self):
        return lax.div(self.ref[0, 0, 0], self.sources * self.targets)

    def starts(self, slot):
        packed = self.ref[0, 0, slot]
        source = start_of(lax.rem(packed, self.sources))
        target = start_of(lax.rem(lax.div(packed, self.sources), self.targets))
        return (target, source) if self.kept_source else (source, target)


def fetch(lists_in, lists, sem):
    copy = pltpu.make_async_copy(lists_in, lists, sem)
    copy.start()
    return copy


def sides(xc, yc):
    return xc.shape[1] // CLUSTER, yc.shape[1] // CLUSTER


def first_row_kernel(
    points, sources, targets, xc_out, yc_out, part_out, lists_out, log_source, log_target,
    lists, sem, stack, low, turned, top, total,
):
    cps, cpt = sides(xc_out, yc_out)
    count = points[9:10, 0:1].astype(jnp.int32)
    lists_out[...] = (count.reshape(1, 1, 1) * cpt + targets[...]) * cps + sources[...]
    copy = fetch(lists_out, lists, sem)
    log_source[...] = log2(points[6:7, :])
    log_target[...] = log2(points[7:8, :])
    xs, ys = points[0:3, :], points[3:6, :]
    place(stack, split(ys * KAPPA), TARGET_ORDER)
    yc_out[...] = stack[...].astype(BF16)
    turn(turned, low, yc_out, split(log_target[...] + KAPPA * (points[8:9, :] - half_square(ys))))
    place(stack, split(xs), SOURCE_ORDER)
    xc_out[...] = stack[...].astype(BF16)
    copy.wait()
    part_out[...] = lse_tiles(Tiles(lists, sides(xc_out, yc_out), True), turned, xc_out, top, total)[1]


def col_kernel(
    parts, log_source, xc, yc, lists_in, part_out, top_out, u_out, lists, sem, low, turned, top, total
):
    copy = fetch(lists_in, lists, sem)
    u = -combine([ref[...] for ref in parts])[0]
    u_out[...] = u
    turn(turned, low, xc, split(log_source[...] + u))
    copy.wait()
    top_out[...], part_out[...] = lse_tiles(Tiles(lists, sides(xc, yc), False), turned, yc, top, total)


def row_kernel(parts, log_target, xc, yc, lists_in, part_out, lists, sem, low, turned, top, total):
    copy = fetch(lists_in, lists, sem)
    turn(turned, low, yc, split(log_target[...] - combine([ref[...] for ref in parts])[0]))
    copy.wait()
    part_out[...] = lse_tiles(Tiles(lists, sides(xc, yc), True), turned, xc, top, total)[1]


def last_col_kernel(
    parts, u_before, top_before, kept, log_source, points, xc, yc, lists_in, f_out, u_out, part_out,
    lists, sem, low, turned, top, sums, columns, f, sem_out,
):
    copy = fetch(lists_in, lists, sem)
    u = -combine([ref[...] for ref in parts])[0]
    u_out[...] = log_source[...] + u
    f[...] = u * (1.0 / KAPPA) + half_square(points[0:3, :])
    back = fetch(f, f_out, sem_out)
    change = u - u_before[...]
    highest = jnp.max(change)
    shift = top_before[...] + highest
    turn(turned, low, xc, split(u_out[...] - highest), [jnp.ones_like(u)] * 3)
    copy.wait()
    tiles = Tiles(lists, sides(xc, yc), False)
    near = highest - jnp.min(change) < RANGE

    @pl.when(near)
    def _():
        mass, *moved = plan_tiles(tiles, turned, kept, columns, points, 0, sums)
        part_out[0:1, :] = shift + log2(mass)
        for c, total in enumerate(moved):
            part_out[c + 1 : c + 2, :] = total / mass

    @pl.when(jnp.logical_not(near))
    def _():
        part, *means = mean_tiles(tiles, turned, kept, columns, points, 0, top, sums, loop=True)
        part_out[0:1, :] = shift + part
        for c, mean in enumerate(means):
            part_out[c + 1 : c + 2, :] = mean

    back.wait()


def merged(parts):
    lse, shares = combine([ref[0:1, :] for ref in parts])
    rows = range(1, parts[0].shape[0])
    return [lse] + [functools.reduce(jnp.add, [w * ref[r : r + 1, :] for w, ref in zip(shares, parts)]) for r in rows]


def merge_kernel(*refs):
    for r, row in enumerate(merged(refs[:-1])):
        refs[-1][r : r + 1, :] = row


def kept_kernel(potential, static, out, low, sign):
    out[0:16, :] = static[0:16, :]
    out[16:32, :] = lower_half(low, static, None, split(sign * potential[...]))


def target_kernel(parts, points, after, out):
    means = merged(parts)[1:]
    for c in range(3):
        out[c : c + 1, :] = points[7:8, :] * (points[3 + c : 4 + c, :] - means[c])


def gradient_kernel(parts, kept, log_target, points, xc, yc, lists_in, g_out, *rest, shares):
    source_out, (lists, sem, low, turned, sums, other, columns, g, whole, sem_out) = rest[:shares], rest[shares:]
    copy = fetch(lists_in, lists, sem)
    lse = combine([ref[0:1, :] for ref in parts])[0]
    xs = points[0:3, :]
    g[...] = half_square(points[3:6, :]) - lse * (1.0 / KAPPA)
    back = fetch(g, g_out, sem_out)
    turn(turned, low, yc, split(log_target[...] - lse), [jnp.ones_like(lse)] * 3)
    copy.wait()
    tiles = Tiles(lists, sides(xc, yc), True)
    mass, *moved = plan_tiles(
        tiles, turned, kept, columns, points, 3, sums, (yc, TARGET_PARTS, 1.0 / KAPPA, other)
    )
    for c in range(3):
        whole[c : c + 1, :] = xs[c : c + 1, :] * mass - moved[c]
    place_tgt = lax.axis_index("tgt")
    for k, out in enumerate(source_out):
        width = out.shape[1]
        at = pl.multiple_of(peer(place_tgt, k, shares) * width, width)
        out[...] = whole[:, pl.ds(at, width)]
    back.wait()


VMEM = pl.BlockSpec(memory_space=pltpu.VMEM)
HBM = pl.BlockSpec(memory_space=pltpu.HBM)


def call(kernel, ins, lists, outs, scratch, far=()):
    return pl.pallas_call(
        kernel,
        out_shape=outs,
        in_specs=[VMEM] * len(ins) + [HBM] * len(lists),
        out_specs=[HBM if at in far else VMEM for at in range(len(outs))],
        scratch_shapes=scratch,
        compiler_params=pltpu.CompilerParams(vmem_limit_bytes=48 * 1024 * 1024),
    )(*ins, *lists)


def peer(i, k, n):
    return i ^ k if n & (n - 1) == 0 else (i + k) % n


def exchange(values, axis):
    n = lax.axis_size(axis)
    return values[:1] + [
        lax.ppermute(values[k], axis, [(i, peer(i, k, n)) for i in range(n)]) for k in range(1, n)
    ]


def sum_up(value, axis):
    n = lax.axis_size(axis)
    step = 1
    while True:
        others = [k * step for k in range(1, min(4, n // step))]
        values = [value] + [lax.ppermute(value, axis, [(i, i ^ k) for i in range(n)]) for k in others]
        step *= 4
        if step >= n:
            return values
        (value,) = call(merge_kernel, values, (), [jax.ShapeDtypeStruct(value.shape, F32)], [])


def bunch(kernel, size):
    return lambda *refs: kernel(refs[:size], *refs[size:])


def stacked(values, width):
    whole = sum(value.shape[0] for value in values)
    total, first = None, 0
    for value in values:
        after = whole - first - value.shape[0]
        padded = lax.pad(value, jnp.zeros((), value.dtype), [(first, after, 0), (0, width - value.shape[1], 0)]).astype(F32)
        total = padded if total is None else total + padded
        first += value.shape[0]
    return total


def body(source_points, target_points, source_weight, target_weight, target_start, tile_source, tile_target, tile_count):
    ns, nt = source_points.shape[1], target_points.shape[1]
    n_tgt = lax.axis_size("tgt")
    given = (source_points, target_points) + tuple(a.reshape(1, -1) for a in (source_weight, target_weight, target_start))
    points = stacked(given + (tile_count,), ns)
    given = (tile_source, tile_target)

    def rows(n, *k):
        return jax.ShapeDtypeStruct((*k, n), F32)

    def split_rows(n):
        return jax.ShapeDtypeStruct((DEPTH, n), BF16)

    def work(red):
        return [
            pltpu.SMEM(tile_source.shape, jnp.int32),
            pltpu.SemaphoreType.DMA,
            pltpu.VMEM((DEPTH // 2, red), F32),
            pltpu.VMEM((red, DEPTH), BF16),
        ]

    def state(kept):
        return [pltpu.VMEM((8, kept), F32), pltpu.VMEM((8, kept), F32)]

    def kept_operand(potential, static, sign):
        n = static.shape[1]
        kernel = functools.partial(kept_kernel, sign=sign)
        return call(kernel, (potential, static), (), [split_rows(n)], [pltpu.VMEM((DEPTH // 2, n), F32)])[0]

    first = work(nt)
    xc, yc, part, lists, log_source, log_target = call(
        first_row_kernel,
        (points, *given),
        (),
        [split_rows(ns), split_rows(nt), rows(ns, 1), jax.ShapeDtypeStruct(tile_source.shape, jnp.int32), rows(ns, 1), rows(nt, 1)],
        first[:2] + [pltpu.VMEM((DEPTH, ns), F32)] + first[2:] + state(ns),
    )
    known, lists = (xc, yc), (lists,)
    parts = exchange([part] * n_tgt, "tgt")
    part, top, u = call(
        bunch(col_kernel, n_tgt),
        (*parts, log_source, *known),
        lists,
        [rows(nt, 1), rows(nt, 1), rows(ns, 1)],
        work(ns) + state(nt),
    )
    kept = kept_operand(top, yc, -1.0)
    parts = sum_up(part, "src")
    (part,) = call(
        bunch(row_kernel, len(parts)),
        (*parts, log_target, *known),
        lists,
        [rows(ns, 1)],
        work(nt) + state(ns),
    )
    parts = exchange([part] * n_tgt, "tgt")
    f, u, part = call(
        bunch(last_col_kernel, n_tgt),
        (*parts, u, top, kept, log_source, points, *known),
        lists,
        [rows(ns, 1), rows(ns, 1), rows(nt, 4)],
        work(ns)
        + [
            pltpu.VMEM((8, nt), F32),
            pltpu.VMEM((4, 8, nt), F32),
            pltpu.VMEM((ns, 384), F32),
            pltpu.VMEM((1, ns), F32),
            pltpu.SemaphoreType.DMA,
        ],
        far=(0,),
    )
    kept = kept_operand(u, xc, 1.0)
    parts = sum_up(part, "src")
    g, *moved = call(
        bunch(functools.partial(gradient_kernel, shares=n_tgt), len(parts)),
        (*parts, kept, log_target, points, *known),
        lists,
        [rows(nt, 1)] + [rows(ns // n_tgt, 3)] * n_tgt,
        work(nt)
        + [
            pltpu.VMEM((4, 8, ns), F32),
            pltpu.VMEM((DEPTH, ns), F32),
            pltpu.VMEM((nt, 384), F32),
            pltpu.VMEM((1, nt), F32),
            pltpu.VMEM((3, ns), F32),
            pltpu.SemaphoreType.DMA,
        ],
        far=(0,),
    )
    (target_grad,) = call(bunch(target_kernel, len(parts)), (*parts, points, moved[0]), (), [rows(nt, 3)], [])
    own_grad = functools.reduce(jnp.add, exchange(moved, "tgt"))
    return (f.reshape(-1), g.reshape(-1), own_grad, target_grad)


def solution(mesh):
    return jax.shard_map(
        body,
        mesh=mesh,
        in_specs=(
            P(None, "src"),
            P(None, "tgt"),
            P("src"),
            P("tgt"),
            P("tgt"),
            P("src", "tgt", None),
            P("src", "tgt", None),
            P("src", "tgt"),
        ),
        out_specs=(P("src"), P("tgt"), P(None, ("src", "tgt")), P(None, "tgt")),
        check_vma=False,
    )
```

```python
import functools
import math

import jax
import jax.numpy as jnp
from jax import lax
from jax.experimental import pallas as pl
from jax.experimental.pallas import tpu as pltpu
from jax.sharding import PartitionSpec as P

CLUSTER = 512
EPSILON = 0.02
KAPPA = math.log2(math.e) / EPSILON
LOG2E = math.log2(math.e)
DEPTH = 32
FLOOR = -1e30
LIMIT = 60.0
F32 = jnp.float32
BF16 = jnp.bfloat16


def log2(value):
    return jnp.log(value) * LOG2E


def split(value):
    high = value.astype(BF16).astype(F32)
    rest = value - high
    middle = rest.astype(BF16).astype(F32)
    return (high, middle, rest - middle)


def half_square(points):
    return 0.5 * (points[0:1] * points[0:1] + points[1:2] * points[1:2] + points[2:3] * points[2:3])


SOURCE_ORDER = (0, 1, 2, 0, 0, 1)
TARGET_ORDER = (0, 0, 0, 1, 2, 1)


def place(scratch, parts, order):
    scratch[...] = jnp.zeros_like(scratch)
    for at, which in enumerate(order[:5]):
        scratch[3 * at : 3 * at + 3, :] = parts[which]
    scratch[16:19, :] = parts[order[5]]
    scratch[19:22, :] = jnp.ones_like(parts[0])


def lower_half(low, static, first=None, second=None):
    low[...] = static[16:32, :].astype(F32)
    for start, parts in ((3, first), (6, second)):
        for at, part in enumerate(parts or ()):
            low[start + at : start + at + 1, :] = part
    return low[...].astype(BF16)


def turn(turned, low, static, first, second=None):
    turned[...] = jnp.concatenate([static[0:16, :], lower_half(low, static, first, second)], axis=0).T


def start_of(index):
    return pl.multiple_of(index * CLUSTER, CLUSTER)


def grouped(value):
    return value.reshape(value.shape[0] // 8, 8, value.shape[1])


def each_tile(tiles, left, right, visit, first, more, points=None, ahead=1, chunk=128, lanes=CLUSTER, loop=False):
    once = right.shape[1] // CLUSTER
    chunks, blocks = CLUSTER // chunk, CLUSTER // lanes

    def group_states(group, fresh):
        steps = []
        for which, slot in enumerate(group):
            r, k = tiles.starts(slot)
            given = points[0:8, pl.ds(r, CLUSTER)].T if fresh and points is not None else None
            for block in range(blocks):
                here = pl.ds(pl.multiple_of(k + block * lanes, lanes), lanes)
                for at in range(chunks):
                    rows = pl.ds(pl.multiple_of(r + at * chunk, chunk), chunk)
                    some = None if given is None or block else given[at * chunk : (at + 1) * chunk, :]
                    steps.append((which * blocks + block, some, here, rows))
        states = [None] * (len(group) * blocks)
        scores = [None] * len(steps)

        def start(n):
            if n < len(steps):
                _, _, here, rows = steps[n]
                scores[n] = grouped(jnp.dot(left[rows, :], right[:, here], preferred_element_type=F32))

        for n in range(ahead):
            start(n)
        for n, (which, some, here, rows) in enumerate(steps):
            start(n + ahead)
            states[which] = visit(scores[n], states[which], rows, some)
        return [(steps[which * chunks][2], state) for which, state in enumerate(states)]

    count = tiles.count()
    if loop:

        def one(slot, carry):
            for here, state in group_states([slot], True):
                first(here, state)
            return carry

        def another(slot, carry):
            for here, state in group_states([slot], False):
                more(here, state, slot < count)
            return carry

        lax.fori_loop(0, once, one, 0)
        lax.fori_loop(once, count, another, 0)
        return
    for here, state in group_states(range(once), True):
        first(here, state)
    for n, (here, state) in enumerate(group_states(range(once, tiles.slots), False)):
        more(here, state, once + n // blocks < count)


def lse_tiles(tiles, left, right, top, total, **how):
    def visit(s, state, rows, some):
        groups = [s[g] for g in range(s.shape[0])]
        new = functools.reduce(jnp.maximum, groups if state is None else [state[0]] + groups)
        total = None if state is None else state[1] * jnp.exp2(state[0] - new)
        for group in groups:
            p = jnp.exp2(group - new)
            total = p if total is None else total + p
        return new, total

    def first(here, state):
        top[:, here], total[:, here] = state

    def more(here, state, live):
        old, m = top[:, here], jnp.where(live, state[0], FLOOR)
        new = jnp.maximum(old, m)
        top[:, here] = new
        total[:, here] = total[:, here] * jnp.exp2(old - new) + state[1] * jnp.exp2(m - new)

    each_tile(tiles, left, right, visit, first, more, **how)
    m = top[...]
    largest = jnp.max(m, axis=0, keepdims=True)
    return largest, largest + log2(jnp.sum(total[...] * jnp.exp2(m - largest), axis=0, keepdims=True))


def weighed(groups, totals, columns, start, rows, some):
    for g, p in enumerate(groups):
        here = pl.ds(pl.multiple_of(rows.start + 8 * g, 8), 8)
        terms = [p]
        for c in range(3):
            lanes = slice(128 * c, 128 * (c + 1))
            if some is not None:
                col = jnp.broadcast_to(some[8 * g : 8 * (g + 1), start + c : start + c + 1], (8, 128))
                columns[here, lanes] = col
            else:
                col = columns[here, lanes]
            terms.append(p * jnp.concatenate([col] * (p.shape[1] // 128), axis=1))
        totals = terms if totals is None else [total + term for total, term in zip(totals, terms)]
    return totals


def mean_tiles(tiles, left, right, columns, points, start, top, sums, **how):
    def visit(s, state, rows, some):
        largest = jnp.max(s, axis=0)
        new = largest if state is None else jnp.maximum(state[0], largest)
        totals = None
        if state is not None:
            scale = jnp.exp2(state[0] - new)
            totals = [old * scale for old in state[1:]]
        groups = [jnp.exp2(s[g] - new) for g in range(s.shape[0])]
        return [new] + weighed(groups, totals, columns, start, rows, some)

    def first(here, state):
        top[:, here] = state[0]
        for c, total in enumerate(state[1:]):
            sums[c, :, here] = total

    def more(here, state, live):
        old, m = top[:, here], jnp.where(live, state[0], FLOOR)
        new = jnp.maximum(old, m)
        before, now = jnp.exp2(old - new), jnp.exp2(m - new)
        top[:, here] = new
        for c, total in enumerate(state[1:]):
            sums[c, :, here] = sums[c, :, here] * before + total * now

    each_tile(tiles, left, right, visit, first, more, points, **how)
    m = top[...]
    largest = jnp.max(m, axis=0, keepdims=True)
    scale = jnp.exp2(m - largest)
    mass, *others = [jnp.sum(sums[c] * scale, axis=0, keepdims=True) for c in range(4)]
    return [largest + log2(mass)] + [other / mass for other in others]


def plan_tiles(tiles, left, right, columns, points, start, sums, **how):
    def visit(s, state, rows, some):
        groups = (jnp.exp2(s[g]) for g in range(s.shape[0]))
        return weighed(groups, state, columns, start, rows, some)

    def first(here, state):
        for c, total in enumerate(state):
            sums[c, :, here] = total

    def more(here, state, live):
        for c, total in enumerate(state):
            sums[c, :, here] += jnp.where(live, total, 0.0)

    each_tile(tiles, left, right, visit, first, more, points, **how)
    return [jnp.sum(sums[c], axis=0, keepdims=True) for c in range(4)]


def combine(parts):
    largest = functools.reduce(jnp.maximum, parts)
    terms = [jnp.exp2(part - largest) for part in parts]
    whole = functools.reduce(jnp.add, terms)
    return largest + log2(whole), [term / whole for term in terms]


def rows_of(refs):
    return [refs[at] for at in range(refs.shape[0])]


class Tiles:
    def __init__(self, ref, points, kept_source):
        self.ref, self.slots, self.kept_source = ref, ref.shape[-1], kept_source
        self.sources, self.targets = points

    def count(self):
        return lax.div(self.ref[0, 0, 0], self.sources * self.targets)

    def starts(self, slot):
        packed = self.ref[0, 0, slot]
        source = start_of(lax.rem(packed, self.sources))
        target = start_of(lax.rem(lax.div(packed, self.sources), self.targets))
        return (target, source) if self.kept_source else (source, target)


def fetch(lists_in, lists, sem):
    copy = pltpu.make_async_copy(lists_in, lists, sem)
    copy.start()
    return copy


def sides(xc, yc):
    return xc.shape[1] // CLUSTER, yc.shape[1] // CLUSTER


def first_row_kernel(
    points, sources, targets, xc_out, yc_out, part_out, lists_out, log_source, log_target,
    lists, sem, stack, low, turned, top, total,
):
    cps, cpt = sides(xc_out, yc_out)
    count = points[9:10, 0:1].astype(jnp.int32)
    lists_out[...] = (count.reshape(1, 1, 1) * cpt + targets[...]) * cps + sources[...]
    copy = fetch(lists_out, lists, sem)
    log_source[...] = log2(points[6:7, :])
    log_target[...] = log2(points[7:8, :])
    xs, ys = points[0:3, :], points[3:6, :]
    place(stack, split(ys * KAPPA), TARGET_ORDER)
    yc_out[...] = stack[...].astype(BF16)
    turn(turned, low, yc_out, split(log_target[...] + KAPPA * (points[8:9, :] - half_square(ys))))
    place(stack, split(xs), SOURCE_ORDER)
    xc_out[...] = stack[...].astype(BF16)
    copy.wait()
    part_out[...] = lse_tiles(Tiles(lists, sides(xc_out, yc_out), True), turned, xc_out, top, total, lanes=256)[1]


def col_kernel(
    parts, log_source, xc, yc, lists_in, part_out, top_out, u_out, lists, sem, low, turned, top, total
):
    copy = fetch(lists_in, lists, sem)
    u = -combine([ref[...] for ref in parts])[0]
    u_out[...] = u
    turn(turned, low, xc, split(log_source[...] + u))
    copy.wait()
    top_out[...], part_out[...] = lse_tiles(Tiles(lists, sides(xc, yc), False), turned, yc, top, total, lanes=256)


def row_kernel(parts, log_target, xc, yc, lists_in, part_out, lists, sem, low, turned, top, total):
    copy = fetch(lists_in, lists, sem)
    turn(turned, low, yc, split(log_target[...] - combine([ref[...] for ref in parts])[0]))
    copy.wait()
    part_out[...] = lse_tiles(Tiles(lists, sides(xc, yc), True), turned, xc, top, total, chunk=64)[1]


def last_col_kernel(
    parts, u_before, top_before, kept, log_source, points, xc, yc, lists_in, f_out, u_out, part_out,
    lists, sem, low, turned, top, sums, columns, f, sem_out,
):
    copy = fetch(lists_in, lists, sem)
    u = -combine([ref[...] for ref in parts])[0]
    u_out[...] = log_source[...] + u
    f[...] = u * (1.0 / KAPPA) + half_square(points[0:3, :])
    back = fetch(f, f_out, sem_out)
    near = jnp.max(jnp.abs(u - u_before[...])) < LIMIT
    turn(turned, low, xc, split(u_out[...]), [jnp.ones_like(u)] * 3)
    copy.wait()
    tiles = Tiles(lists, sides(xc, yc), False)

    @pl.when(near)
    def _():
        mass, *moved = plan_tiles(tiles, turned, kept, columns, points, 0, sums, chunk=32, ahead=2)
        part_out[0:1, :] = top_before[...] + log2(mass)
        inverse = 1.0 / mass
        for c, total in enumerate(moved):
            part_out[c + 1 : c + 2, :] = total * inverse

    @pl.when(jnp.logical_not(near))
    def _():
        part, *means = mean_tiles(tiles, turned, kept, columns, points, 0, top, sums, loop=True)
        part_out[0:1, :] = top_before[...] + part
        for c, mean in enumerate(means):
            part_out[c + 1 : c + 2, :] = mean

    back.wait()


def merged(parts):
    lse, shares = combine([ref[0:1, :] for ref in parts])
    rows = range(1, parts[0].shape[0])
    return [lse] + [functools.reduce(jnp.add, [w * ref[r : r + 1, :] for w, ref in zip(shares, parts)]) for r in rows]


def merge_kernel(*refs):
    for r, row in enumerate(merged(refs[:-1])):
        refs[-1][r : r + 1, :] = row


def kept_kernel(potential, static, out, low, sign):
    out[0:16, :] = static[0:16, :]
    out[16:32, :] = lower_half(low, static, None, split(sign * potential[...]))


def target_kernel(parts, points, after, out):
    means = merged(parts)[1:]
    for c in range(3):
        out[c : c + 1, :] = points[7:8, :] * (points[3 + c : 4 + c, :] - means[c])


def gradient_kernel(parts, kept, log_target, points, xc, yc, lists_in, g_out, *rest, shares):
    source_out, (lists, sem, low, turned, sums, columns, g, whole, sem_out) = rest[:shares], rest[shares:]
    copy = fetch(lists_in, lists, sem)
    lse = combine([ref[0:1, :] for ref in parts])[0]
    xs = points[0:3, :]
    g[...] = half_square(points[3:6, :]) - lse * (1.0 / KAPPA)
    back = fetch(g, g_out, sem_out)
    turn(turned, low, yc, split(log_target[...] - lse), [jnp.ones_like(lse)] * 3)
    copy.wait()
    tiles = Tiles(lists, sides(xc, yc), True)
    mass, *moved = plan_tiles(tiles, turned, kept, columns, points, 3, sums, chunk=32, ahead=2)
    for c in range(3):
        whole[c : c + 1, :] = xs[c : c + 1, :] * mass - moved[c]
    place_tgt = lax.axis_index("tgt")
    for k, out in enumerate(source_out):
        width = out.shape[1]
        at = pl.multiple_of(peer(place_tgt, k, shares) * width, width)
        out[...] = whole[:, pl.ds(at, width)]
    back.wait()


VMEM = pl.BlockSpec(memory_space=pltpu.VMEM)
HBM = pl.BlockSpec(memory_space=pltpu.HBM)


def call(kernel, ins, lists, outs, scratch, far=()):
    return pl.pallas_call(
        kernel,
        out_shape=outs,
        in_specs=[VMEM] * len(ins) + [HBM] * len(lists),
        out_specs=[HBM if at in far else VMEM for at in range(len(outs))],
        scratch_shapes=scratch,
        compiler_params=pltpu.CompilerParams(vmem_limit_bytes=48 * 1024 * 1024),
    )(*ins, *lists)


def peer(i, k, n):
    return i ^ k if n & (n - 1) == 0 else (i + k) % n


def exchange(values, axis):
    n = lax.axis_size(axis)
    return values[:1] + [
        lax.ppermute(values[k], axis, [(i, peer(i, k, n)) for i in range(n)]) for k in range(1, n)
    ]


def sum_up(value, axis):
    n = lax.axis_size(axis)
    step = 1
    while True:
        others = [k * step for k in range(1, min(4, n // step))]
        values = [value] + [lax.ppermute(value, axis, [(i, i ^ k) for i in range(n)]) for k in others]
        step *= 4
        if step >= n:
            return values
        (value,) = call(merge_kernel, values, (), [jax.ShapeDtypeStruct(value.shape, F32)], [])


def bunch(kernel, size):
    return lambda *refs: kernel(refs[:size], *refs[size:])


def stacked(values, width):
    whole = sum(value.shape[0] for value in values)
    total, first = None, 0
    for value in values:
        after = whole - first - value.shape[0]
        padded = lax.pad(value, jnp.zeros((), value.dtype), [(first, after, 0), (0, width - value.shape[1], 0)]).astype(F32)
        total = padded if total is None else total + padded
        first += value.shape[0]
    return total


def body(source_points, target_points, source_weight, target_weight, target_start, tile_source, tile_target, tile_count):
    ns, nt = source_points.shape[1], target_points.shape[1]
    n_tgt = lax.axis_size("tgt")
    given = (source_points, target_points) + tuple(a.reshape(1, -1) for a in (source_weight, target_weight, target_start))
    points = stacked(given + (tile_count,), ns)
    given = (tile_source, tile_target)

    def rows(n, *k):
        return jax.ShapeDtypeStruct((*k, n), F32)

    def split_rows(n):
        return jax.ShapeDtypeStruct((DEPTH, n), BF16)

    def work(red):
        return [
            pltpu.SMEM(tile_source.shape, jnp.int32),
            pltpu.SemaphoreType.DMA,
            pltpu.VMEM((DEPTH // 2, red), F32),
            pltpu.VMEM((red, DEPTH), BF16),
        ]

    def state(kept):
        return [pltpu.VMEM((8, kept), F32), pltpu.VMEM((8, kept), F32)]

    def kept_operand(potential, static, sign):
        n = static.shape[1]
        kernel = functools.partial(kept_kernel, sign=sign)
        return call(kernel, (potential, static), (), [split_rows(n)], [pltpu.VMEM((DEPTH // 2, n), F32)])[0]

    first = work(nt)
    xc, yc, part, lists, log_source, log_target = call(
        first_row_kernel,
        (points, *given),
        (),
        [split_rows(ns), split_rows(nt), rows(ns, 1), jax.ShapeDtypeStruct(tile_source.shape, jnp.int32), rows(ns, 1), rows(nt, 1)],
        first[:2] + [pltpu.VMEM((DEPTH, ns), F32)] + first[2:] + state(ns),
    )
    known, lists = (xc, yc), (lists,)
    parts = exchange([part] * n_tgt, "tgt")
    part, top, u = call(
        bunch(col_kernel, n_tgt),
        (*parts, log_source, *known),
        lists,
        [rows(nt, 1), rows(nt, 1), rows(ns, 1)],
        work(ns) + state(nt),
    )
    kept = kept_operand(top, yc, -1.0)
    parts = sum_up(part, "src")
    (part,) = call(
        bunch(row_kernel, len(parts)),
        (*parts, log_target, *known),
        lists,
        [rows(ns, 1)],
        work(nt) + state(ns),
    )
    parts = exchange([part] * n_tgt, "tgt")
    f, u, part = call(
        bunch(last_col_kernel, n_tgt),
        (*parts, u, top, kept, log_source, points, *known),
        lists,
        [rows(ns, 1), rows(ns, 1), rows(nt, 4)],
        work(ns)
        + [
            pltpu.VMEM((8, nt), F32),
            pltpu.VMEM((4, 8, nt), F32),
            pltpu.VMEM((ns, 384), F32),
            pltpu.VMEM((1, ns), F32),
            pltpu.SemaphoreType.DMA,
        ],
        far=(0,),
    )
    kept = kept_operand(u, xc, 1.0)
    parts = sum_up(part, "src")
    g, *moved = call(
        bunch(functools.partial(gradient_kernel, shares=n_tgt), len(parts)),
        (*parts, kept, log_target, points, *known),
        lists,
        [rows(nt, 1)] + [rows(ns // n_tgt, 3)] * n_tgt,
        work(nt)
        + [
            pltpu.VMEM((4, 8, ns), F32),
            pltpu.VMEM((nt, 384), F32),
            pltpu.VMEM((1, nt), F32),
            pltpu.VMEM((3, ns), F32),
            pltpu.SemaphoreType.DMA,
        ],
        far=(0,),
    )
    (target_grad,) = call(bunch(target_kernel, len(parts)), (*parts, points, moved[0]), (), [rows(nt, 3)], [])
    own_grad = functools.reduce(jnp.add, exchange(moved, "tgt"))
    return (f.reshape(-1), g.reshape(-1), own_grad, target_grad)


def solution(mesh):
    return jax.shard_map(
        body,
        mesh=mesh,
        in_specs=(
            P(None, "src"),
            P(None, "tgt"),
            P("src"),
            P("tgt"),
            P("tgt"),
            P("src", "tgt", None),
            P("src", "tgt", None),
            P("src", "tgt"),
        ),
        out_specs=(P("src"), P("tgt"), P(None, ("src", "tgt")), P(None, "tgt")),
        check_vma=False,
    )
```

```python
import functools
import math

import jax
import jax.numpy as jnp
from jax import lax
from jax.experimental import pallas as pl
from jax.experimental.pallas import tpu as pltpu
from jax.sharding import PartitionSpec as P

CLUSTER = 512
EPSILON = 0.02
KAPPA = math.log2(math.e) / EPSILON
LOG2E = math.log2(math.e)
DEPTH = 32
FLOOR = -1e30
LIMIT = 60.0
F32 = jnp.float32
BF16 = jnp.bfloat16


def log2(value):
    return jnp.log(value) * LOG2E


def split(value):
    high = value.astype(BF16).astype(F32)
    rest = value - high
    middle = rest.astype(BF16).astype(F32)
    return (high, middle, rest - middle)


def half_square(points):
    return 0.5 * (points[0:1] * points[0:1] + points[1:2] * points[1:2] + points[2:3] * points[2:3])


SOURCE_ORDER = (0, 1, 2, 0, 0, 1)
TARGET_ORDER = (0, 0, 0, 1, 2, 1)


def place(scratch, parts, order):
    scratch[...] = jnp.zeros_like(scratch)
    for at, which in enumerate(order[:5]):
        scratch[3 * at : 3 * at + 3, :] = parts[which]
    scratch[16:19, :] = parts[order[5]]
    scratch[19:22, :] = jnp.ones_like(parts[0])


def lower_half(low, static, first=None, second=None):
    low[...] = static[16:32, :].astype(F32)
    for start, parts in ((3, first), (6, second)):
        for at, part in enumerate(parts or ()):
            low[start + at : start + at + 1, :] = part
    return low[...].astype(BF16)


def turn(turned, low, static, first, second=None):
    turned[...] = jnp.concatenate([static[0:16, :], lower_half(low, static, first, second)], axis=0).T


def start_of(index):
    return pl.multiple_of(index * CLUSTER, CLUSTER)


def grouped(value):
    return value.reshape(value.shape[0] // 8, 8, value.shape[1])


def each_tile(tiles, left, right, visit, first, more, points=None, ahead=1, chunk=128, lanes=CLUSTER, loop=False):
    once = right.shape[1] // CLUSTER
    chunks, blocks = CLUSTER // chunk, CLUSTER // lanes

    def group_states(group, fresh):
        steps = []
        for which, slot in enumerate(group):
            r, k = tiles.starts(slot)
            given = points[0:8, pl.ds(r, CLUSTER)].T if fresh and points is not None else None
            for block in range(blocks):
                here = pl.ds(pl.multiple_of(k + block * lanes, lanes), lanes)
                for at in range(chunks):
                    rows = pl.ds(pl.multiple_of(r + at * chunk, chunk), chunk)
                    some = None if given is None or block else given[at * chunk : (at + 1) * chunk, :]
                    steps.append((which * blocks + block, some, here, rows))
        states = [None] * (len(group) * blocks)
        scores = [None] * len(steps)

        def start(n):
            if n < len(steps):
                _, _, here, rows = steps[n]
                scores[n] = grouped(jnp.dot(left[rows, :], right[:, here], preferred_element_type=F32))

        for n in range(ahead):
            start(n)
        for n, (which, some, here, rows) in enumerate(steps):
            start(n + ahead)
            states[which] = visit(scores[n], states[which], rows, some)
        return [(steps[which * chunks][2], state) for which, state in enumerate(states)]

    count = tiles.count()
    if loop:

        def one(slot, carry):
            for here, state in group_states([slot], True):
                first(here, state)
            return carry

        def another(slot, carry):
            for here, state in group_states([slot], False):
                more(here, state, slot < count)
            return carry

        lax.fori_loop(0, once, one, 0)
        lax.fori_loop(once, count, another, 0)
        return
    for here, state in group_states(range(once), True):
        first(here, state)
    for n, (here, state) in enumerate(group_states(range(once, tiles.slots), False)):
        more(here, state, once + n // blocks < count)


def lse_tiles(tiles, left, right, top, total, **how):
    def visit(s, state, rows, some):
        groups = [s[g] for g in range(s.shape[0])]
        new = functools.reduce(jnp.maximum, groups if state is None else [state[0]] + groups)
        total = None if state is None else state[1] * jnp.exp2(state[0] - new)
        for group in groups:
            p = jnp.exp2(group - new)
            total = p if total is None else total + p
        return new, total

    def first(here, state):
        top[:, here], total[:, here] = state

    def more(here, state, live):
        old, m = top[:, here], jnp.where(live, state[0], FLOOR)
        new = jnp.maximum(old, m)
        top[:, here] = new
        total[:, here] = total[:, here] * jnp.exp2(old - new) + state[1] * jnp.exp2(m - new)

    each_tile(tiles, left, right, visit, first, more, **how)
    m = top[...]
    largest = jnp.max(m, axis=0, keepdims=True)
    return largest, largest + log2(jnp.sum(total[...] * jnp.exp2(m - largest), axis=0, keepdims=True))


def weighed(groups, totals, columns, start, rows, some):
    for g, p in enumerate(groups):
        here = pl.ds(pl.multiple_of(rows.start + 8 * g, 8), 8)
        terms = [p]
        for c in range(3):
            lanes = slice(128 * c, 128 * (c + 1))
            if some is not None:
                col = jnp.broadcast_to(some[8 * g : 8 * (g + 1), start + c : start + c + 1], (8, 128))
                columns[here, lanes] = col
            else:
                col = columns[here, lanes]
            terms.append(p * jnp.concatenate([col] * (p.shape[1] // 128), axis=1))
        totals = terms if totals is None else [total + term for total, term in zip(totals, terms)]
    return totals


def mean_tiles(tiles, left, right, columns, points, start, top, sums, **how):
    def visit(s, state, rows, some):
        largest = jnp.max(s, axis=0)
        new = largest if state is None else jnp.maximum(state[0], largest)
        totals = None
        if state is not None:
            scale = jnp.exp2(state[0] - new)
            totals = [old * scale for old in state[1:]]
        groups = [jnp.exp2(s[g] - new) for g in range(s.shape[0])]
        return [new] + weighed(groups, totals, columns, start, rows, some)

    def first(here, state):
        top[:, here] = state[0]
        for c, total in enumerate(state[1:]):
            sums[c, :, here] = total

    def more(here, state, live):
        old, m = top[:, here], jnp.where(live, state[0], FLOOR)
        new = jnp.maximum(old, m)
        before, now = jnp.exp2(old - new), jnp.exp2(m - new)
        top[:, here] = new
        for c, total in enumerate(state[1:]):
            sums[c, :, here] = sums[c, :, here] * before + total * now

    each_tile(tiles, left, right, visit, first, more, points, **how)
    m = top[...]
    largest = jnp.max(m, axis=0, keepdims=True)
    scale = jnp.exp2(m - largest)
    mass, *others = [jnp.sum(sums[c] * scale, axis=0, keepdims=True) for c in range(4)]
    return [largest + log2(mass)] + [other / mass for other in others]


def plan_tiles(tiles, left, right, columns, points, start, sums, **how):
    def visit(s, state, rows, some):
        groups = (jnp.exp2(s[g]) for g in range(s.shape[0]))
        return weighed(groups, state, columns, start, rows, some)

    def first(here, state):
        for c, total in enumerate(state):
            sums[c, :, here] = total

    def more(here, state, live):
        for c, total in enumerate(state):
            sums[c, :, here] += jnp.where(live, total, 0.0)

    each_tile(tiles, left, right, visit, first, more, points, **how)
    return [jnp.sum(sums[c], axis=0, keepdims=True) for c in range(4)]


def combine(parts):
    largest = functools.reduce(jnp.maximum, parts)
    terms = [jnp.exp2(part - largest) for part in parts]
    whole = functools.reduce(jnp.add, terms)
    return largest + log2(whole), [term / whole for term in terms]


def rows_of(refs):
    return [refs[at] for at in range(refs.shape[0])]


class Tiles:
    def __init__(self, ref, points, kept_source):
        self.ref, self.slots, self.kept_source = ref, ref.shape[-1], kept_source
        self.sources, self.targets = points

    def count(self):
        return lax.div(self.ref[0, 0, 0], self.sources * self.targets)

    def starts(self, slot):
        packed = self.ref[0, 0, slot]
        source = start_of(lax.rem(packed, self.sources))
        target = start_of(lax.rem(lax.div(packed, self.sources), self.targets))
        return (target, source) if self.kept_source else (source, target)


def fetch(lists_in, lists, sem):
    copy = pltpu.make_async_copy(lists_in, lists, sem)
    copy.start()
    return copy


def sides(xc, yc):
    return xc.shape[1] // CLUSTER, yc.shape[1] // CLUSTER


def first_row_kernel(
    points, sources, targets, xc_out, yc_out, part_out, lists_out, log_source, log_target,
    lists, sem, stack, low, turned, top, total,
):
    cps, cpt = sides(xc_out, yc_out)
    count = points[9:10, 0:1].astype(jnp.int32)
    lists_out[...] = (count.reshape(1, 1, 1) * cpt + targets[...]) * cps + sources[...]
    copy = fetch(lists_out, lists, sem)
    log_source[...] = log2(points[6:7, :])
    log_target[...] = log2(points[7:8, :])
    xs, ys = points[0:3, :], points[3:6, :]
    place(stack, split(ys * KAPPA), TARGET_ORDER)
    yc_out[...] = stack[...].astype(BF16)
    turn(turned, low, yc_out, split(log_target[...] + KAPPA * (points[8:9, :] - half_square(ys))))
    place(stack, split(xs), SOURCE_ORDER)
    xc_out[...] = stack[...].astype(BF16)
    copy.wait()
    part_out[...] = lse_tiles(Tiles(lists, sides(xc_out, yc_out), True), turned, xc_out, top, total, lanes=256, ahead=2)[1]


def col_kernel(
    parts, log_source, xc, yc, lists_in, part_out, top_out, u_out, lists, sem, low, turned, top, total
):
    copy = fetch(lists_in, lists, sem)
    u = -combine([ref[...] for ref in parts])[0]
    u_out[...] = u
    turn(turned, low, xc, split(log_source[...] + u))
    copy.wait()
    top_out[...], part_out[...] = lse_tiles(Tiles(lists, sides(xc, yc), False), turned, yc, top, total, lanes=256)


def row_kernel(parts, log_target, xc, yc, lists_in, part_out, lists, sem, low, turned, top, total):
    copy = fetch(lists_in, lists, sem)
    turn(turned, low, yc, split(log_target[...] - combine([ref[...] for ref in parts])[0]))
    copy.wait()
    part_out[...] = lse_tiles(Tiles(lists, sides(xc, yc), True), turned, xc, top, total, lanes=256)[1]


def last_col_kernel(
    parts, u_before, top_before, kept, log_source, points, xc, yc, lists_in, f_out, u_out, part_out,
    lists, sem, low, turned, top, sums, columns, f, sem_out,
):
    copy = fetch(lists_in, lists, sem)
    u = -combine([ref[...] for ref in parts])[0]
    u_out[...] = log_source[...] + u
    f[...] = u * (1.0 / KAPPA) + half_square(points[0:3, :])
    back = fetch(f, f_out, sem_out)
    near = jnp.max(jnp.abs(u - u_before[...])) < LIMIT
    turn(turned, low, xc, split(u_out[...]), [jnp.ones_like(u)] * 3)
    copy.wait()
    tiles = Tiles(lists, sides(xc, yc), False)

    @pl.when(near)
    def _():
        mass, *moved = plan_tiles(tiles, turned, kept, columns, points, 0, sums, chunk=64, lanes=256, ahead=2)
        part_out[0:1, :] = top_before[...] + log2(mass)
        inverse = 1.0 / mass
        for c, total in enumerate(moved):
            part_out[c + 1 : c + 2, :] = total * inverse

    @pl.when(jnp.logical_not(near))
    def _():
        part, *means = mean_tiles(tiles, turned, kept, columns, points, 0, top, sums, loop=True)
        part_out[0:1, :] = top_before[...] + part
        for c, mean in enumerate(means):
            part_out[c + 1 : c + 2, :] = mean

    back.wait()


def merged(parts):
    lse, shares = combine([ref[0:1, :] for ref in parts])
    rows = range(1, parts[0].shape[0])
    return [lse] + [functools.reduce(jnp.add, [w * ref[r : r + 1, :] for w, ref in zip(shares, parts)]) for r in rows]


def merge_kernel(*refs):
    for r, row in enumerate(merged(refs[:-1])):
        refs[-1][r : r + 1, :] = row


def kept_kernel(potential, static, out, low, sign):
    out[0:16, :] = static[0:16, :]
    out[16:32, :] = lower_half(low, static, None, split(sign * potential[...]))


def target_kernel(parts, points, after, out):
    means = merged(parts)[1:]
    for c in range(3):
        out[c : c + 1, :] = points[7:8, :] * (points[3 + c : 4 + c, :] - means[c])


def gradient_kernel(parts, kept, log_target, points, xc, yc, lists_in, g_out, *rest, shares):
    source_out, (lists, sem, low, turned, sums, columns, g, whole, sem_out) = rest[:shares], rest[shares:]
    copy = fetch(lists_in, lists, sem)
    lse = combine([ref[0:1, :] for ref in parts])[0]
    xs = points[0:3, :]
    g[...] = half_square(points[3:6, :]) - lse * (1.0 / KAPPA)
    back = fetch(g, g_out, sem_out)
    turn(turned, low, yc, split(log_target[...] - lse), [jnp.ones_like(lse)] * 3)
    copy.wait()
    tiles = Tiles(lists, sides(xc, yc), True)
    mass, *moved = plan_tiles(tiles, turned, kept, columns, points, 3, sums, lanes=256)
    for c in range(3):
        whole[c : c + 1, :] = xs[c : c + 1, :] * mass - moved[c]
    place_tgt = lax.axis_index("tgt")
    for k, out in enumerate(source_out):
        width = out.shape[1]
        at = pl.multiple_of(peer(place_tgt, k, shares) * width, width)
        out[...] = whole[:, pl.ds(at, width)]
    back.wait()


VMEM = pl.BlockSpec(memory_space=pltpu.VMEM)
HBM = pl.BlockSpec(memory_space=pltpu.HBM)


def call(kernel, ins, lists, outs, scratch, far=()):
    return pl.pallas_call(
        kernel,
        out_shape=outs,
        in_specs=[VMEM] * len(ins) + [HBM] * len(lists),
        out_specs=[HBM if at in far else VMEM for at in range(len(outs))],
        scratch_shapes=scratch,
        compiler_params=pltpu.CompilerParams(vmem_limit_bytes=48 * 1024 * 1024),
    )(*ins, *lists)


def peer(i, k, n):
    return i ^ k if n & (n - 1) == 0 else (i + k) % n


def exchange(values, axis):
    n = lax.axis_size(axis)
    return values[:1] + [
        lax.ppermute(values[k], axis, [(i, peer(i, k, n)) for i in range(n)]) for k in range(1, n)
    ]


def sum_up(value, axis):
    n = lax.axis_size(axis)
    step = 1
    while True:
        others = [k * step for k in range(1, min(4, n // step))]
        values = [value] + [lax.ppermute(value, axis, [(i, i ^ k) for i in range(n)]) for k in others]
        step *= 4
        if step >= n:
            return values
        (value,) = call(merge_kernel, values, (), [jax.ShapeDtypeStruct(value.shape, F32)], [])


def bunch(kernel, size):
    return lambda *refs: kernel(refs[:size], *refs[size:])


def stacked(values, width):
    whole = sum(value.shape[0] for value in values)
    total, first = None, 0
    for value in values:
        after = whole - first - value.shape[0]
        padded = lax.pad(value, jnp.zeros((), value.dtype), [(first, after, 0), (0, width - value.shape[1], 0)]).astype(F32)
        total = padded if total is None else total + padded
        first += value.shape[0]
    return total


def body(source_points, target_points, source_weight, target_weight, target_start, tile_source, tile_target, tile_count):
    ns, nt = source_points.shape[1], target_points.shape[1]
    n_tgt = lax.axis_size("tgt")
    given = (source_points, target_points) + tuple(a.reshape(1, -1) for a in (source_weight, target_weight, target_start))
    points = stacked(given + (tile_count,), ns)
    given = (tile_source, tile_target)

    def rows(n, *k):
        return jax.ShapeDtypeStruct((*k, n), F32)

    def split_rows(n):
        return jax.ShapeDtypeStruct((DEPTH, n), BF16)

    def work(red):
        return [
            pltpu.SMEM(tile_source.shape, jnp.int32),
            pltpu.SemaphoreType.DMA,
            pltpu.VMEM((DEPTH // 2, red), F32),
            pltpu.VMEM((red, DEPTH), BF16),
        ]

    def state(kept):
        return [pltpu.VMEM((8, kept), F32), pltpu.VMEM((8, kept), F32)]

    def kept_operand(potential, static, sign):
        n = static.shape[1]
        kernel = functools.partial(kept_kernel, sign=sign)
        return call(kernel, (potential, static), (), [split_rows(n)], [pltpu.VMEM((DEPTH // 2, n), F32)])[0]

    first = work(nt)
    xc, yc, part, lists, log_source, log_target = call(
        first_row_kernel,
        (points, *given),
        (),
        [split_rows(ns), split_rows(nt), rows(ns, 1), jax.ShapeDtypeStruct(tile_source.shape, jnp.int32), rows(ns, 1), rows(nt, 1)],
        first[:2] + [pltpu.VMEM((DEPTH, ns), F32)] + first[2:] + state(ns),
    )
    known, lists = (xc, yc), (lists,)
    parts = exchange([part] * n_tgt, "tgt")
    part, top, u = call(
        bunch(col_kernel, n_tgt),
        (*parts, log_source, *known),
        lists,
        [rows(nt, 1), rows(nt, 1), rows(ns, 1)],
        work(ns) + state(nt),
    )
    kept = kept_operand(top, yc, -1.0)
    parts = sum_up(part, "src")
    (part,) = call(
        bunch(row_kernel, len(parts)),
        (*parts, log_target, *known),
        lists,
        [rows(ns, 1)],
        work(nt) + state(ns),
    )
    parts = exchange([part] * n_tgt, "tgt")
    f, u, part = call(
        bunch(last_col_kernel, n_tgt),
        (*parts, u, top, kept, log_source, points, *known),
        lists,
        [rows(ns, 1), rows(ns, 1), rows(nt, 4)],
        work(ns)
        + [
            pltpu.VMEM((8, nt), F32),
            pltpu.VMEM((4, 8, nt), F32),
            pltpu.VMEM((ns, 384), F32),
            pltpu.VMEM((1, ns), F32),
            pltpu.SemaphoreType.DMA,
        ],
        far=(0,),
    )
    kept = kept_operand(u, xc, 1.0)
    parts = sum_up(part, "src")
    g, *moved = call(
        bunch(functools.partial(gradient_kernel, shares=n_tgt), len(parts)),
        (*parts, kept, log_target, points, *known),
        lists,
        [rows(nt, 1)] + [rows(ns // n_tgt, 3)] * n_tgt,
        work(nt)
        + [
            pltpu.VMEM((4, 8, ns), F32),
            pltpu.VMEM((nt, 384), F32),
            pltpu.VMEM((1, nt), F32),
            pltpu.VMEM((3, ns), F32),
            pltpu.SemaphoreType.DMA,
        ],
        far=(0,),
    )
    (target_grad,) = call(bunch(target_kernel, len(parts)), (*parts, points, moved[0]), (), [rows(nt, 3)], [])
    own_grad = functools.reduce(jnp.add, exchange(moved, "tgt"))
    return (f.reshape(-1), g.reshape(-1), own_grad, target_grad)


def solution(mesh):
    return jax.shard_map(
        body,
        mesh=mesh,
        in_specs=(
            P(None, "src"),
            P(None, "tgt"),
            P("src"),
            P("tgt"),
            P("tgt"),
            P("src", "tgt", None),
            P("src", "tgt", None),
            P("src", "tgt"),
        ),
        out_specs=(P("src"), P("tgt"), P(None, ("src", "tgt")), P(None, "tgt")),
        check_vma=False,
    )
```

```python
import functools
import math

import jax
import jax.numpy as jnp
from jax import lax
from jax.experimental import pallas as pl
from jax.experimental.pallas import tpu as pltpu
from jax.sharding import PartitionSpec as P

CLUSTER = 512
EPSILON = 0.02
KAPPA = math.log2(math.e) / EPSILON
LOG2E = math.log2(math.e)
DEPTH = 32
FLOOR = -1e30
LIMIT = 60.0
F32 = jnp.float32
BF16 = jnp.bfloat16


def log2(value):
    return jnp.log(value) * LOG2E


def split(value):
    high = value.astype(BF16).astype(F32)
    rest = value - high
    middle = rest.astype(BF16).astype(F32)
    return (high, middle, rest - middle)


def half_square(points):
    return 0.5 * (points[0:1] * points[0:1] + points[1:2] * points[1:2] + points[2:3] * points[2:3])


SOURCE_ORDER = (0, 1, 2, 0, 0, 1)
TARGET_ORDER = (0, 0, 0, 1, 2, 1)


def place(scratch, parts, order):
    scratch[...] = jnp.zeros_like(scratch)
    for at, which in enumerate(order[:5]):
        scratch[3 * at : 3 * at + 3, :] = parts[which]
    scratch[16:19, :] = parts[order[5]]
    scratch[19:22, :] = jnp.ones_like(parts[0])


def lower_half(low, static, first=None, second=None):
    low[...] = static[16:32, :].astype(F32)
    for start, parts in ((3, first), (6, second)):
        for at, part in enumerate(parts or ()):
            low[start + at : start + at + 1, :] = part
    return low[...].astype(BF16)


def turn(turned, low, static, first, second=None):
    turned[...] = jnp.concatenate([static[0:16, :], lower_half(low, static, first, second)], axis=0).T


def start_of(index):
    return pl.multiple_of(index * CLUSTER, CLUSTER)


def grouped(value):
    return value.reshape(value.shape[0] // 8, 8, value.shape[1])


def each_tile(tiles, left, right, visit, first, more, points=None, ahead=1, chunk=128, lanes=CLUSTER, loop=False):
    once = right.shape[1] // CLUSTER
    chunks, blocks = CLUSTER // chunk, CLUSTER // lanes

    def group_states(group, fresh):
        steps = []
        for which, slot in enumerate(group):
            r, k = tiles.starts(slot)
            given = points[0:8, pl.ds(r, CLUSTER)].T if fresh and points is not None else None
            for block in range(blocks):
                here = pl.ds(pl.multiple_of(k + block * lanes, lanes), lanes)
                for at in range(chunks):
                    rows = pl.ds(pl.multiple_of(r + at * chunk, chunk), chunk)
                    some = None if given is None or block else given[at * chunk : (at + 1) * chunk, :]
                    steps.append((which * blocks + block, some, here, rows))
        states = [None] * (len(group) * blocks)
        scores = [None] * len(steps)

        def start(n):
            if n < len(steps):
                _, _, here, rows = steps[n]
                scores[n] = grouped(jnp.dot(left[rows, :], right[:, here], preferred_element_type=F32))

        for n in range(ahead):
            start(n)
        for n, (which, some, here, rows) in enumerate(steps):
            start(n + ahead)
            states[which] = visit(scores[n], states[which], rows, some)
        return [(steps[which * chunks][2], state) for which, state in enumerate(states)]

    count = tiles.count()
    if loop:

        def one(slot, carry):
            for here, state in group_states([slot], True):
                first(here, state)
            return carry

        def another(slot, carry):
            for here, state in group_states([slot], False):
                more(here, state, slot < count)
            return carry

        lax.fori_loop(0, once, one, 0)
        lax.fori_loop(once, count, another, 0)
        return
    for here, state in group_states(range(once), True):
        first(here, state)
    for n, (here, state) in enumerate(group_states(range(once, tiles.slots), False)):
        more(here, state, once + n // blocks < count)


def lse_tiles(tiles, left, right, top, total, **how):
    def visit(s, state, rows, some):
        groups = [s[g] for g in range(s.shape[0])]
        new = functools.reduce(jnp.maximum, groups if state is None else [state[0]] + groups)
        total = None if state is None else state[1] * jnp.exp2(state[0] - new)
        for group in groups:
            p = jnp.exp2(group - new)
            total = p if total is None else total + p
        return new, total

    def first(here, state):
        top[:, here], total[:, here] = state

    def more(here, state, live):
        old, m = top[:, here], jnp.where(live, state[0], FLOOR)
        new = jnp.maximum(old, m)
        top[:, here] = new
        total[:, here] = total[:, here] * jnp.exp2(old - new) + state[1] * jnp.exp2(m - new)

    each_tile(tiles, left, right, visit, first, more, **how)
    m = top[...]
    largest = jnp.max(m, axis=0, keepdims=True)
    return largest, largest + log2(jnp.sum(total[...] * jnp.exp2(m - largest), axis=0, keepdims=True))


def weighed(groups, totals, columns, start, rows, some):
    for g, p in enumerate(groups):
        here = pl.ds(pl.multiple_of(rows.start + 8 * g, 8), 8)
        terms = [p]
        for c in range(3):
            lanes = slice(128 * c, 128 * (c + 1))
            if some is not None:
                col = jnp.broadcast_to(some[8 * g : 8 * (g + 1), start + c : start + c + 1], (8, 128))
                columns[here, lanes] = col
            else:
                col = columns[here, lanes]
            terms.append(p * jnp.concatenate([col] * (p.shape[1] // 128), axis=1))
        totals = terms if totals is None else [total + term for total, term in zip(totals, terms)]
    return totals


def mean_tiles(tiles, left, right, columns, points, start, top, sums, **how):
    def visit(s, state, rows, some):
        largest = jnp.max(s, axis=0)
        new = largest if state is None else jnp.maximum(state[0], largest)
        totals = None
        if state is not None:
            scale = jnp.exp2(state[0] - new)
            totals = [old * scale for old in state[1:]]
        groups = [jnp.exp2(s[g] - new) for g in range(s.shape[0])]
        return [new] + weighed(groups, totals, columns, start, rows, some)

    def first(here, state):
        top[:, here] = state[0]
        for c, total in enumerate(state[1:]):
            sums[c, :, here] = total

    def more(here, state, live):
        old, m = top[:, here], jnp.where(live, state[0], FLOOR)
        new = jnp.maximum(old, m)
        before, now = jnp.exp2(old - new), jnp.exp2(m - new)
        top[:, here] = new
        for c, total in enumerate(state[1:]):
            sums[c, :, here] = sums[c, :, here] * before + total * now

    each_tile(tiles, left, right, visit, first, more, points, **how)
    m = top[...]
    largest = jnp.max(m, axis=0, keepdims=True)
    scale = jnp.exp2(m - largest)
    mass, *others = [jnp.sum(sums[c] * scale, axis=0, keepdims=True) for c in range(4)]
    return [largest + log2(mass)] + [other / mass for other in others]


def plan_tiles(tiles, left, right, columns, points, start, sums, **how):
    def visit(s, state, rows, some):
        groups = (jnp.exp2(s[g]) for g in range(s.shape[0]))
        return weighed(groups, state, columns, start, rows, some)

    def first(here, state):
        for c, total in enumerate(state):
            sums[c, :, here] = total

    def more(here, state, live):
        for c, total in enumerate(state):
            sums[c, :, here] += jnp.where(live, total, 0.0)

    each_tile(tiles, left, right, visit, first, more, points, **how)
    return [jnp.sum(sums[c], axis=0, keepdims=True) for c in range(4)]


def combine(parts):
    largest = functools.reduce(jnp.maximum, parts)
    terms = [jnp.exp2(part - largest) for part in parts]
    whole = functools.reduce(jnp.add, terms)
    return largest + log2(whole), [term / whole for term in terms]


def rows_of(refs):
    return [refs[at] for at in range(refs.shape[0])]


class Tiles:
    def __init__(self, ref, points, kept_source):
        self.ref, self.slots, self.kept_source = ref, ref.shape[-1], kept_source
        self.sources, self.targets = points

    def count(self):
        return lax.div(self.ref[0, 0, 0], self.sources * self.targets)

    def starts(self, slot):
        packed = self.ref[0, 0, slot]
        source = start_of(lax.rem(packed, self.sources))
        target = start_of(lax.rem(lax.div(packed, self.sources), self.targets))
        return (target, source) if self.kept_source else (source, target)


def fetch(lists_in, lists, sem):
    copy = pltpu.make_async_copy(lists_in, lists, sem)
    copy.start()
    return copy


def sides(xc, yc):
    return xc.shape[1] // CLUSTER, yc.shape[1] // CLUSTER


def first_row_kernel(
    points, sources, targets, xc_out, yc_out, part_out, lists_out, log_source, log_target,
    lists, sem, stack, low, turned, top, total,
):
    cps, cpt = sides(xc_out, yc_out)
    count = points[9:10, 0:1].astype(jnp.int32)
    lists_out[...] = (count.reshape(1, 1, 1) * cpt + targets[...]) * cps + sources[...]
    copy = fetch(lists_out, lists, sem)
    log_source[...] = log2(points[6:7, :])
    log_target[...] = log2(points[7:8, :])
    xs, ys = points[0:3, :], points[3:6, :]
    place(stack, split(ys * KAPPA), TARGET_ORDER)
    yc_out[...] = stack[...].astype(BF16)
    turn(turned, low, yc_out, split(log_target[...] + KAPPA * (points[8:9, :] - half_square(ys))))
    place(stack, split(xs), SOURCE_ORDER)
    xc_out[...] = stack[...].astype(BF16)
    copy.wait()
    part_out[...] = lse_tiles(Tiles(lists, sides(xc_out, yc_out), True), turned, xc_out, top, total, lanes=256)[1]


def col_kernel(
    parts, log_source, xc, yc, lists_in, part_out, top_out, u_out, lists, sem, low, turned, top, total
):
    copy = fetch(lists_in, lists, sem)
    u = -combine([ref[...] for ref in parts])[0]
    u_out[...] = u
    turn(turned, low, xc, split(log_source[...] + u))
    copy.wait()
    top_out[...], part_out[...] = lse_tiles(Tiles(lists, sides(xc, yc), False), turned, yc, top, total, lanes=256)


def row_kernel(parts, log_target, xc, yc, lists_in, part_out, lists, sem, low, turned, top, total):
    copy = fetch(lists_in, lists, sem)
    turn(turned, low, yc, split(log_target[...] - combine([ref[...] for ref in parts])[0]))
    copy.wait()
    part_out[...] = lse_tiles(Tiles(lists, sides(xc, yc), True), turned, xc, top, total, lanes=256)[1]


def last_col_kernel(
    parts, u_before, top_before, kept, log_source, points, xc, yc, lists_in, f_out, u_out, part_out,
    lists, sem, low, turned, top, sums, columns, f, sem_out,
):
    copy = fetch(lists_in, lists, sem)
    u = -combine([ref[...] for ref in parts])[0]
    u_out[...] = log_source[...] + u
    f[...] = u * (1.0 / KAPPA) + half_square(points[0:3, :])
    back = fetch(f, f_out, sem_out)
    near = jnp.max(jnp.abs(u - u_before[...])) < LIMIT
    turn(turned, low, xc, split(u_out[...]), [jnp.ones_like(u)] * 3)
    copy.wait()
    tiles = Tiles(lists, sides(xc, yc), False)

    @pl.when(near)
    def _():
        mass, *moved = plan_tiles(tiles, turned, kept, columns, points, 0, sums, chunk=32, ahead=2)
        part_out[0:1, :] = top_before[...] + log2(mass)
        inverse = 1.0 / mass
        for c, total in enumerate(moved):
            part_out[c + 1 : c + 2, :] = total * inverse

    @pl.when(jnp.logical_not(near))
    def _():
        part, *means = mean_tiles(tiles, turned, kept, columns, points, 0, top, sums, loop=True)
        part_out[0:1, :] = top_before[...] + part
        for c, mean in enumerate(means):
            part_out[c + 1 : c + 2, :] = mean

    back.wait()


def merged(parts):
    lse, shares = combine([ref[0:1, :] for ref in parts])
    rows = range(1, parts[0].shape[0])
    return [lse] + [functools.reduce(jnp.add, [w * ref[r : r + 1, :] for w, ref in zip(shares, parts)]) for r in rows]


def merge_kernel(*refs):
    for r, row in enumerate(merged(refs[:-1])):
        refs[-1][r : r + 1, :] = row


def kept_kernel(potential, static, out, low, sign):
    out[0:16, :] = static[0:16, :]
    out[16:32, :] = lower_half(low, static, None, split(sign * potential[...]))


def target_kernel(parts, points, after, out):
    means = merged(parts)[1:]
    for c in range(3):
        out[c : c + 1, :] = points[7:8, :] * (points[3 + c : 4 + c, :] - means[c])


def gradient_kernel(parts, kept, log_target, points, xc, yc, lists_in, g_out, *rest, shares):
    source_out, (lists, sem, low, turned, sums, columns, g, whole, sem_out) = rest[:shares], rest[shares:]
    copy = fetch(lists_in, lists, sem)
    lse = combine([ref[0:1, :] for ref in parts])[0]
    xs = points[0:3, :]
    g[...] = half_square(points[3:6, :]) - lse * (1.0 / KAPPA)
    back = fetch(g, g_out, sem_out)
    turn(turned, low, yc, split(log_target[...] - lse), [jnp.ones_like(lse)] * 3)
    copy.wait()
    tiles = Tiles(lists, sides(xc, yc), True)
    mass, *moved = plan_tiles(tiles, turned, kept, columns, points, 3, sums, chunk=32, ahead=2)
    for c in range(3):
        whole[c : c + 1, :] = xs[c : c + 1, :] * mass - moved[c]
    place_tgt = lax.axis_index("tgt")
    for k, out in enumerate(reversed(source_out)):
        width = out.shape[1]
        at = pl.multiple_of(peer(place_tgt, k, shares) * width, width)
        out[...] = whole[:, pl.ds(at, width)]
    back.wait()


VMEM = pl.BlockSpec(memory_space=pltpu.VMEM)
HBM = pl.BlockSpec(memory_space=pltpu.HBM)


def call(kernel, ins, lists, outs, scratch, far=()):
    return pl.pallas_call(
        kernel,
        out_shape=outs,
        in_specs=[VMEM] * len(ins) + [HBM] * len(lists),
        out_specs=[HBM if at in far else VMEM for at in range(len(outs))],
        scratch_shapes=scratch,
        compiler_params=pltpu.CompilerParams(vmem_limit_bytes=48 * 1024 * 1024),
    )(*ins, *lists)


def peer(i, k, n):
    return i ^ k if n & (n - 1) == 0 else (i + k) % n


def exchange(values, axis):
    n = lax.axis_size(axis)
    far_first = [lax.ppermute(values[k], axis, [(i, peer(i, k, n)) for i in range(n)]) for k in range(n - 1, 0, -1)]
    return values[:1] + far_first[::-1]


def sum_up(value, axis):
    n = lax.axis_size(axis)
    step = 1
    while True:
        others = [k * step for k in range(1, min(4, n // step))]
        values = [value] + [lax.ppermute(value, axis, [(i, i ^ k) for i in range(n)]) for k in others]
        step *= 4
        if step >= n:
            return values
        (value,) = call(merge_kernel, values, (), [jax.ShapeDtypeStruct(value.shape, F32)], [])


def bunch(kernel, size):
    return lambda *refs: kernel(refs[:size], *refs[size:])


def stacked(values, width):
    whole = sum(value.shape[0] for value in values)
    total, first = None, 0
    for value in values:
        after = whole - first - value.shape[0]
        padded = lax.pad(value, jnp.zeros((), value.dtype), [(first, after, 0), (0, width - value.shape[1], 0)]).astype(F32)
        total = padded if total is None else total + padded
        first += value.shape[0]
    return total


def body(source_points, target_points, source_weight, target_weight, target_start, tile_source, tile_target, tile_count):
    ns, nt = source_points.shape[1], target_points.shape[1]
    n_tgt = lax.axis_size("tgt")
    given = (source_points, target_points) + tuple(a.reshape(1, -1) for a in (source_weight, target_weight, target_start))
    points = stacked(given + (tile_count,), ns)
    given = (tile_source, tile_target)

    def rows(n, *k):
        return jax.ShapeDtypeStruct((*k, n), F32)

    def split_rows(n):
        return jax.ShapeDtypeStruct((DEPTH, n), BF16)

    def work(red):
        return [
            pltpu.SMEM(tile_source.shape, jnp.int32),
            pltpu.SemaphoreType.DMA,
            pltpu.VMEM((DEPTH // 2, red), F32),
            pltpu.VMEM((red, DEPTH), BF16),
        ]

    def state(kept):
        return [pltpu.VMEM((8, kept), F32), pltpu.VMEM((8, kept), F32)]

    def kept_operand(potential, static, sign):
        n = static.shape[1]
        kernel = functools.partial(kept_kernel, sign=sign)
        return call(kernel, (potential, static), (), [split_rows(n)], [pltpu.VMEM((DEPTH // 2, n), F32)])[0]

    first = work(nt)
    xc, yc, part, lists, log_source, log_target = call(
        first_row_kernel,
        (points, *given),
        (),
        [split_rows(ns), split_rows(nt), rows(ns, 1), jax.ShapeDtypeStruct(tile_source.shape, jnp.int32), rows(ns, 1), rows(nt, 1)],
        first[:2] + [pltpu.VMEM((DEPTH, ns), F32)] + first[2:] + state(ns),
    )
    known, lists = (xc, yc), (lists,)
    parts = exchange([part] * n_tgt, "tgt")
    part, top, u = call(
        bunch(col_kernel, n_tgt),
        (*parts, log_source, *known),
        lists,
        [rows(nt, 1), rows(nt, 1), rows(ns, 1)],
        work(ns) + state(nt),
    )
    kept = kept_operand(top, yc, -1.0)
    parts = sum_up(part, "src")
    (part,) = call(
        bunch(row_kernel, len(parts)),
        (*parts, log_target, *known),
        lists,
        [rows(ns, 1)],
        work(nt) + state(ns),
    )
    parts = exchange([part] * n_tgt, "tgt")
    f, u, part = call(
        bunch(last_col_kernel, n_tgt),
        (*parts, u, top, kept, log_source, points, *known),
        lists,
        [rows(ns, 1), rows(ns, 1), rows(nt, 4)],
        work(ns)
        + [
            pltpu.VMEM((8, nt), F32),
            pltpu.VMEM((4, 8, nt), F32),
            pltpu.VMEM((ns, 384), F32),
            pltpu.VMEM((1, ns), F32),
            pltpu.SemaphoreType.DMA,
        ],
        far=(0,),
    )
    kept = kept_operand(u, xc, 1.0)
    parts = sum_up(part, "src")
    g, *moved = call(
        bunch(functools.partial(gradient_kernel, shares=n_tgt), len(parts)),
        (*parts, kept, log_target, points, *known),
        lists,
        [rows(nt, 1)] + [rows(ns // n_tgt, 3)] * n_tgt,
        work(nt)
        + [
            pltpu.VMEM((4, 8, ns), F32),
            pltpu.VMEM((nt, 384), F32),
            pltpu.VMEM((1, nt), F32),
            pltpu.VMEM((3, ns), F32),
            pltpu.SemaphoreType.DMA,
        ],
        far=(0,),
    )
    (target_grad,) = call(bunch(target_kernel, len(parts)), (*parts, points, moved[-1]), (), [rows(nt, 3)], [])
    own, *others = exchange(moved[::-1], "tgt")
    own_grad = functools.reduce(jnp.add, others[::-1], own)
    return (f.reshape(-1), g.reshape(-1), own_grad, target_grad)


def solution(mesh):
    return jax.shard_map(
        body,
        mesh=mesh,
        in_specs=(
            P(None, "src"),
            P(None, "tgt"),
            P("src"),
            P("tgt"),
            P("tgt"),
            P("src", "tgt", None),
            P("src", "tgt", None),
            P("src", "tgt"),
        ),
        out_specs=(P("src"), P("tgt"), P(None, ("src", "tgt")), P(None, "tgt")),
        check_vma=False,
    )
```

```python
import functools
import math

import jax
import jax.numpy as jnp
from jax import lax
from jax.experimental import pallas as pl
from jax.experimental.pallas import tpu as pltpu
from jax.sharding import PartitionSpec as P

CLUSTER = 512
EPSILON = 0.02
KAPPA = math.log2(math.e) / EPSILON
LOG2E = math.log2(math.e)
DEPTH = 32
FLOOR = -1e30
LIMIT = 60.0
F32 = jnp.float32
BF16 = jnp.bfloat16


def log2(value):
    return jnp.log(value) * LOG2E


def split(value):
    high = value.astype(BF16).astype(F32)
    rest = value - high
    middle = rest.astype(BF16).astype(F32)
    return (high, middle, rest - middle)


def half_square(points):
    return 0.5 * (points[0:1] * points[0:1] + points[1:2] * points[1:2] + points[2:3] * points[2:3])


SOURCE_ORDER = (0, 1, 2, 0, 0, 1)
TARGET_ORDER = (0, 0, 0, 1, 2, 1)


def place(scratch, parts, order):
    scratch[15:16, :] = jnp.zeros((1, scratch.shape[1]), F32)
    scratch[22:DEPTH, :] = jnp.zeros((DEPTH - 22, scratch.shape[1]), F32)
    for at, which in enumerate(order[:5]):
        scratch[3 * at : 3 * at + 3, :] = parts[which]
    scratch[16:19, :] = parts[order[5]]
    scratch[19:22, :] = jnp.ones_like(parts[0])


def lower_half(low, static, first=None, second=None):
    low[...] = static[16:32, :].astype(F32)
    for start, parts in ((3, first), (6, second)):
        for at, part in enumerate(parts or ()):
            low[start + at : start + at + 1, :] = part
    return low[...].astype(BF16)


def turn(turned, low, static, first, second=None):
    turned[...] = jnp.concatenate([static[0:16, :], lower_half(low, static, first, second)], axis=0).T


def start_of(index):
    return pl.multiple_of(index * CLUSTER, CLUSTER)


def grouped(value):
    return value.reshape(value.shape[0] // 8, 8, value.shape[1])


def each_tile(tiles, left, right, visit, first, more, points=None, ahead=1, chunk=128, lanes=CLUSTER, loop=False):
    once = right.shape[1] // CLUSTER
    chunks, blocks = CLUSTER // chunk, CLUSTER // lanes

    def group_states(group, fresh):
        steps = []
        for which, slot in enumerate(group):
            r, k = tiles.starts(slot)
            given = points[0:8, pl.ds(r, CLUSTER)].T if fresh and points is not None else None
            for block in range(blocks):
                here = pl.ds(pl.multiple_of(k + block * lanes, lanes), lanes)
                for at in range(chunks):
                    rows = pl.ds(pl.multiple_of(r + at * chunk, chunk), chunk)
                    some = None if given is None or block else given[at * chunk : (at + 1) * chunk, :]
                    steps.append((which * blocks + block, some, here, rows))
        states = [None] * (len(group) * blocks)
        scores = [None] * len(steps)

        def start(n):
            if n < len(steps):
                _, _, here, rows = steps[n]
                scores[n] = grouped(jnp.dot(left[rows, :], right[:, here], preferred_element_type=F32))

        for n in range(ahead):
            start(n)
        for n, (which, some, here, rows) in enumerate(steps):
            start(n + ahead)
            states[which] = visit(scores[n], states[which], rows, some)
        return [(steps[which * chunks][2], state) for which, state in enumerate(states)]

    count = tiles.count()
    if loop:

        def one(slot, carry):
            for here, state in group_states([slot], True):
                first(here, state)
            return carry

        def another(slot, carry):
            for here, state in group_states([slot], False):
                more(here, state, slot < count)
            return carry

        lax.fori_loop(0, once, one, 0)
        lax.fori_loop(once, count, another, 0)
        return
    for here, state in group_states(range(once), True):
        first(here, state)
    for n, (here, state) in enumerate(group_states(range(once, tiles.slots), False)):
        more(here, state, once + n // blocks < count)


def lse_tiles(tiles, left, right, top, total, **how):
    def visit(s, state, rows, some):
        groups = [s[g] for g in range(s.shape[0])]
        new = functools.reduce(jnp.maximum, groups if state is None else [state[0]] + groups)
        total = None if state is None else state[1] * jnp.exp2(state[0] - new)
        for group in groups:
            p = jnp.exp2(group - new)
            total = p if total is None else total + p
        return new, total

    def first(here, state):
        top[:, here], total[:, here] = state

    def more(here, state, live):
        old, m = top[:, here], jnp.where(live, state[0], FLOOR)
        new = jnp.maximum(old, m)
        top[:, here] = new
        total[:, here] = total[:, here] * jnp.exp2(old - new) + state[1] * jnp.exp2(m - new)

    each_tile(tiles, left, right, visit, first, more, **how)
    m = top[...]
    largest = jnp.max(m, axis=0, keepdims=True)
    return largest, largest + log2(jnp.sum(total[...] * jnp.exp2(m - largest), axis=0, keepdims=True))


def weighed(groups, totals, columns, start, rows, some):
    for g, p in enumerate(groups):
        here = pl.ds(pl.multiple_of(rows.start + 8 * g, 8), 8)
        terms = [p]
        for c in range(3):
            lanes = slice(128 * c, 128 * (c + 1))
            if some is not None:
                col = jnp.broadcast_to(some[8 * g : 8 * (g + 1), start + c : start + c + 1], (8, 128))
                columns[here, lanes] = col
            else:
                col = columns[here, lanes]
            terms.append(p * jnp.concatenate([col] * (p.shape[1] // 128), axis=1))
        totals = terms if totals is None else [total + term for total, term in zip(totals, terms)]
    return totals


def mean_tiles(tiles, left, right, columns, points, start, top, sums, **how):
    def visit(s, state, rows, some):
        largest = jnp.max(s, axis=0)
        new = largest if state is None else jnp.maximum(state[0], largest)
        totals = None
        if state is not None:
            scale = jnp.exp2(state[0] - new)
            totals = [old * scale for old in state[1:]]
        groups = [jnp.exp2(s[g] - new) for g in range(s.shape[0])]
        return [new] + weighed(groups, totals, columns, start, rows, some)

    def first(here, state):
        top[:, here] = state[0]
        for c, total in enumerate(state[1:]):
            sums[c, :, here] = total

    def more(here, state, live):
        old, m = top[:, here], jnp.where(live, state[0], FLOOR)
        new = jnp.maximum(old, m)
        before, now = jnp.exp2(old - new), jnp.exp2(m - new)
        top[:, here] = new
        for c, total in enumerate(state[1:]):
            sums[c, :, here] = sums[c, :, here] * before + total * now

    each_tile(tiles, left, right, visit, first, more, points, **how)
    m = top[...]
    largest = jnp.max(m, axis=0, keepdims=True)
    scale = jnp.exp2(m - largest)
    mass, *others = [jnp.sum(sums[c] * scale, axis=0, keepdims=True) for c in range(4)]
    return [largest + log2(mass)] + [other / mass for other in others]


def plan_tiles(tiles, left, right, columns, points, start, sums, **how):
    def visit(s, state, rows, some):
        groups = (jnp.exp2(s[g]) for g in range(s.shape[0]))
        return weighed(groups, state, columns, start, rows, some)

    def first(here, state):
        for c, total in enumerate(state):
            sums[c, :, here] = total

    def more(here, state, live):
        for c, total in enumerate(state):
            sums[c, :, here] += jnp.where(live, total, 0.0)

    each_tile(tiles, left, right, visit, first, more, points, **how)
    return [jnp.sum(sums[c], axis=0, keepdims=True) for c in range(4)]


def combine(parts):
    largest = functools.reduce(jnp.maximum, parts)
    terms = [jnp.exp2(part - largest) for part in parts]
    whole = functools.reduce(jnp.add, terms)
    return largest + log2(whole), [term / whole for term in terms]


def rows_of(refs):
    return [refs[at] for at in range(refs.shape[0])]


class Tiles:
    def __init__(self, ref, points, kept_source):
        self.ref, self.slots, self.kept_source = ref, ref.shape[-1], kept_source
        self.sources, self.targets = points

    def count(self):
        return lax.div(self.ref[0, 0, 0], self.sources * self.targets)

    def starts(self, slot):
        packed = self.ref[0, 0, slot]
        source = start_of(lax.rem(packed, self.sources))
        target = start_of(lax.rem(lax.div(packed, self.sources), self.targets))
        return (target, source) if self.kept_source else (source, target)


def fetch(lists_in, lists, sem):
    copy = pltpu.make_async_copy(lists_in, lists, sem)
    copy.start()
    return copy


def sides(xc, yc):
    return xc.shape[1] // CLUSTER, yc.shape[1] // CLUSTER


def first_row_kernel(
    points, sources, targets, xc_out, yc_out, part_out, lists_out, log_source, log_target,
    lists, sem, stack, low, turned, top, total,
):
    cps, cpt = sides(xc_out, yc_out)
    count = points[9:10, 0:1].astype(jnp.int32)
    lists_out[...] = (count.reshape(1, 1, 1) * cpt + targets[...]) * cps + sources[...]
    copy = fetch(lists_out, lists, sem)
    log_source[...] = log2(points[6:7, :])
    log_target[...] = log2(points[7:8, :])
    xs, ys = points[0:3, :], points[3:6, :]
    place(stack, split(ys * KAPPA), TARGET_ORDER)
    yc_out[...] = stack[...].astype(BF16)
    turn(turned, low, yc_out, split(log_target[...] + KAPPA * (points[8:9, :] - half_square(ys))))
    place(stack, split(xs), SOURCE_ORDER)
    xc_out[...] = stack[...].astype(BF16)
    copy.wait()
    part_out[...] = lse_tiles(Tiles(lists, sides(xc_out, yc_out), True), turned, xc_out, top, total, lanes=256)[1]


def col_kernel(
    parts, log_source, xc, yc, lists_in, part_out, top_out, u_out, lists, sem, low, turned, top, total
):
    copy = fetch(lists_in, lists, sem)
    u = -combine([ref[...] for ref in parts])[0]
    u_out[...] = u
    turn(turned, low, xc, split(log_source[...] + u))
    copy.wait()
    top_out[...], part_out[...] = lse_tiles(Tiles(lists, sides(xc, yc), False), turned, yc, top, total, lanes=256)


def row_kernel(parts, log_target, xc, yc, lists_in, part_out, lists, sem, low, turned, top, total):
    copy = fetch(lists_in, lists, sem)
    turn(turned, low, yc, split(log_target[...] - combine([ref[...] for ref in parts])[0]))
    copy.wait()
    part_out[...] = lse_tiles(Tiles(lists, sides(xc, yc), True), turned, xc, top, total, lanes=256)[1]


def last_col_kernel(
    parts, u_before, top_before, kept, log_source, points, xc, yc, lists_in, f_out, u_out, part_out,
    lists, sem, low, turned, top, sums, columns, f, sem_out,
):
    copy = fetch(lists_in, lists, sem)
    u = -combine([ref[...] for ref in parts])[0]
    u_out[...] = log_source[...] + u
    f[...] = u * (1.0 / KAPPA) + half_square(points[0:3, :])
    back = fetch(f, f_out, sem_out)
    near = jnp.max(jnp.abs(u - u_before[...])) < LIMIT
    turn(turned, low, xc, split(u_out[...]), [jnp.ones_like(u)] * 3)
    copy.wait()
    tiles = Tiles(lists, sides(xc, yc), False)

    @pl.when(near)
    def _():
        mass, *moved = plan_tiles(tiles, turned, kept, columns, points, 0, sums, chunk=32, ahead=4)
        part_out[0:1, :] = top_before[...] + log2(mass)
        inverse = 1.0 / mass
        for c, total in enumerate(moved):
            part_out[c + 1 : c + 2, :] = total * inverse

    @pl.when(jnp.logical_not(near))
    def _():
        part, *means = mean_tiles(tiles, turned, kept, columns, points, 0, top, sums, loop=True)
        part_out[0:1, :] = top_before[...] + part
        for c, mean in enumerate(means):
            part_out[c + 1 : c + 2, :] = mean

    back.wait()


def merged(parts):
    lse, shares = combine([ref[0:1, :] for ref in parts])
    rows = range(1, parts[0].shape[0])
    return [lse] + [functools.reduce(jnp.add, [w * ref[r : r + 1, :] for w, ref in zip(shares, parts)]) for r in rows]


def merge_kernel(*refs):
    for r, row in enumerate(merged(refs[:-1])):
        refs[-1][r : r + 1, :] = row


def kept_kernel(potential, static, out, low, sign):
    out[0:16, :] = static[0:16, :]
    out[16:32, :] = lower_half(low, static, None, split(sign * potential[...]))


def target_kernel(parts, points, after, out):
    means = merged(parts)[1:]
    for c in range(3):
        out[c : c + 1, :] = points[7:8, :] * (points[3 + c : 4 + c, :] - means[c])


def gradient_kernel(parts, kept, log_target, points, xc, yc, lists_in, g_out, *rest, shares):
    source_out, (lists, sem, low, turned, sums, columns, g, whole, sem_out) = rest[:shares], rest[shares:]
    copy = fetch(lists_in, lists, sem)
    lse = combine([ref[0:1, :] for ref in parts])[0]
    xs = points[0:3, :]
    g[...] = half_square(points[3:6, :]) - lse * (1.0 / KAPPA)
    back = fetch(g, g_out, sem_out)
    turn(turned, low, yc, split(log_target[...] - lse), [jnp.ones_like(lse)] * 3)
    copy.wait()
    tiles = Tiles(lists, sides(xc, yc), True)
    mass, *moved = plan_tiles(tiles, turned, kept, columns, points, 3, sums, chunk=64, ahead=2)
    for c in range(3):
        whole[c : c + 1, :] = xs[c : c + 1, :] * mass - moved[c]
    place_tgt = lax.axis_index("tgt")
    for k, out in enumerate(reversed(source_out)):
        width = out.shape[1]
        at = pl.multiple_of(peer(place_tgt, k, shares) * width, width)
        out[...] = whole[:, pl.ds(at, width)]
    back.wait()


VMEM = pl.BlockSpec(memory_space=pltpu.VMEM)
HBM = pl.BlockSpec(memory_space=pltpu.HBM)


def call(kernel, ins, lists, outs, scratch, far=()):
    return pl.pallas_call(
        kernel,
        out_shape=outs,
        in_specs=[VMEM] * len(ins) + [HBM] * len(lists),
        out_specs=[HBM if at in far else VMEM for at in range(len(outs))],
        scratch_shapes=scratch,
        compiler_params=pltpu.CompilerParams(vmem_limit_bytes=48 * 1024 * 1024),
    )(*ins, *lists)


def peer(i, k, n):
    return i ^ k if n & (n - 1) == 0 else (i + k) % n


def exchange(values, axis):
    n = lax.axis_size(axis)
    far_first = [lax.ppermute(values[k], axis, [(i, peer(i, k, n)) for i in range(n)]) for k in range(n - 1, 0, -1)]
    return values[:1] + far_first[::-1]


def sum_up(value, axis):
    n = lax.axis_size(axis)
    step = 1
    while True:
        others = [k * step for k in range(1, min(4, n // step))]
        values = [value] + [lax.ppermute(value, axis, [(i, i ^ k) for i in range(n)]) for k in others]
        step *= 4
        if step >= n:
            return values
        (value,) = call(merge_kernel, values, (), [jax.ShapeDtypeStruct(value.shape, F32)], [])


def bunch(kernel, size):
    return lambda *refs: kernel(refs[:size], *refs[size:])


def stacked(values, width):
    whole = sum(value.shape[0] for value in values)
    total, first = None, 0
    for value in values:
        after = whole - first - value.shape[0]
        padded = lax.pad(value, jnp.zeros((), value.dtype), [(first, after, 0), (0, width - value.shape[1], 0)]).astype(F32)
        total = padded if total is None else total + padded
        first += value.shape[0]
    return total


def body(source_points, target_points, source_weight, target_weight, target_start, tile_source, tile_target, tile_count):
    ns, nt = source_points.shape[1], target_points.shape[1]
    n_tgt = lax.axis_size("tgt")
    given = (source_points, target_points) + tuple(a.reshape(1, -1) for a in (source_weight, target_weight, target_start))
    points = stacked(given + (tile_count,), ns)
    given = (tile_source, tile_target)

    def rows(n, *k):
        return jax.ShapeDtypeStruct((*k, n), F32)

    def split_rows(n):
        return jax.ShapeDtypeStruct((DEPTH, n), BF16)

    def work(red):
        return [
            pltpu.SMEM(tile_source.shape, jnp.int32),
            pltpu.SemaphoreType.DMA,
            pltpu.VMEM((DEPTH // 2, red), F32),
            pltpu.VMEM((red, DEPTH), BF16),
        ]

    def state(kept):
        return [pltpu.VMEM((8, kept), F32), pltpu.VMEM((8, kept), F32)]

    def kept_operand(potential, static, sign):
        n = static.shape[1]
        kernel = functools.partial(kept_kernel, sign=sign)
        return call(kernel, (potential, static), (), [split_rows(n)], [pltpu.VMEM((DEPTH // 2, n), F32)])[0]

    first = work(nt)
    xc, yc, part, lists, log_source, log_target = call(
        first_row_kernel,
        (points, *given),
        (),
        [split_rows(ns), split_rows(nt), rows(ns, 1), jax.ShapeDtypeStruct(tile_source.shape, jnp.int32), rows(ns, 1), rows(nt, 1)],
        first[:2] + [pltpu.VMEM((DEPTH, ns), F32)] + first[2:] + state(ns),
    )
    known, lists = (xc, yc), (lists,)
    parts = exchange([part] * n_tgt, "tgt")
    part, top, u = call(
        bunch(col_kernel, n_tgt),
        (*parts, log_source, *known),
        lists,
        [rows(nt, 1), rows(nt, 1), rows(ns, 1)],
        work(ns) + state(nt),
    )
    kept = kept_operand(top, yc, -1.0)
    parts = sum_up(part, "src")
    (part,) = call(
        bunch(row_kernel, len(parts)),
        (*parts, log_target, *known),
        lists,
        [rows(ns, 1)],
        work(nt) + state(ns),
    )
    parts = exchange([part] * n_tgt, "tgt")
    f, u, part = call(
        bunch(last_col_kernel, n_tgt),
        (*parts, u, top, kept, log_source, points, *known),
        lists,
        [rows(ns, 1), rows(ns, 1), rows(nt, 4)],
        work(ns)
        + [
            pltpu.VMEM((8, nt), F32),
            pltpu.VMEM((4, 8, nt), F32),
            pltpu.VMEM((ns, 384), F32),
            pltpu.VMEM((1, ns), F32),
            pltpu.SemaphoreType.DMA,
        ],
        far=(0,),
    )
    kept = kept_operand(u, xc, 1.0)
    parts = sum_up(part, "src")
    g, *moved = call(
        bunch(functools.partial(gradient_kernel, shares=n_tgt), len(parts)),
        (*parts, kept, log_target, points, *known),
        lists,
        [rows(nt, 1)] + [rows(ns // n_tgt, 3)] * n_tgt,
        work(nt)
        + [
            pltpu.VMEM((4, 8, ns), F32),
            pltpu.VMEM((nt, 384), F32),
            pltpu.VMEM((1, nt), F32),
            pltpu.VMEM((3, ns), F32),
            pltpu.SemaphoreType.DMA,
        ],
        far=(0,),
    )
    (target_grad,) = call(bunch(target_kernel, len(parts)), (*parts, points, moved[-1]), (), [rows(nt, 3)], [])
    own, *others = exchange(moved[::-1], "tgt")
    own_grad = functools.reduce(jnp.add, others[::-1], own)
    return (f.reshape(-1), g.reshape(-1), own_grad, target_grad)


def solution(mesh):
    return jax.shard_map(
        body,
        mesh=mesh,
        in_specs=(
            P(None, "src"),
            P(None, "tgt"),
            P("src"),
            P("tgt"),
            P("tgt"),
            P("src", "tgt", None),
            P("src", "tgt", None),
            P("src", "tgt"),
        ),
        out_specs=(P("src"), P("tgt"), P(None, ("src", "tgt")), P(None, "tgt")),
        check_vma=False,
    )
```
